32 devices in a mesh: pts: 8 (over y, x, core), lmk: 4 (over z).
Axes of the slice: x: 2, y: 2, z: 4, core: 2. Of those that a mesh axis runs over, the one named last changes fastest.
Arguments:
- points: bfloat16 [2048, 768], P('pts'), may hold values from -6 to 6
- landmarks: bfloat16 [384, 768], P('lmk'), may hold values from -6 to 6
- panels: bfloat16 [8, 384, 2048], P('pts', None, 'lmk'), may hold values from -0.3125 to 0.3125
- panel_index: int32 [1], replicated, may hold values from 0 to 7
- assignment: int32 [2048], P('pts'), may hold values from 0 to 4095, as said below
Outputs:
- centroid_sums: float32 [4096, 2048], P('pts', 'lmk')
- cluster_counts: int32 [4096], P('pts')
The draws below stay inside these ranges and needn't reach their ends.
Inputs may be any that keep to these rules, and one draw needn't show every extreme that they name: `assignment`: owner of a cluster c is c // 512. In each aligned block of 256 points (the points of one device) at most 64 points have clusters of one owner; one owner, the same for every block, has exactly 64 points in every block.
All inputs are finite; a program needn't handle non-finite values.
Results may differ from the reference program's by a relative error of at most 0.0017.
Values may be sent and summed in bfloat16 or wider, within the bound.
No kernel may reach another device: no remote copies, remote signals or barrier semaphores. Data moves between devices by JAX's collectives and lax.ppermute only.
A program may use at most 64 MiB of HBM per device.

```python
import math
import jax
import jax.numpy as jnp
from jax import lax

D = 768
FEAT = 2048
CLUSTERS = 4096
P_DEV = 256
NPTS = 2048
LMK = 384
PANELS = 8
CL_DEV = 512
CAP = 64
N_PTS = 8


def draw_assignment(key, part):
    key_hot = jax.random.fold_in(key, 11)
    key_blocks = jax.random.fold_in(key, 23)
    hot_owner = jax.random.randint(key_hot, (), 0, N_PTS).astype(jnp.int32)

    def one_block(block_key):
        key_slots = jax.random.fold_in(block_key, 1)
        key_order = jax.random.fold_in(block_key, 2)
        key_within = jax.random.fold_in(block_key, 3)
        slot_ids = jax.random.permutation(key_slots, (N_PTS - 1) * CAP)[:P_DEV - CAP].astype(jnp.int32)
        others = slot_ids // CAP
        others = others + (others >= hot_owner).astype(jnp.int32)
        owners = jnp.concatenate([jnp.full((CAP,), 1, jnp.int32) * hot_owner, others])
        owners = owners[jax.random.permutation(key_order, P_DEV)]
        within = jax.random.randint(key_within, (P_DEV,), 0, CL_DEV).astype(jnp.int32)
        return owners * CL_DEV + within
    block_keys = jax.random.split(key_blocks, N_PTS)
    return jax.vmap(one_block)(block_keys).reshape(-1)


def level_of(own_key, shape, pieces, least, top_value):
    level, own = 1.0, jax.random.fold_in(own_key, 6)
    for axis_at, parts in pieces:
        steps = jnp.exp(jax.random.uniform(jax.random.fold_in(own, axis_at), (parts,), jnp.float32, least / len(pieces), top_value / len(pieces)))
        level = level * jnp.repeat(steps, shape[axis_at] // parts).reshape([-1 if axis == axis_at else 1 for axis in range(len(shape))])
    return level


def gaussian(key, dims, width, limit, shards=(), kind=jnp.bfloat16):
    gain = level_of(key, dims, shards, -0.22, 0.18) if shards else 1.0
    values = jax.random.normal(key, dims, jnp.float32) * width * gain
    return jnp.minimum(jnp.maximum(values, -limit), limit).astype(kind)


def setup_inputs(seed: int = 0) -> dict:
    seeds = jax.random.split(jax.random.key(seed), 6)
    return {
        "points": gaussian(seeds[0], (NPTS, D), 1.0, 6.0, ((0, 8),)),
        "landmarks": gaussian(seeds[1], (LMK, D), 1.0, 6.0, ((0, 4),)),
        "panels": gaussian(seeds[2], (PANELS, LMK, FEAT), LMK ** -0.5, 0.3125, ((0, 8), (2, 4))),
        "panel_index": jax.random.randint(seeds[3], (1,), 0, PANELS).astype(jnp.int32),
        "assignment": draw_assignment(jax.random.fold_in(seeds[5], 71), 0),
    }


def unit_rows(values_in):
    widened = values_in.astype(jnp.float32)
    scale = lax.rsqrt(lax.optimization_barrier(jnp.mean(widened * widened, axis=1, keepdims=True)) + 1e-06)
    return (widened * scale).astype(jnp.bfloat16)

def kernel_rows(unit_points, unit_marks):
    scores = lax.dot_general(unit_points, unit_marks, (((1,), (1,)), ((), ())), preferred_element_type=jnp.float32)
    return jnp.exp(scores * (0.5 / math.sqrt(unit_points.shape[1]))).astype(jnp.bfloat16)

def reference(points, landmarks, panels, panel_index, assignment):
    unit_marks = unit_rows(landmarks)
    factor_panel = lax.dynamic_index_in_dim(panels, panel_index[0], 0, keepdims=False)

    def block_step(carry, block_index):
        totals, counts = carry
        first_row = (block_index * P_DEV).astype(jnp.int32)
        block_points = lax.dynamic_slice_in_dim(points, first_row, P_DEV, 0)
        block_ids = lax.dynamic_slice_in_dim(assignment, first_row, P_DEV, 0)
        kernel = kernel_rows(unit_rows(block_points), unit_marks)
        features = jnp.dot(kernel, factor_panel, preferred_element_type=jnp.float32).astype(jnp.bfloat16)
        totals = totals + jax.ops.segment_sum(features.astype(jnp.float32), block_ids, CLUSTERS)
        counts = counts + jax.ops.segment_sum(jnp.ones((P_DEV,), jnp.int32), block_ids, CLUSTERS)
        return ((totals, counts), None)
    start = (jnp.zeros((CLUSTERS, FEAT), jnp.float32), jnp.zeros((CLUSTERS,), jnp.int32))
    (totals, counts), unused = lax.scan(block_step, start, jnp.arange(N_PTS, dtype=jnp.int32))
    return (totals / (NPTS / CLUSTERS), counts)
```

```python
import math

import jax
import jax.numpy as jnp
from jax import lax
from jax.experimental import pallas as pl
from jax.experimental.pallas import tpu as pltpu
from jax.sharding import PartitionSpec as P

CLUSTERS = 4096
LANES = 128
VMEM_LIMIT = 48 * 1024 * 1024
NT = (((1,), (1,)), ((), ()))


def unit_rows(values_in):
    widened = values_in.astype(jnp.float32)
    scale = lax.rsqrt(jnp.mean(widened * widened, axis=1, keepdims=True) + 1e-06)
    return (widened * scale).astype(jnp.bfloat16)


def rows_kernel(groups, capacity, points_ref, marks_ref, assignment_ref, out_ref):
    point_rows, marks = points_ref.shape[0], marks_ref.shape[0]
    owned = CLUSTERS // groups
    ids = assignment_ref[...]
    owners = lax.div(ids, owned)
    tags = ids - owners * owned + 1
    hits = lax.broadcasted_iota(jnp.int32, (groups, point_rows), 0) == owners
    earlier = lax.broadcasted_iota(jnp.int32, (point_rows, point_rows), 0) < lax.broadcasted_iota(
        jnp.int32, (point_rows, point_rows), 1
    )
    before = jnp.dot(
        hits.astype(jnp.float32).astype(jnp.bfloat16),
        earlier.astype(jnp.float32).astype(jnp.bfloat16),
        preferred_element_type=jnp.float32,
    )
    rank = jnp.sum(jnp.where(hits, before, 0.0), axis=0, keepdims=True).astype(jnp.int32)
    slots = owners * capacity + rank
    placed = (
        (lax.broadcasted_iota(jnp.int32, (groups * capacity, point_rows), 0) == slots)
        .astype(jnp.float32)
        .astype(jnp.bfloat16)
    )
    scores = lax.dot_general(
        unit_rows(points_ref[...]), unit_rows(marks_ref[...]), NT, preferred_element_type=jnp.float32
    )
    kernel = jnp.exp(scores * (0.5 / math.sqrt(points_ref.shape[1]))).astype(jnp.bfloat16)
    out_ref[:, :marks] = jnp.dot(placed, kernel, preferred_element_type=jnp.float32).astype(
        jnp.bfloat16
    )
    high = lax.div(tags, 256)
    which = lax.broadcasted_iota(jnp.int32, (LANES - marks, point_rows), 0)
    coded = jnp.where(which == 0, high, jnp.where(which == 1, tags - high * 256, 0))
    out_ref[:, marks:] = lax.dot_general(
        placed,
        coded.astype(jnp.float32).astype(jnp.bfloat16),
        NT,
        preferred_element_type=jnp.float32,
    ).astype(jnp.bfloat16)


def sums_kernel(scale, rows_ref, panel_ref, totals_ref, counts_ref):
    parts, slots, lanes = rows_ref.shape
    marks = panel_ref.shape[0] // parts
    owned = totals_ref.shape[0]
    features = jnp.dot(
        rows_ref[0, :, :marks], panel_ref[:marks, :], preferred_element_type=jnp.float32
    )
    for part in range(1, parts):
        features += jnp.dot(
            rows_ref[part, :, :marks],
            panel_ref[part * marks : (part + 1) * marks, :],
            preferred_element_type=jnp.float32,
        )
    features = features.astype(jnp.bfloat16)
    which = lax.broadcasted_iota(jnp.int32, (8, lanes - marks), 1)
    weights = jnp.where(which == 0, 256.0, jnp.where(which == 1, 1.0, 0.0)).astype(jnp.bfloat16)
    tags = lax.dot_general(
        weights, rows_ref[0, :, marks:], NT, preferred_element_type=jnp.float32
    )[:1].astype(jnp.int32)
    member = (
        (lax.broadcasted_iota(jnp.int32, (owned, slots), 0) + 1 == tags)
        .astype(jnp.float32)
        .astype(jnp.bfloat16)
    )
    totals_ref[...] = jnp.dot(member, features, preferred_element_type=jnp.float32) * scale
    counts_ref[...] = lax.dot_general(
        jnp.ones((8, slots), jnp.bfloat16), member, NT, preferred_element_type=jnp.float32
    )[:1].astype(jnp.int32)


def call(kernel, shapes, *operands):
    whole = pl.BlockSpec(memory_space=pltpu.VMEM)
    many = isinstance(shapes, tuple)
    return pl.pallas_call(
        kernel,
        out_shape=shapes,
        in_specs=[whole] * len(operands),
        out_specs=(whole,) * len(shapes) if many else whole,
        compiler_params=pltpu.CompilerParams(vmem_limit_bytes=VMEM_LIMIT),
    )(*operands)


def gather(block, axis):
    size = lax.axis_size(axis)
    return lax.all_to_all(
        jnp.broadcast_to(block[None], (size,) + block.shape), axis, split_axis=0, concat_axis=0, tiled=True
    )


def body(points, landmarks, panels, panel_index, assignment):
    groups = lax.axis_size("pts")
    point_rows = points.shape[0]
    capacity = 2 * point_rows // groups
    owned = CLUSTERS // groups
    depth, columns = panels.shape[1:]
    chunks = lax.all_to_all(
        panels.reshape(groups, depth // groups, columns), "pts", split_axis=0, concat_axis=0, tiled=True
    )
    chunk = lax.dynamic_index_in_dim(chunks, panel_index[0], 0, keepdims=False)
    panel = gather(chunk, "pts").reshape(depth, columns)
    rows = call(
        lambda *refs: rows_kernel(groups, capacity, *refs),
        jax.ShapeDtypeStruct((groups * capacity, LANES), jnp.bfloat16),
        points,
        landmarks,
        assignment.reshape(1, point_rows),
    )
    arrived = lax.all_to_all(
        rows.reshape(groups, capacity, LANES), "pts", split_axis=0, concat_axis=0, tiled=True
    ).reshape(groups * capacity, LANES)
    totals, counts = call(
        lambda *refs: sums_kernel(CLUSTERS / (point_rows * groups), *refs),
        (
            jax.ShapeDtypeStruct((owned, columns), jnp.float32),
            jax.ShapeDtypeStruct((1, owned), jnp.int32),
        ),
        gather(arrived, "lmk"),
        panel,
    )
    return (totals, counts.reshape(owned))


def solution(mesh):
    in_specs = (P("pts", None), P("lmk", None), P("pts", None, "lmk"), P(), P("pts"))
    out_specs = (P("pts", "lmk"), P("pts"))
    return jax.shard_map(body, mesh=mesh, in_specs=in_specs, out_specs=out_specs, check_vma=False)
```

```python
import math

import jax
import jax.numpy as jnp
from jax import lax
from jax.experimental import pallas as pl
from jax.experimental.pallas import tpu as pltpu
from jax.sharding import PartitionSpec as P

CLUSTERS = 4096
LANES = 128
VMEM_LIMIT = 48 * 1024 * 1024
NT = (((1,), (1,)), ((), ()))


def unit_rows(values_in):
    widened = values_in.astype(jnp.float32)
    scale = lax.rsqrt(jnp.mean(widened * widened, axis=1, keepdims=True) + 1e-06)
    return (widened * scale).astype(jnp.bfloat16)


def rows_kernel(groups, capacity, *refs):
    place_ref, points_ref, own_ref, assignment_ref = refs[:4]
    halves, out_ref, marks_ref = refs[4:-2], refs[-2], refs[-1]
    point_rows = points_ref.shape[0]
    own, all_marks = own_ref.shape[0], marks_ref.shape[0]
    half = own // 2
    parity = lax.rem(place_ref[0], 2)
    ids = assignment_ref[...]
    owned = CLUSTERS // groups
    owners = lax.div(ids, owned)
    tags = ids - owners * owned + 1
    hits = lax.broadcasted_iota(jnp.int32, (groups, point_rows), 0) == owners
    earlier = lax.broadcasted_iota(jnp.int32, (point_rows, point_rows), 0) < lax.broadcasted_iota(
        jnp.int32, (point_rows, point_rows), 1
    )
    before = jnp.dot(
        hits.astype(jnp.float32).astype(jnp.bfloat16),
        earlier.astype(jnp.float32).astype(jnp.bfloat16),
        preferred_element_type=jnp.float32,
    )
    rank = jnp.sum(jnp.where(hits, before, 0.0), axis=0, keepdims=True).astype(jnp.int32)
    slots = owners * capacity + rank
    placed = (
        (lax.broadcasted_iota(jnp.int32, (groups * capacity, point_rows), 0) == slots)
        .astype(jnp.float32)
        .astype(jnp.bfloat16)
    )
    marks_ref[:own, :] = unit_rows(own_ref[...])
    for at, (mine, other) in enumerate(zip(halves[::2], halves[1::2])):
        first = own * (at + 1)
        marks_ref[pl.ds(pl.multiple_of(first + half * parity, 16), half), :] = unit_rows(mine[...])
        marks_ref[pl.ds(pl.multiple_of(first + half * (1 - parity), 16), half), :] = unit_rows(
            other[...]
        )
    scores = lax.dot_general(
        unit_rows(points_ref[...]), marks_ref[...], NT, preferred_element_type=jnp.float32
    )
    kernel = jnp.exp(scores * (0.5 / math.sqrt(points_ref.shape[1]))).astype(jnp.bfloat16)
    out_ref[:, :all_marks] = jnp.dot(placed, kernel, preferred_element_type=jnp.float32).astype(
        jnp.bfloat16
    )
    high = lax.div(tags, 256)
    which = lax.broadcasted_iota(jnp.int32, (LANES, point_rows), 0)
    coded = jnp.where(which == 0, high, jnp.where(which == 1, tags - high * 256, 0))
    out_ref[:, all_marks:] = lax.dot_general(
        placed,
        coded.astype(jnp.float32).astype(jnp.bfloat16),
        NT,
        preferred_element_type=jnp.float32,
    ).astype(jnp.bfloat16)


def sums_kernel(scale, parts, place_ref, rows_ref, panel_ref, totals_ref, counts_ref, turned_ref):
    slots = rows_ref.shape[0]
    depth = panel_ref.shape[0]
    owned, own = totals_ref.shape[0], depth // parts
    for part in range(parts):
        source = lax.rem(place_ref[1] + parts - part, parts)
        turned_ref[part * own : (part + 1) * own, :] = panel_ref[
            pl.ds(pl.multiple_of(source * own, 16), own), :
        ]
    features = jnp.dot(
        rows_ref[:, :depth], turned_ref[...], preferred_element_type=jnp.float32
    ).astype(jnp.bfloat16)
    which = lax.broadcasted_iota(jnp.int32, (8, LANES), 1)
    weights = jnp.where(which == 0, 256.0, jnp.where(which == 1, 1.0, 0.0)).astype(jnp.bfloat16)
    tags = lax.dot_general(
        weights, rows_ref[:, depth:], NT, preferred_element_type=jnp.float32
    )[:1].astype(jnp.int32)
    member = (
        (lax.broadcasted_iota(jnp.int32, (owned, slots), 0) + 1 == tags)
        .astype(jnp.float32)
        .astype(jnp.bfloat16)
    )
    totals_ref[...] = jnp.dot(member, features, preferred_element_type=jnp.float32) * scale
    counts_ref[...] = lax.dot_general(
        jnp.ones((8, slots), jnp.bfloat16), member, NT, preferred_element_type=jnp.float32
    )[:1].astype(jnp.int32)


def call(kernel, shapes, scratch, place, *operands):
    whole = pl.BlockSpec(memory_space=pltpu.VMEM)
    many = isinstance(shapes, tuple)
    return pl.pallas_call(
        kernel,
        out_shape=shapes,
        in_specs=[pl.BlockSpec(memory_space=pltpu.SMEM)] + [whole] * len(operands),
        out_specs=(whole,) * len(shapes) if many else whole,
        scratch_shapes=[scratch],
        compiler_params=pltpu.CompilerParams(vmem_limit_bytes=VMEM_LIMIT),
    )(place, *operands)


def gather(block, axis):
    size = lax.axis_size(axis)
    return lax.all_to_all(
        jnp.broadcast_to(block[None], (size,) + block.shape), axis, split_axis=0, concat_axis=0, tiled=True
    )


def shift(block, axis, by):
    size = lax.axis_size(axis)
    return lax.ppermute(block, axis, [(i, (i + by) % size) for i in range(size)])


def swap(block, axis):
    return lax.ppermute(block, axis, [(i, i ^ 1) for i in range(lax.axis_size(axis))])


def body(points, landmarks, panels, panel_index, assignment):
    groups, parts = lax.axis_size("pts"), lax.axis_size("lmk")
    point_rows = points.shape[0]
    capacity = 2 * point_rows // groups
    owned = CLUSTERS // groups
    depth, columns = panels.shape[1:]
    own, width = landmarks.shape
    place = jnp.stack([lax.axis_index("pts"), lax.axis_index("lmk")]).astype(jnp.int32)
    mine = lax.dynamic_slice_in_dim(landmarks, (place[0] % 2) * (own // 2), own // 2, 0)
    halves = []
    for by in range(1, parts):
        half = shift(mine, "lmk", by)
        halves += [half, swap(half, "pts")]
    chunks = lax.all_to_all(
        panels.reshape(groups, depth // groups, columns), "pts", split_axis=0, concat_axis=0, tiled=True
    )
    chunk = lax.dynamic_index_in_dim(chunks, panel_index[0], 0, keepdims=False)
    panel = gather(chunk, "pts").reshape(depth, columns)
    row_lanes = depth + LANES
    rows = call(
        lambda *refs: rows_kernel(groups, capacity, *refs),
        jax.ShapeDtypeStruct((groups * capacity, row_lanes), jnp.bfloat16),
        pltpu.VMEM((depth, width), jnp.bfloat16),
        place,
        points,
        landmarks,
        assignment.reshape(1, point_rows),
        *halves,
    )
    arrived = lax.all_to_all(
        rows.reshape(groups, capacity, row_lanes), "pts", split_axis=0, concat_axis=0, tiled=True
    ).reshape(groups * capacity, row_lanes)
    totals, counts = call(
        lambda *refs: sums_kernel(CLUSTERS / (point_rows * groups), parts, *refs),
        (
            jax.ShapeDtypeStruct((owned, columns), jnp.float32),
            jax.ShapeDtypeStruct((1, owned), jnp.int32),
        ),
        pltpu.VMEM((depth, columns), jnp.bfloat16),
        place,
        arrived,
        panel,
    )
    return (totals, counts.reshape(owned))


def solution(mesh):
    in_specs = (P("pts", None), P("lmk", None), P("pts", None, "lmk"), P(), P("pts"))
    out_specs = (P("pts", "lmk"), P("pts"))
    return jax.shard_map(body, mesh=mesh, in_specs=in_specs, out_specs=out_specs, check_vma=False)
```

```python
import math

import jax
import jax.numpy as jnp
from jax import lax
from jax.experimental import pallas as pl
from jax.experimental.pallas import tpu as pltpu
from jax.sharding import PartitionSpec as P

CLUSTERS = 4096
LANES = 128
VMEM_LIMIT = 48 * 1024 * 1024
NT = (((1,), (1,)), ((), ()))


def unit_rows(values_in):
    widened = values_in.astype(jnp.float32)
    scale = lax.rsqrt(jnp.mean(widened * widened, axis=1, keepdims=True) + 1e-06)
    return (widened * scale).astype(jnp.bfloat16)


def place_kernel(groups, capacity, points_ref, own_ref, assignment_ref, points_out, marks_out, tags_out):
    point_rows = points_ref.shape[0]
    ids = assignment_ref[...]
    owned = CLUSTERS // groups
    owners = lax.div(ids, owned)
    tags = ids - owners * owned + 1
    hits = lax.broadcasted_iota(jnp.int32, (groups, point_rows), 0) == owners
    earlier = lax.broadcasted_iota(jnp.int32, (point_rows, point_rows), 0) < lax.broadcasted_iota(
        jnp.int32, (point_rows, point_rows), 1
    )
    before = jnp.dot(
        hits.astype(jnp.float32).astype(jnp.bfloat16),
        earlier.astype(jnp.float32).astype(jnp.bfloat16),
        preferred_element_type=jnp.float32,
    )
    rank = jnp.sum(jnp.where(hits, before, 0.0), axis=0, keepdims=True).astype(jnp.int32)
    slots = owners * capacity + rank
    placed = (
        (lax.broadcasted_iota(jnp.int32, (groups * capacity, point_rows), 0) == slots)
        .astype(jnp.float32)
        .astype(jnp.bfloat16)
    )
    points_out[...] = jnp.dot(
        placed, unit_rows(points_ref[...]), preferred_element_type=jnp.float32
    ).astype(jnp.bfloat16)
    marks_out[...] = unit_rows(own_ref[...])
    high = lax.div(tags, 256)
    which = lax.broadcasted_iota(jnp.int32, (LANES, point_rows), 0)
    coded = jnp.where(which == 0, high, jnp.where(which == 1, tags - high * 256, 0))
    tags_out[...] = lax.dot_general(
        placed,
        coded.astype(jnp.float32).astype(jnp.bfloat16),
        NT,
        preferred_element_type=jnp.float32,
    ).astype(jnp.bfloat16)


def rows_kernel(place_ref, points_ref, own_ref, tags_ref, *refs):
    halves, out_ref, marks_ref = refs[:-2], refs[-2], refs[-1]
    own, all_marks = own_ref.shape[0], marks_ref.shape[0]
    half = own // 2
    parity = lax.rem(place_ref[0], 2)
    marks_ref[:own, :] = own_ref[...]
    for at, (mine, other) in enumerate(zip(halves[::2], halves[1::2])):
        first = own * (at + 1)
        marks_ref[pl.ds(pl.multiple_of(first + half * parity, 16), half), :] = unit_rows(mine[...])
        marks_ref[pl.ds(pl.multiple_of(first + half * (1 - parity), 16), half), :] = unit_rows(
            other[...]
        )
    scores = lax.dot_general(points_ref[...], marks_ref[...], NT, preferred_element_type=jnp.float32)
    out_ref[:, :all_marks] = jnp.exp(scores * (0.5 / math.sqrt(points_ref.shape[1]))).astype(
        jnp.bfloat16
    )
    out_ref[:, all_marks:] = tags_ref[...]


def sums_kernel(scale, parts, place_ref, rows_ref, *refs):
    blocks, totals_ref, counts_ref, turned_ref = refs[:-3], refs[-3], refs[-2], refs[-1]
    slots = rows_ref.shape[0]
    depth = turned_ref.shape[0]
    owned, own, size = totals_ref.shape[0], depth // parts, blocks[0].shape[0]
    parity = lax.rem(place_ref[0], 2)
    for at, block in enumerate(blocks):
        core, part = divmod(at, len(blocks) // 2)
        first = (parity if core == 0 else 1 - parity) * (depth // 2) + part * size
        holder = lax.div(first, own)
        first = lax.bitwise_xor(holder, place_ref[1]) * own + first - holder * own
        turned_ref[pl.ds(pl.multiple_of(first, 16), size), :] = block[...]
    features = jnp.dot(
        rows_ref[:, :depth], turned_ref[...], preferred_element_type=jnp.float32
    ).astype(jnp.bfloat16)
    which = lax.broadcasted_iota(jnp.int32, (8, LANES), 1)
    weights = jnp.where(which == 0, 256.0, jnp.where(which == 1, 1.0, 0.0)).astype(jnp.bfloat16)
    tags = lax.dot_general(
        weights, rows_ref[:, depth:], NT, preferred_element_type=jnp.float32
    )[:1].astype(jnp.int32)
    member = (
        (lax.broadcasted_iota(jnp.int32, (owned, slots), 0) + 1 == tags)
        .astype(jnp.float32)
        .astype(jnp.bfloat16)
    )
    totals_ref[...] = jnp.dot(member, features, preferred_element_type=jnp.float32) * scale
    counts_ref[...] = lax.dot_general(
        jnp.ones((8, slots), jnp.bfloat16), member, NT, preferred_element_type=jnp.float32
    )[:1].astype(jnp.int32)


def call(kernel, shapes, place, *operands, scratch=()):
    whole = pl.BlockSpec(memory_space=pltpu.VMEM)
    many = isinstance(shapes, tuple)
    scalar = [] if place is None else [place]
    return pl.pallas_call(
        kernel,
        out_shape=shapes,
        in_specs=[pl.BlockSpec(memory_space=pltpu.SMEM)] * len(scalar) + [whole] * len(operands),
        out_specs=(whole,) * len(shapes) if many else whole,
        scratch_shapes=scratch,
        compiler_params=pltpu.CompilerParams(vmem_limit_bytes=VMEM_LIMIT),
    )(*scalar, *operands)


def swap(block, axis, mask):
    return lax.ppermute(block, axis, [(i, i ^ mask) for i in range(lax.axis_size(axis))])


def spread(panel, holder, groups):
    me = lax.axis_index("pts")
    half = panel.shape[0] // 2
    mine = lax.dynamic_slice_in_dim(panel, (me % 2) * half, half, 0)
    other = lax.dynamic_slice_in_dim(panel, (1 - me % 2) * half, half, 0)

    def pick(block, mask):
        return jnp.where(((holder ^ me) & mask) == 0, block, swap(block, "pts", mask))

    mine = jnp.where(((holder ^ me) & 1) == 0, mine, swap(other, "pts", 1))
    masks = [1 << bit for bit in range(1, groups.bit_length() - 1)]
    size = half // len(masks)
    blocks = [mine[at * size : (at + 1) * size] for at in range(len(masks))]
    for turn in range(len(masks)):
        blocks = [
            pick(block, masks[(at + turn) % len(masks)]) for at, block in enumerate(blocks)
        ]
    return blocks + [swap(block, "pts", 1) for block in blocks]


def body(points, landmarks, panels, panel_index, assignment):
    groups, parts = lax.axis_size("pts"), lax.axis_size("lmk")
    point_rows, width = points.shape
    capacity = 2 * point_rows // groups
    slots = groups * capacity
    owned = CLUSTERS // groups
    depth, columns = panels.shape[1:]
    own = landmarks.shape[0]
    place = jnp.stack([lax.axis_index("pts"), lax.axis_index("lmk")]).astype(jnp.int32)
    mine = lax.dynamic_slice_in_dim(landmarks, (place[0] % 2) * (own // 2), own // 2, 0)
    halves = []
    for mask in range(1, parts):
        half = swap(mine, "lmk", mask)
        halves += [half, swap(half, "pts", 1)]
    blocks = spread(panels[0], panel_index[0], groups)
    placed, unit_marks, tags = call(
        lambda *refs: place_kernel(groups, capacity, *refs),
        (
            jax.ShapeDtypeStruct((slots, width), jnp.bfloat16),
            jax.ShapeDtypeStruct((own, width), jnp.bfloat16),
            jax.ShapeDtypeStruct((slots, LANES), jnp.bfloat16),
        ),
        None,
        points,
        landmarks,
        assignment.reshape(1, point_rows),
    )
    row_lanes = depth + LANES
    rows = call(
        rows_kernel,
        jax.ShapeDtypeStruct((slots, row_lanes), jnp.bfloat16),
        place,
        placed,
        unit_marks,
        tags,
        *halves,
        scratch=[pltpu.VMEM((depth, width), jnp.bfloat16)],
    )
    arrived = lax.all_to_all(
        rows.reshape(groups, capacity, row_lanes), "pts", split_axis=0, concat_axis=0, tiled=True
    ).reshape(slots, row_lanes)
    totals, counts = call(
        lambda *refs: sums_kernel(CLUSTERS / (point_rows * groups), parts, *refs),
        (
            jax.ShapeDtypeStruct((owned, columns), jnp.float32),
            jax.ShapeDtypeStruct((1, owned), jnp.int32),
        ),
        place,
        arrived,
        *blocks,
        scratch=[pltpu.VMEM((depth, columns), jnp.bfloat16)],
    )
    return (totals, counts.reshape(owned))


def solution(mesh):
    in_specs = (P("pts", None), P("lmk", None), P("pts", None, "lmk"), P(), P("pts"))
    out_specs = (P("pts", "lmk"), P("pts"))
    return jax.shard_map(body, mesh=mesh, in_specs=in_specs, out_specs=out_specs, check_vma=False)
```

```python
import math

import jax
import jax.numpy as jnp
from jax import lax
from jax.experimental import pallas as pl
from jax.experimental.pallas import tpu as pltpu
from jax.sharding import PartitionSpec as P

CLUSTERS = 4096
LANES = 128
VMEM_LIMIT = 48 * 1024 * 1024
NT = (((1,), (1,)), ((), ()))


def unit_rows(values_in):
    widened = values_in.astype(jnp.float32)
    scale = lax.rsqrt(jnp.mean(widened * widened, axis=1, keepdims=True) + 1e-06)
    return (widened * scale).astype(jnp.bfloat16)


def place_kernel(groups, capacity, parts, place_ref, points_ref, assignment_ref, panel_ref, *outs):
    points_out, tags_out, mine_out, other_out = outs
    point_rows = points_ref.shape[0]
    ids = assignment_ref[...]
    owned = CLUSTERS // groups
    owners = lax.div(ids, owned)
    tags = ids - owners * owned + 1
    hits = lax.broadcasted_iota(jnp.int32, (groups, point_rows), 0) == owners
    earlier = lax.broadcasted_iota(jnp.int32, (point_rows, point_rows), 0) < lax.broadcasted_iota(
        jnp.int32, (point_rows, point_rows), 1
    )
    before = jnp.dot(
        hits.astype(jnp.float32).astype(jnp.bfloat16),
        earlier.astype(jnp.float32).astype(jnp.bfloat16),
        preferred_element_type=jnp.float32,
    )
    rank = jnp.sum(jnp.where(hits, before, 0.0), axis=0, keepdims=True).astype(jnp.int32)
    slots = owners * capacity + rank
    placed = (
        (lax.broadcasted_iota(jnp.int32, (groups * capacity, point_rows), 0) == slots)
        .astype(jnp.float32)
        .astype(jnp.bfloat16)
    )
    points_out[...] = jnp.dot(
        placed, unit_rows(points_ref[...]), preferred_element_type=jnp.float32
    ).astype(jnp.bfloat16)
    high = lax.div(tags, 256)
    which = lax.broadcasted_iota(jnp.int32, (tags_out.shape[1], point_rows), 0)
    coded = jnp.where(which == 0, high, jnp.where(which == 1, tags - high * 256, 0))
    tags_out[...] = lax.dot_general(
        placed,
        coded.astype(jnp.float32).astype(jnp.bfloat16),
        NT,
        preferred_element_type=jnp.float32,
    ).astype(jnp.bfloat16)
    half = panel_ref.shape[1] // parts // 2
    core = lax.rem(place_ref[0], 2)
    for part in range(parts):
        first = part * (2 * half)
        for out, side in ((mine_out, core), (other_out, 1 - core)):
            out[part * half : (part + 1) * half, :] = panel_ref[
                0, pl.ds(pl.multiple_of(first + side * half, 16), half), :
            ]


def rows_kernel(groups, capacity, points_ref, partner_ref, tags_ref, halves_ref, out_ref, marks_ref):
    half, marks = halves_ref.shape[1], marks_ref.shape[0]
    slots = points_ref.shape[0]
    tag_lanes = tags_ref.shape[1]
    for part in range(halves_ref.shape[0]):
        marks_ref[part * half : (part + 1) * half, :] = unit_rows(halves_ref[part])
    for core, (placed, tags) in enumerate(
        ((points_ref, tags_ref[...]), (partner_ref, jnp.zeros((slots, tag_lanes), jnp.bfloat16)))
    ):
        scores = lax.dot_general(placed[...], marks_ref[...], NT, preferred_element_type=jnp.float32)
        rows = jnp.exp(scores * (0.5 / math.sqrt(placed.shape[1]))).astype(jnp.bfloat16)
        if len(out_ref.shape) == 4:
            for group in range(groups):
                here = slice(group * capacity, (group + 1) * capacity)
                out_ref[group, core, :, :marks] = rows[here]
                out_ref[group, core, :, marks:] = tags[here]
        else:
            out_ref[core, :, :marks] = rows
            out_ref[core, :, marks:] = tags


def sums_kernel(scale, even_ref, odd_ref, *refs):
    blocks, totals_ref, counts_ref, panel_ref = refs[:-3], refs[-3], refs[-2], refs[-1]
    slots, lanes = even_ref.shape
    owned = totals_ref.shape[0]
    for side in range(2):
        first = 0
        for block in blocks[side * len(blocks) // 2 : (side + 1) * len(blocks) // 2]:
            panel_ref[side, first : first + block.shape[0], :] = block[...]
            first += block.shape[0]
        marks = first
        panel_ref[side, marks:, :] = jnp.zeros((lanes - marks, panel_ref.shape[2]), jnp.bfloat16)
    features = (
        jnp.dot(even_ref[...], panel_ref[0], preferred_element_type=jnp.float32)
        + jnp.dot(odd_ref[...], panel_ref[1], preferred_element_type=jnp.float32)
    ).astype(jnp.bfloat16)
    which = lax.broadcasted_iota(jnp.int32, (8, lanes - marks), 1)
    weights = jnp.where(which == 0, 256.0, jnp.where(which == 1, 1.0, 0.0)).astype(jnp.bfloat16)
    tags = lax.dot_general(weights, even_ref[:, marks:], NT, preferred_element_type=jnp.float32)
    tags += lax.dot_general(weights, odd_ref[:, marks:], NT, preferred_element_type=jnp.float32)
    tags = tags[:1].astype(jnp.int32)
    member = (
        (lax.broadcasted_iota(jnp.int32, (owned, slots), 0) + 1 == tags)
        .astype(jnp.float32)
        .astype(jnp.bfloat16)
    )
    totals_ref[...] = jnp.dot(member, features, preferred_element_type=jnp.float32) * scale
    counts_ref[...] = lax.dot_general(
        jnp.ones((8, slots), jnp.bfloat16), member, NT, preferred_element_type=jnp.float32
    )[:1].astype(jnp.int32)


def call(kernel, shapes, *operands, place=None, scratch=()):
    whole = pl.BlockSpec(memory_space=pltpu.VMEM)
    many = isinstance(shapes, tuple)
    scalar = [] if place is None else [place]
    return pl.pallas_call(
        kernel,
        out_shape=shapes,
        in_specs=[pl.BlockSpec(memory_space=pltpu.SMEM)] * len(scalar) + [whole] * len(operands),
        out_specs=(whole,) * len(shapes) if many else whole,
        scratch_shapes=scratch,
        compiler_params=pltpu.CompilerParams(vmem_limit_bytes=VMEM_LIMIT),
    )(*scalar, *operands)


def array(shape, dtype=jnp.bfloat16):
    return jax.ShapeDtypeStruct(shape, dtype)


def swap(block, axis, mask):
    return lax.ppermute(block, axis, [(i, i ^ mask) for i in range(lax.axis_size(axis))])


def gather(block, axis):
    size = lax.axis_size(axis)
    return lax.all_to_all(
        jnp.broadcast_to(block[None], (size,) + block.shape), axis, split_axis=0, concat_axis=0, tiled=True
    )


def spread(mine, other, holder, groups):
    me = lax.axis_index("pts")

    def pick(block, mask):
        return jnp.where(((holder ^ me) & mask) == 0, block, swap(block, "pts", mask))

    mine = jnp.where(((holder ^ me) & 1) == 0, mine, swap(other, "pts", 1))
    masks = [1 << bit for bit in range(1, groups.bit_length() - 1)]
    size = mine.shape[0] // len(masks)
    blocks = [mine[at * size : (at + 1) * size] for at in range(len(masks))]
    for turn in range(len(masks)):
        blocks = [
            pick(block, masks[(at + turn) % len(masks)]) for at, block in enumerate(blocks)
        ]
    return blocks + [swap(block, "pts", 1) for block in blocks]


def exchange(rows, groups, capacity):
    slots, lanes = groups * capacity, rows.shape[-1]
    if rows.ndim == 3:
        rows = rows.reshape(2, groups, capacity, lanes).swapaxes(0, 1)
    arrived = lax.all_to_all(
        rows.reshape(groups, 2 * capacity, lanes), "pts", split_axis=0, concat_axis=0, tiled=True
    ).reshape(groups // 2, 2, 2 * capacity, lanes)
    core = lax.axis_index("pts") % 2
    even = lax.dynamic_index_in_dim(arrived, core, 1, keepdims=False)
    odd = lax.dynamic_index_in_dim(arrived, 1 - core, 1, keepdims=False)
    odd = jnp.concatenate([odd[:, capacity:], odd[:, :capacity]], axis=1)
    return even.reshape(slots, lanes), odd.reshape(slots, lanes)


def body(points, landmarks, panels, panel_index, assignment):
    groups, parts = lax.axis_size("pts"), lax.axis_size("lmk")
    point_rows, width = points.shape
    capacity = 2 * point_rows // groups
    slots = groups * capacity
    owned = CLUSTERS // groups
    depth, columns = panels.shape[1:]
    half = landmarks.shape[0] // 2
    lanes = -(-(depth // 2 + 2) // LANES) * LANES
    place = jnp.stack([lax.axis_index("pts"), lax.axis_index("lmk")]).astype(jnp.int32)
    mine = lax.dynamic_slice_in_dim(landmarks, (place[0] % 2) * half, half, 0)
    halves = gather(mine, "lmk")
    placed, tags, panel_mine, panel_other = call(
        lambda *refs: place_kernel(groups, capacity, parts, *refs),
        (
            array((slots, width)),
            array((slots, lanes - depth // 2)),
            array((depth // 2, columns)),
            array((depth // 2, columns)),
        ),
        points,
        assignment.reshape(1, point_rows),
        panels,
        place=place,
    )
    partner = swap(placed, "pts", 1)
    blocks = spread(panel_mine, panel_other, panel_index[0], groups)
    rows = call(
        lambda *refs: rows_kernel(groups, capacity, *refs),
        array((groups, 2, capacity, lanes) if capacity % 16 == 0 else (2, slots, lanes)),
        placed,
        partner,
        tags,
        halves,
        scratch=[pltpu.VMEM((depth // 2, width), jnp.bfloat16)],
    )
    even, odd = exchange(rows, groups, capacity)
    totals, counts = call(
        lambda *refs: sums_kernel(CLUSTERS / (point_rows * groups), *refs),
        (array((owned, columns), jnp.float32), array((1, owned), jnp.int32)),
        even,
        odd,
        *blocks,
        scratch=[pltpu.VMEM((2, lanes, columns), jnp.bfloat16)],
    )
    return (totals, counts.reshape(owned))


def solution(mesh):
    in_specs = (P("pts", None), P("lmk", None), P("pts", None, "lmk"), P(), P("pts"))
    out_specs = (P("pts", "lmk"), P("pts"))
    return jax.shard_map(body, mesh=mesh, in_specs=in_specs, out_specs=out_specs, check_vma=False)
```

```python
import math

import jax
import jax.numpy as jnp
from jax import lax
from jax.experimental import pallas as pl
from jax.experimental.pallas import tpu as pltpu
from jax.sharding import PartitionSpec as P

CLUSTERS = 4096
LANES = 128
VMEM_LIMIT = 48 * 1024 * 1024
NT = (((1,), (1,)), ((), ()))


def unit_rows(values_in):
    widened = values_in.astype(jnp.float32)
    scale = lax.rsqrt(jnp.mean(widened * widened, axis=1, keepdims=True) + 1e-06)
    return (widened * scale).astype(jnp.bfloat16)


def fetch_kernel(place_ref, points_ref, marks_ref, assignment_ref, panel_ref, *refs):
    points_out, halves_out, assignment_out, mine_out, other_out, sems = refs
    parts, half = halves_out.shape[:2]
    core = lax.rem(place_ref[0], 2)
    pairs = [(points_ref, points_out), (assignment_ref, assignment_out)]
    for part in range(parts):
        pairs.append(
            (marks_ref.at[pl.ds(pl.multiple_of(core * half, 16), half), :], halves_out.at[part])
        )
        for out, side in ((mine_out, core), (other_out, 1 - core)):
            first = pl.multiple_of((2 * part + side) * half, 16)
            pairs.append(
                (
                    panel_ref.at[0, pl.ds(first, half), :],
                    out.at[part * half : (part + 1) * half, :],
                )
            )
    copies = [pltpu.make_async_copy(*pair, sems.at[at]) for at, pair in enumerate(pairs)]
    for copy in copies:
        copy.start()
    for copy in copies:
        copy.wait()


def place_kernel(groups, capacity, points_ref, assignment_ref, points_out, tags_out):
    point_rows = points_ref.shape[0]
    ids = assignment_ref[...]
    owned = CLUSTERS // groups
    owners = lax.div(ids, owned)
    tags = ids - owners * owned + 1
    hits = lax.broadcasted_iota(jnp.int32, (groups, point_rows), 0) == owners
    earlier = lax.broadcasted_iota(jnp.int32, (point_rows, point_rows), 0) < lax.broadcasted_iota(
        jnp.int32, (point_rows, point_rows), 1
    )
    before = jnp.dot(
        hits.astype(jnp.float32).astype(jnp.bfloat16),
        earlier.astype(jnp.float32).astype(jnp.bfloat16),
        preferred_element_type=jnp.float32,
    )
    rank = jnp.sum(jnp.where(hits, before, 0.0), axis=0, keepdims=True).astype(jnp.int32)
    slots = owners * capacity + rank
    placed = (
        (lax.broadcasted_iota(jnp.int32, (groups * capacity, point_rows), 0) == slots)
        .astype(jnp.float32)
        .astype(jnp.bfloat16)
    )
    points_out[...] = jnp.dot(
        placed, unit_rows(points_ref[...]), preferred_element_type=jnp.float32
    ).astype(jnp.bfloat16)
    high = lax.div(tags, 256)
    which = lax.broadcasted_iota(jnp.int32, (tags_out.shape[1], point_rows), 0)
    coded = jnp.where(which == 0, high, jnp.where(which == 1, tags - high * 256, 0))
    tags_out[...] = lax.dot_general(
        placed,
        coded.astype(jnp.float32).astype(jnp.bfloat16),
        NT,
        preferred_element_type=jnp.float32,
    ).astype(jnp.bfloat16)


def rows_kernel(groups, capacity, points_ref, partner_ref, tags_ref, halves_ref, out_ref, marks_ref):
    half, marks = halves_ref.shape[1], marks_ref.shape[0]
    slots = points_ref.shape[0]
    tag_lanes = tags_ref.shape[1]
    for part in range(halves_ref.shape[0]):
        marks_ref[part * half : (part + 1) * half, :] = unit_rows(halves_ref[part])
    for core, (placed, tags) in enumerate(
        ((points_ref, tags_ref[...]), (partner_ref, jnp.zeros((slots, tag_lanes), jnp.bfloat16)))
    ):
        scores = lax.dot_general(placed[...], marks_ref[...], NT, preferred_element_type=jnp.float32)
        rows = jnp.exp(scores * (0.5 / math.sqrt(placed.shape[1]))).astype(jnp.bfloat16)
        if len(out_ref.shape) == 4:
            for group in range(groups):
                here = slice(group * capacity, (group + 1) * capacity)
                out_ref[group, core, :, :marks] = rows[here]
                out_ref[group, core, :, marks:] = tags[here]
        else:
            out_ref[core, :, :marks] = rows
            out_ref[core, :, marks:] = tags


def sums_kernel(scale, even_ref, odd_ref, *refs):
    blocks, totals_ref, counts_ref, panel_ref = refs[:-3], refs[-3], refs[-2], refs[-1]
    slots, lanes = even_ref.shape
    owned = totals_ref.shape[0]
    for side in range(2):
        first = 0
        for block in blocks[side * len(blocks) // 2 : (side + 1) * len(blocks) // 2]:
            panel_ref[side, first : first + block.shape[0], :] = block[...]
            first += block.shape[0]
        marks = first
        panel_ref[side, marks:, :] = jnp.zeros((lanes - marks, panel_ref.shape[2]), jnp.bfloat16)
    features = (
        jnp.dot(even_ref[...], panel_ref[0], preferred_element_type=jnp.float32)
        + jnp.dot(odd_ref[...], panel_ref[1], preferred_element_type=jnp.float32)
    ).astype(jnp.bfloat16)
    which = lax.broadcasted_iota(jnp.int32, (8, lanes - marks), 1)
    weights = jnp.where(which == 0, 256.0, jnp.where(which == 1, 1.0, 0.0)).astype(jnp.bfloat16)
    tags = lax.dot_general(weights, even_ref[:, marks:], NT, preferred_element_type=jnp.float32)
    tags += lax.dot_general(weights, odd_ref[:, marks:], NT, preferred_element_type=jnp.float32)
    tags = tags[:1].astype(jnp.int32)
    member = (
        (lax.broadcasted_iota(jnp.int32, (owned, slots), 0) + 1 == tags)
        .astype(jnp.float32)
        .astype(jnp.bfloat16)
    )
    totals_ref[...] = jnp.dot(member, features, preferred_element_type=jnp.float32) * scale
    counts_ref[...] = lax.dot_general(
        jnp.ones((8, slots), jnp.bfloat16), member, NT, preferred_element_type=jnp.float32
    )[:1].astype(jnp.int32)


def call(kernel, shapes, *operands, place=None, scratch=(), kept=False):
    whole = pl.BlockSpec(memory_space=pltpu.VMEM)
    many = isinstance(shapes, tuple)
    scalar = [] if place is None else [place]
    return pl.pallas_call(
        kernel,
        out_shape=shapes,
        in_specs=[pl.BlockSpec(memory_space=pltpu.SMEM)] * len(scalar)
        + [pl.BlockSpec(memory_space=pl.ANY) if kept else whole] * len(operands),
        out_specs=(whole,) * len(shapes) if many else whole,
        scratch_shapes=scratch,
        compiler_params=pltpu.CompilerParams(vmem_limit_bytes=VMEM_LIMIT),
    )(*scalar, *operands)


def array(shape, dtype=jnp.bfloat16):
    return jax.ShapeDtypeStruct(shape, dtype)


def swap(block, axis, mask):
    return lax.ppermute(block, axis, [(i, i ^ mask) for i in range(lax.axis_size(axis))])


def spread(mine, other, holder, groups):
    me = lax.axis_index("pts")

    def pick(block, mask):
        return jnp.where(((holder ^ me) & mask) == 0, block, swap(block, "pts", mask))

    mine = jnp.where(((holder ^ me) & 1) == 0, mine, swap(other, "pts", 1))
    masks = [1 << bit for bit in range(1, groups.bit_length() - 1)]
    size = mine.shape[0] // len(masks)
    blocks = [mine[at * size : (at + 1) * size] for at in range(len(masks))]
    for turn in range(len(masks)):
        blocks = [
            pick(block, masks[(at + turn) % len(masks)]) for at, block in enumerate(blocks)
        ]
    return blocks + [swap(block, "pts", 1) for block in blocks]


def exchange(rows, groups, capacity):
    slots, lanes = groups * capacity, rows.shape[-1]
    if rows.ndim == 3:
        rows = rows.reshape(2, groups, capacity, lanes).swapaxes(0, 1)
    arrived = lax.all_to_all(
        rows.reshape(groups, 2 * capacity, lanes), "pts", split_axis=0, concat_axis=0, tiled=True
    ).reshape(groups // 2, 2, 2 * capacity, lanes)
    core = lax.axis_index("pts") % 2
    even = lax.dynamic_index_in_dim(arrived, core, 1, keepdims=False)
    odd = lax.dynamic_index_in_dim(arrived, 1 - core, 1, keepdims=False)
    odd = jnp.concatenate([odd[:, capacity:], odd[:, :capacity]], axis=1)
    return even.reshape(slots, lanes), odd.reshape(slots, lanes)


def body(points, landmarks, panels, panel_index, assignment):
    groups, parts = lax.axis_size("pts"), lax.axis_size("lmk")
    point_rows, width = points.shape
    capacity = 2 * point_rows // groups
    slots = groups * capacity
    owned = CLUSTERS // groups
    depth, columns = panels.shape[1:]
    half = landmarks.shape[0] // 2
    lanes = -(-(depth // 2 + 2) // LANES) * LANES
    place = jnp.stack([lax.axis_index("pts"), lax.axis_index("lmk")]).astype(jnp.int32)
    points, halves, assignment, panel_mine, panel_other = call(
        fetch_kernel,
        (
            array((point_rows, width)),
            array((parts, half, width)),
            array((1, point_rows), jnp.int32),
            array((depth // 2, columns)),
            array((depth // 2, columns)),
        ),
        points,
        landmarks,
        assignment.reshape(1, point_rows),
        panels,
        place=place,
        scratch=[pltpu.SemaphoreType.DMA((3 * parts + 2,))],
        kept=True,
    )
    halves = lax.all_to_all(halves, "lmk", split_axis=0, concat_axis=0, tiled=True)
    placed, tags = call(
        lambda *refs: place_kernel(groups, capacity, *refs),
        (array((slots, width)), array((slots, lanes - depth // 2))),
        points,
        assignment,
    )
    partner = swap(placed, "pts", 1)
    blocks = spread(panel_mine, panel_other, panel_index[0], groups)
    rows = call(
        lambda *refs: rows_kernel(groups, capacity, *refs),
        array((groups, 2, capacity, lanes) if capacity % 16 == 0 else (2, slots, lanes)),
        placed,
        partner,
        tags,
        halves,
        scratch=[pltpu.VMEM((depth // 2, width), jnp.bfloat16)],
    )
    even, odd = exchange(rows, groups, capacity)
    totals, counts = call(
        lambda *refs: sums_kernel(CLUSTERS / (point_rows * groups), *refs),
        (array((owned, columns), jnp.float32), array((1, owned), jnp.int32)),
        even,
        odd,
        *blocks,
        scratch=[pltpu.VMEM((2, lanes, columns), jnp.bfloat16)],
    )
    return (totals, counts.reshape(owned))


def solution(mesh):
    in_specs = (P("pts", None), P("lmk", None), P("pts", None, "lmk"), P(), P("pts"))
    out_specs = (P("pts", "lmk"), P("pts"))
    return jax.shard_map(body, mesh=mesh, in_specs=in_specs, out_specs=out_specs, check_vma=False)
```

```python
import math

import jax
import jax.numpy as jnp
from jax import lax
from jax.experimental import pallas as pl
from jax.experimental.pallas import tpu as pltpu
from jax.sharding import PartitionSpec as P

CLUSTERS = 4096
LANES = 128
VMEM_LIMIT = 48 * 1024 * 1024
FETCH_LIMIT = 60 * 1024 * 1024
NT = (((1,), (1,)), ((), ()))


def unit_rows(values_in):
    widened = values_in.astype(jnp.float32)
    scale = lax.rsqrt(jnp.mean(widened * widened, axis=1, keepdims=True) + 1e-06)
    return (widened * scale).astype(jnp.bfloat16)


def fetch_kernel(place_ref, marks_ref, panel_ref, halves_out, mine_out, other_out, sems):
    parts, half = halves_out.shape[:2]
    core = lax.rem(place_ref[0], 2)
    pairs = []
    for part in range(parts):
        pairs.append(
            (marks_ref.at[pl.ds(pl.multiple_of(core * half, 16), half), :], halves_out.at[part])
        )
        for out, side in ((mine_out, core), (other_out, 1 - core)):
            first = pl.multiple_of((2 * part + side) * half, 16)
            pairs.append(
                (
                    panel_ref.at[0, pl.ds(first, half), :],
                    out.at[part * half : (part + 1) * half, :],
                )
            )
    copies = [pltpu.make_async_copy(*pair, sems.at[at]) for at, pair in enumerate(pairs)]
    for copy in copies:
        copy.start()
    for copy in copies:
        copy.wait()


def place_kernel(groups, capacity, points_ref, assignment_ref, points_out, tags_out):
    point_rows = points_ref.shape[0]
    ids = assignment_ref[...]
    owned = CLUSTERS // groups
    owners = lax.div(ids, owned)
    tags = ids - owners * owned + 1
    hits = lax.broadcasted_iota(jnp.int32, (groups, point_rows), 0) == owners
    earlier = lax.broadcasted_iota(jnp.int32, (point_rows, point_rows), 0) < lax.broadcasted_iota(
        jnp.int32, (point_rows, point_rows), 1
    )
    before = jnp.dot(
        hits.astype(jnp.float32).astype(jnp.bfloat16),
        earlier.astype(jnp.float32).astype(jnp.bfloat16),
        preferred_element_type=jnp.float32,
    )
    rank = jnp.sum(jnp.where(hits, before, 0.0), axis=0, keepdims=True).astype(jnp.int32)
    slots = owners * capacity + rank
    placed = (
        (lax.broadcasted_iota(jnp.int32, (groups * capacity, point_rows), 0) == slots)
        .astype(jnp.float32)
        .astype(jnp.bfloat16)
    )
    points_out[...] = jnp.dot(
        placed, unit_rows(points_ref[...]), preferred_element_type=jnp.float32
    ).astype(jnp.bfloat16)
    high = lax.div(tags, 256)
    which = lax.broadcasted_iota(jnp.int32, (tags_out.shape[1], point_rows), 0)
    coded = jnp.where(which == 0, high, jnp.where(which == 1, tags - high * 256, 0))
    tags_out[...] = lax.dot_general(
        placed,
        coded.astype(jnp.float32).astype(jnp.bfloat16),
        NT,
        preferred_element_type=jnp.float32,
    ).astype(jnp.bfloat16)


def rows_kernel(groups, capacity, points_ref, partner_ref, tags_ref, halves_ref, out_ref, marks_ref):
    half, marks = halves_ref.shape[1], marks_ref.shape[0]
    slots = points_ref.shape[0]
    tag_lanes = tags_ref.shape[1]
    for part in range(halves_ref.shape[0]):
        marks_ref[part * half : (part + 1) * half, :] = unit_rows(halves_ref[part])
    for core, (placed, tags) in enumerate(
        ((points_ref, tags_ref[...]), (partner_ref, jnp.zeros((slots, tag_lanes), jnp.bfloat16)))
    ):
        scores = lax.dot_general(placed[...], marks_ref[...], NT, preferred_element_type=jnp.float32)
        rows = jnp.exp(scores * (0.5 / math.sqrt(placed.shape[1]))).astype(jnp.bfloat16)
        if len(out_ref.shape) == 4:
            for group in range(groups):
                here = slice(group * capacity, (group + 1) * capacity)
                out_ref[group, core, :, :marks] = rows[here]
                out_ref[group, core, :, marks:] = tags[here]
        else:
            out_ref[core, :, :marks] = rows
            out_ref[core, :, marks:] = tags


def sums_kernel(scale, even_ref, odd_ref, *refs):
    blocks, totals_ref, counts_ref, panel_ref = refs[:-3], refs[-3], refs[-2], refs[-1]
    slots, lanes = even_ref.shape
    owned = totals_ref.shape[0]
    for side in range(2):
        first = 0
        for block in blocks[side * len(blocks) // 2 : (side + 1) * len(blocks) // 2]:
            panel_ref[side, first : first + block.shape[0], :] = block[...]
            first += block.shape[0]
        marks = first
        panel_ref[side, marks:, :] = jnp.zeros((lanes - marks, panel_ref.shape[2]), jnp.bfloat16)
    features = (
        jnp.dot(even_ref[...], panel_ref[0], preferred_element_type=jnp.float32)
        + jnp.dot(odd_ref[...], panel_ref[1], preferred_element_type=jnp.float32)
    ).astype(jnp.bfloat16)
    which = lax.broadcasted_iota(jnp.int32, (8, lanes - marks), 1)
    weights = jnp.where(which == 0, 256.0, jnp.where(which == 1, 1.0, 0.0)).astype(jnp.bfloat16)
    tags = lax.dot_general(weights, even_ref[:, marks:], NT, preferred_element_type=jnp.float32)
    tags += lax.dot_general(weights, odd_ref[:, marks:], NT, preferred_element_type=jnp.float32)
    tags = tags[:1].astype(jnp.int32)
    member = (
        (lax.broadcasted_iota(jnp.int32, (owned, slots), 0) + 1 == tags)
        .astype(jnp.float32)
        .astype(jnp.bfloat16)
    )
    totals_ref[...] = jnp.dot(member, features, preferred_element_type=jnp.float32) * scale
    counts_ref[...] = lax.dot_general(
        jnp.ones((8, slots), jnp.bfloat16), member, NT, preferred_element_type=jnp.float32
    )[:1].astype(jnp.int32)


def call(kernel, shapes, *operands, place=None, scratch=(), kept=False):
    held = pl.BlockSpec(memory_space=pl.ANY if kept else pltpu.VMEM)
    many = isinstance(shapes, tuple)
    scalar = [] if place is None else [place]
    return pl.pallas_call(
        kernel,
        out_shape=shapes,
        in_specs=[pl.BlockSpec(memory_space=pltpu.SMEM)] * len(scalar) + [held] * len(operands),
        out_specs=(held,) * len(shapes) if many else held,
        scratch_shapes=scratch,
        compiler_params=pltpu.CompilerParams(vmem_limit_bytes=FETCH_LIMIT if kept else VMEM_LIMIT),
    )(*scalar, *operands)


def array(shape, dtype=jnp.bfloat16):
    return jax.ShapeDtypeStruct(shape, dtype)


def swap(block, axis, mask):
    return lax.ppermute(block, axis, [(i, i ^ mask) for i in range(lax.axis_size(axis))])


def spread(mine, other, holder, groups):
    me = lax.axis_index("pts")

    def pick(block, mask):
        return jnp.where(((holder ^ me) & mask) == 0, block, swap(block, "pts", mask))

    mine = jnp.where(((holder ^ me) & 1) == 0, mine, swap(other, "pts", 1))
    masks = [1 << bit for bit in range(1, groups.bit_length() - 1)]
    size = mine.shape[0] // len(masks)
    blocks = [mine[at * size : (at + 1) * size] for at in range(len(masks))]
    for turn in range(len(masks)):
        blocks = [
            pick(block, masks[(at + turn) % len(masks)]) for at, block in enumerate(blocks)
        ]
    return blocks + [swap(block, "pts", 1) for block in blocks]


def exchange(rows, groups, capacity):
    slots, lanes = groups * capacity, rows.shape[-1]
    if rows.ndim == 3:
        rows = rows.reshape(2, groups, capacity, lanes).swapaxes(0, 1)
    arrived = lax.all_to_all(
        rows.reshape(groups, 2 * capacity, lanes), "pts", split_axis=0, concat_axis=0, tiled=True
    ).reshape(groups // 2, 2, 2 * capacity, lanes)
    core = lax.axis_index("pts") % 2
    even = lax.dynamic_index_in_dim(arrived, core, 1, keepdims=False)
    odd = lax.dynamic_index_in_dim(arrived, 1 - core, 1, keepdims=False)
    odd = jnp.concatenate([odd[:, capacity:], odd[:, :capacity]], axis=1)
    return even.reshape(slots, lanes), odd.reshape(slots, lanes)


def body(points, landmarks, panels, panel_index, assignment):
    groups, parts = lax.axis_size("pts"), lax.axis_size("lmk")
    point_rows, width = points.shape
    capacity = 2 * point_rows // groups
    slots = groups * capacity
    owned = CLUSTERS // groups
    depth, columns = panels.shape[1:]
    half = landmarks.shape[0] // 2
    lanes = -(-(depth // 2 + 2) // LANES) * LANES
    place = jnp.stack([lax.axis_index("pts"), lax.axis_index("lmk")]).astype(jnp.int32)
    halves, panel_mine, panel_other = call(
        fetch_kernel,
        (
            array((parts, half, width)),
            array((depth // 2, columns)),
            array((depth // 2, columns)),
        ),
        landmarks,
        panels,
        place=place,
        scratch=[pltpu.SemaphoreType.DMA((3 * parts,))],
        kept=True,
    )
    halves = lax.all_to_all(halves, "lmk", split_axis=0, concat_axis=0, tiled=True)
    placed, tags = call(
        lambda *refs: place_kernel(groups, capacity, *refs),
        (array((slots, width)), array((slots, lanes - depth // 2))),
        points,
        assignment.reshape(1, point_rows),
    )
    partner = swap(placed, "pts", 1)
    blocks = spread(panel_mine, panel_other, panel_index[0], groups)
    rows = call(
        lambda *refs: rows_kernel(groups, capacity, *refs),
        array((groups, 2, capacity, lanes) if capacity % 16 == 0 else (2, slots, lanes)),
        placed,
        partner,
        tags,
        halves,
        scratch=[pltpu.VMEM((depth // 2, width), jnp.bfloat16)],
    )
    even, odd = exchange(rows, groups, capacity)
    totals, counts = call(
        lambda *refs: sums_kernel(CLUSTERS / (point_rows * groups), *refs),
        (array((owned, columns), jnp.float32), array((1, owned), jnp.int32)),
        even,
        odd,
        *blocks,
        scratch=[pltpu.VMEM((2, lanes, columns), jnp.bfloat16)],
    )
    return (totals, counts.reshape(owned))


def solution(mesh):
    in_specs = (P("pts", None), P("lmk", None), P("pts", None, "lmk"), P(), P("pts"))
    out_specs = (P("pts", "lmk"), P("pts"))
    return jax.shard_map(body, mesh=mesh, in_specs=in_specs, out_specs=out_specs, check_vma=False)
```

```python
import math

import jax
import jax.numpy as jnp
from jax import lax
from jax.experimental import pallas as pl
from jax.experimental.pallas import tpu as pltpu
from jax.sharding import PartitionSpec as P

CLUSTERS = 4096
LANES = 128
VMEM_LIMIT = 48 * 1024 * 1024
NT = (((1,), (1,)), ((), ()))


def unit_rows(values_in):
    widened = values_in.astype(jnp.float32)
    scale = lax.rsqrt(jnp.mean(widened * widened, axis=1, keepdims=True) + 1e-06)
    return (widened * scale).astype(jnp.bfloat16)


def pick_kernel(keep_ref, *refs):
    outs = refs[-(len(refs) // 3) :]
    for at, out in enumerate(outs):
        out[...] = jnp.where(keep_ref[at] != 0, refs[2 * at][...], refs[2 * at + 1][...])


def place_kernel(groups, capacity, points_ref, assignment_ref, after_ref, points_out, tags_out):
    point_rows = points_ref.shape[0]
    ids = assignment_ref[...]
    owned = CLUSTERS // groups
    owners = lax.div(ids, owned)
    tags = ids - owners * owned + 1
    hits = lax.broadcasted_iota(jnp.int32, (groups, point_rows), 0) == owners
    earlier = lax.broadcasted_iota(jnp.int32, (point_rows, point_rows), 0) < lax.broadcasted_iota(
        jnp.int32, (point_rows, point_rows), 1
    )
    before = jnp.dot(
        hits.astype(jnp.float32).astype(jnp.bfloat16),
        earlier.astype(jnp.float32).astype(jnp.bfloat16),
        preferred_element_type=jnp.float32,
    )
    rank = jnp.sum(jnp.where(hits, before, 0.0), axis=0, keepdims=True).astype(jnp.int32)
    slots = owners * capacity + rank
    placed = (
        (lax.broadcasted_iota(jnp.int32, (groups * capacity, point_rows), 0) == slots)
        .astype(jnp.float32)
        .astype(jnp.bfloat16)
    )
    points_out[...] = jnp.dot(
        placed, unit_rows(points_ref[...]), preferred_element_type=jnp.float32
    ).astype(jnp.bfloat16)
    high = lax.div(tags, 256)
    which = lax.broadcasted_iota(jnp.int32, (tags_out.shape[1], point_rows), 0)
    coded = jnp.where(which == 0, high, jnp.where(which == 1, tags - high * 256, 0))
    tags_out[...] = lax.dot_general(
        placed,
        coded.astype(jnp.float32).astype(jnp.bfloat16),
        NT,
        preferred_element_type=jnp.float32,
    ).astype(jnp.bfloat16)


def rows_kernel(groups, capacity, place_ref, points_ref, partner_ref, tags_ref, *refs):
    halves, out_ref, marks_ref = refs[:-2], refs[-2], refs[-1]
    half, marks = halves[0].shape[0], marks_ref.shape[0]
    slots = points_ref.shape[0]
    tag_lanes = tags_ref.shape[1]
    for away, block in enumerate(halves):
        first = pl.multiple_of(lax.bitwise_xor(place_ref[0], away) * half, 16)
        marks_ref[pl.ds(first, half), :] = unit_rows(block[...])
    for core, (placed, tags) in enumerate(
        ((points_ref, tags_ref[...]), (partner_ref, jnp.zeros((slots, tag_lanes), jnp.bfloat16)))
    ):
        scores = lax.dot_general(placed[...], marks_ref[...], NT, preferred_element_type=jnp.float32)
        rows = jnp.exp(scores * (0.5 / math.sqrt(placed.shape[1]))).astype(jnp.bfloat16)
        if len(out_ref.shape) == 4:
            for group in range(groups):
                here = slice(group * capacity, (group + 1) * capacity)
                out_ref[group, core, :, :marks] = rows[here]
                out_ref[group, core, :, marks:] = tags[here]
        else:
            out_ref[core, :, :marks] = rows
            out_ref[core, :, marks:] = tags


def sums_kernel(scale, even_ref, odd_ref, *refs):
    blocks, totals_ref, counts_ref, panel_ref = refs[:-3], refs[-3], refs[-2], refs[-1]
    slots, lanes = even_ref.shape
    owned = totals_ref.shape[0]
    for side in range(2):
        first = 0
        for block in blocks[side * len(blocks) // 2 : (side + 1) * len(blocks) // 2]:
            panel_ref[side, first : first + block.shape[0], :] = block[...]
            first += block.shape[0]
        marks = first
        panel_ref[side, marks:, :] = jnp.zeros((lanes - marks, panel_ref.shape[2]), jnp.bfloat16)
    features = (
        jnp.dot(even_ref[...], panel_ref[0], preferred_element_type=jnp.float32)
        + jnp.dot(odd_ref[...], panel_ref[1], preferred_element_type=jnp.float32)
    ).astype(jnp.bfloat16)
    which = lax.broadcasted_iota(jnp.int32, (8, lanes - marks), 1)
    weights = jnp.where(which == 0, 256.0, jnp.where(which == 1, 1.0, 0.0)).astype(jnp.bfloat16)
    tags = lax.dot_general(weights, even_ref[:, marks:], NT, preferred_element_type=jnp.float32)
    tags += lax.dot_general(weights, odd_ref[:, marks:], NT, preferred_element_type=jnp.float32)
    tags = tags[:1].astype(jnp.int32)
    member = (
        (lax.broadcasted_iota(jnp.int32, (owned, slots), 0) + 1 == tags)
        .astype(jnp.float32)
        .astype(jnp.bfloat16)
    )
    totals_ref[...] = jnp.dot(member, features, preferred_element_type=jnp.float32) * scale
    counts_ref[...] = lax.dot_general(
        jnp.ones((8, slots), jnp.bfloat16), member, NT, preferred_element_type=jnp.float32
    )[:1].astype(jnp.int32)


def call(kernel, shapes, *operands, place=None, after=None, scratch=()):
    held, loose = pl.BlockSpec(memory_space=pltpu.VMEM), pl.BlockSpec(memory_space=pl.ANY)
    first = [] if place is None else [place]
    last = [] if after is None else [after]
    return pl.pallas_call(
        kernel,
        out_shape=shapes,
        in_specs=[pl.BlockSpec(memory_space=pltpu.SMEM)] * len(first)
        + [held] * len(operands)
        + [loose] * len(last),
        out_specs=(held,) * len(shapes) if isinstance(shapes, tuple) else held,
        scratch_shapes=scratch,
        compiler_params=pltpu.CompilerParams(vmem_limit_bytes=VMEM_LIMIT),
    )(*first, *operands, *last)


def array(shape, dtype=jnp.bfloat16):
    return jax.ShapeDtypeStruct(shape, dtype)


def swap(block, axis, mask):
    return lax.ppermute(block, axis, [(i, i ^ mask) for i in range(lax.axis_size(axis))])


def spread(panel, parts, holder, groups):
    me = lax.axis_index("pts")
    sides = panel.reshape(parts, 2, -1, panel.shape[1])
    mine, other = (
        lax.dynamic_index_in_dim(sides, side, 1, keepdims=False).reshape(-1, panel.shape[1])
        for side in (me % 2, 1 - me % 2)
    )
    mine = jnp.where(((holder ^ me) & 1) == 0, mine, swap(other, "pts", 1))
    masks = [1 << bit for bit in range(1, groups.bit_length() - 1)]
    size = mine.shape[0] // len(masks)
    pairs = []
    for at, mask in enumerate(masks):
        block = mine[at * size : (at + 1) * size]
        pairs += [block, swap(block, "pts", mask)]
    keep = jnp.stack([((holder ^ me) & mask) == 0 for mask in masks]).astype(jnp.int32)
    return masks, pairs, keep


def spread_on(blocks, masks, holder):
    me = lax.axis_index("pts")
    for turn in range(1, len(masks)):
        for at, block in enumerate(blocks):
            mask = masks[(at + turn) % len(masks)]
            blocks[at] = jnp.where(((holder ^ me) & mask) == 0, block, swap(block, "pts", mask))
    return blocks + [swap(block, "pts", 1) for block in blocks]


def exchange(rows, groups, capacity):
    slots, lanes = groups * capacity, rows.shape[-1]
    if rows.ndim == 3:
        rows = rows.reshape(2, groups, capacity, lanes).swapaxes(0, 1)
    arrived = lax.all_to_all(
        rows.reshape(groups, 2 * capacity, lanes), "pts", split_axis=0, concat_axis=0, tiled=True
    ).reshape(groups // 2, 2, 2 * capacity, lanes)
    core = lax.axis_index("pts") % 2
    even = lax.dynamic_index_in_dim(arrived, core, 1, keepdims=False)
    odd = lax.dynamic_index_in_dim(arrived, 1 - core, 1, keepdims=False)
    odd = jnp.concatenate([odd[:, capacity:], odd[:, :capacity]], axis=1)
    return even.reshape(slots, lanes), odd.reshape(slots, lanes)


def body(points, landmarks, panels, panel_index, assignment):
    groups, parts = lax.axis_size("pts"), lax.axis_size("lmk")
    point_rows, width = points.shape
    capacity = 2 * point_rows // groups
    slots = groups * capacity
    owned = CLUSTERS // groups
    depth, columns = panels.shape[1:]
    half = landmarks.shape[0] // 2
    lanes = -(-(depth // 2 + 2) // LANES) * LANES
    line = lax.axis_index("lmk").astype(jnp.int32).reshape(1)
    mine = lax.dynamic_slice_in_dim(landmarks, (lax.axis_index("pts") % 2) * half, half, 0)
    halves = [mine] + [swap(mine, "lmk", mask) for mask in range(1, parts)]
    masks, pairs, keep = spread(panels[0], parts, panel_index[0], groups)
    placed, tags = call(
        lambda *refs: place_kernel(groups, capacity, *refs),
        (array((slots, width)), array((slots, lanes - depth // 2))),
        points,
        assignment.reshape(1, point_rows),
        after=pairs[0],
    )
    partner = swap(placed, "pts", 1)
    rows = call(
        lambda *refs: rows_kernel(groups, capacity, *refs),
        array((groups, 2, capacity, lanes) if capacity % 16 == 0 else (2, slots, lanes)),
        placed,
        partner,
        tags,
        *halves,
        place=line,
        scratch=[pltpu.VMEM((depth // 2, width), jnp.bfloat16)],
    )
    blocks = call(pick_kernel, (array(pairs[0].shape),) * len(masks), *pairs, place=keep, after=rows)
    blocks = spread_on(list(blocks), masks, panel_index[0])
    even, odd = exchange(rows, groups, capacity)
    totals, counts = call(
        lambda *refs: sums_kernel(CLUSTERS / (point_rows * groups), *refs),
        (array((owned, columns), jnp.float32), array((1, owned), jnp.int32)),
        even,
        odd,
        *blocks,
        scratch=[pltpu.VMEM((2, lanes, columns), jnp.bfloat16)],
    )
    return (totals, counts.reshape(owned))


def solution(mesh):
    in_specs = (P("pts", None), P("lmk", None), P("pts", None, "lmk"), P(), P("pts"))
    out_specs = (P("pts", "lmk"), P("pts"))
    return jax.shard_map(body, mesh=mesh, in_specs=in_specs, out_specs=out_specs, check_vma=False)
```

```python
import math

import jax
import jax.numpy as jnp
from jax import lax
from jax.experimental import pallas as pl
from jax.experimental.pallas import tpu as pltpu
from jax.sharding import PartitionSpec as P

CLUSTERS = 4096
LANES = 128
VMEM_LIMIT = 48 * 1024 * 1024
NT = (((1,), (1,)), ((), ()))


def unit_rows(values_in):
    widened = values_in.astype(jnp.float32)
    scale = lax.rsqrt(jnp.mean(widened * widened, axis=1, keepdims=True) + 1e-06)
    return (widened * scale).astype(jnp.bfloat16)


def place_kernel(groups, capacity, *refs):
    points_out, tags_out = refs[-2:]
    for core in range(2):
        points_ref, assignment_ref = refs[2 * core : 2 * core + 2]
        point_rows = points_ref.shape[0]
        ids = assignment_ref[...]
        owned = CLUSTERS // groups
        owners = lax.div(ids, owned)
        tags = ids - owners * owned + 1
        hits = lax.broadcasted_iota(jnp.int32, (groups, point_rows), 0) == owners
        earlier = lax.broadcasted_iota(
            jnp.int32, (point_rows, point_rows), 0
        ) < lax.broadcasted_iota(jnp.int32, (point_rows, point_rows), 1)
        before = jnp.dot(
            hits.astype(jnp.float32).astype(jnp.bfloat16),
            earlier.astype(jnp.float32).astype(jnp.bfloat16),
            preferred_element_type=jnp.float32,
        )
        rank = jnp.sum(jnp.where(hits, before, 0.0), axis=0, keepdims=True).astype(jnp.int32)
        slots = owners * capacity + rank
        placed = (
            (lax.broadcasted_iota(jnp.int32, (groups * capacity, point_rows), 0) == slots)
            .astype(jnp.float32)
            .astype(jnp.bfloat16)
        )
        points_out[core] = jnp.dot(
            placed, unit_rows(points_ref[...]), preferred_element_type=jnp.float32
        ).astype(jnp.bfloat16)
        if core == 0:
            high = lax.div(tags, 256)
            which = lax.broadcasted_iota(jnp.int32, (tags_out.shape[1], point_rows), 0)
            coded = jnp.where(which == 0, high, jnp.where(which == 1, tags - high * 256, 0))
            tags_out[...] = lax.dot_general(
                placed,
                coded.astype(jnp.float32).astype(jnp.bfloat16),
                NT,
                preferred_element_type=jnp.float32,
            ).astype(jnp.bfloat16)


def rows_kernel(groups, capacity, place_ref, points_ref, tags_ref, *refs):
    halves, out_ref, marks_ref = refs[:-2], refs[-2], refs[-1]
    half, marks = halves[0].shape[0], marks_ref.shape[0]
    no_tags = jnp.zeros(tags_ref.shape, jnp.bfloat16)
    for away, block in enumerate(halves):
        first = pl.multiple_of(lax.bitwise_xor(place_ref[0], away) * half, 16)
        marks_ref[pl.ds(first, half), :] = unit_rows(block[...])
    for core, tags in enumerate((tags_ref[...], no_tags)):
        scores = lax.dot_general(
            points_ref[core], marks_ref[...], NT, preferred_element_type=jnp.float32
        )
        rows = jnp.exp(scores * (0.5 / math.sqrt(points_ref.shape[2]))).astype(jnp.bfloat16)
        if len(out_ref.shape) == 4:
            for group in range(groups):
                here = slice(group * capacity, (group + 1) * capacity)
                out_ref[group, core, :, :marks] = rows[here]
                out_ref[group, core, :, marks:] = tags[here]
        else:
            out_ref[core, :, :marks] = rows
            out_ref[core, :, marks:] = tags


def sums_kernel(scale, even_ref, odd_ref, *refs):
    blocks, totals_ref, counts_ref, panel_ref = refs[:-3], refs[-3], refs[-2], refs[-1]
    slots, lanes = even_ref.shape
    owned = totals_ref.shape[0]
    for side in range(2):
        first = 0
        for block in blocks[side * len(blocks) // 2 : (side + 1) * len(blocks) // 2]:
            panel_ref[side, first : first + block.shape[0], :] = block[...]
            first += block.shape[0]
        marks = first
        panel_ref[side, marks:, :] = jnp.zeros((lanes - marks, panel_ref.shape[2]), jnp.bfloat16)
    features = (
        jnp.dot(even_ref[...], panel_ref[0], preferred_element_type=jnp.float32)
        + jnp.dot(odd_ref[...], panel_ref[1], preferred_element_type=jnp.float32)
    ).astype(jnp.bfloat16)
    which = lax.broadcasted_iota(jnp.int32, (8, lanes - marks), 1)
    weights = jnp.where(which == 0, 256.0, jnp.where(which == 1, 1.0, 0.0)).astype(jnp.bfloat16)
    tags = lax.dot_general(weights, even_ref[:, marks:], NT, preferred_element_type=jnp.float32)
    tags += lax.dot_general(weights, odd_ref[:, marks:], NT, preferred_element_type=jnp.float32)
    tags = tags[:1].astype(jnp.int32)
    member = (
        (lax.broadcasted_iota(jnp.int32, (owned, slots), 0) + 1 == tags)
        .astype(jnp.float32)
        .astype(jnp.bfloat16)
    )
    totals_ref[...] = jnp.dot(member, features, preferred_element_type=jnp.float32) * scale
    counts_ref[...] = lax.dot_general(
        jnp.ones((8, slots), jnp.bfloat16), member, NT, preferred_element_type=jnp.float32
    )[:1].astype(jnp.int32)


def call(kernel, shapes, *operands, place=None, scratch=()):
    held = pl.BlockSpec(memory_space=pltpu.VMEM)
    first = [] if place is None else [place]
    return pl.pallas_call(
        kernel,
        out_shape=shapes,
        in_specs=[pl.BlockSpec(memory_space=pltpu.SMEM)] * len(first) + [held] * len(operands),
        out_specs=(held,) * len(shapes) if isinstance(shapes, tuple) else held,
        scratch_shapes=scratch,
        compiler_params=pltpu.CompilerParams(vmem_limit_bytes=VMEM_LIMIT),
    )(*first, *operands)


def array(shape, dtype=jnp.bfloat16):
    return jax.ShapeDtypeStruct(shape, dtype)


def swap(block, axis, mask):
    return lax.ppermute(block, axis, [(i, i ^ mask) for i in range(lax.axis_size(axis))])


def spread(panel, parts, holder, groups):
    me = lax.axis_index("pts")
    sides = panel.reshape(parts, 2, -1, panel.shape[1])
    mine, other = (
        lax.dynamic_index_in_dim(sides, side, 1, keepdims=False).reshape(-1, panel.shape[1])
        for side in (me % 2, 1 - me % 2)
    )

    def pick(block, mask):
        return jnp.where(((holder ^ me) & mask) == 0, block, swap(block, "pts", mask))

    mine = jnp.where(((holder ^ me) & 1) == 0, mine, swap(other, "pts", 1))
    masks = [1 << bit for bit in range(1, groups.bit_length() - 1)]
    size = mine.shape[0] // len(masks)
    blocks = [mine[at * size : (at + 1) * size] for at in range(len(masks))]
    for turn in range(len(masks)):
        blocks = [
            pick(block, masks[(at + turn) % len(masks)]) for at, block in enumerate(blocks)
        ]
    return blocks + [swap(block, "pts", 1) for block in blocks]


def exchange(rows, groups, capacity):
    slots, lanes = groups * capacity, rows.shape[-1]
    if rows.ndim == 3:
        rows = rows.reshape(2, groups, capacity, lanes).swapaxes(0, 1)
    arrived = lax.all_to_all(
        rows.reshape(groups, 2 * capacity, lanes), "pts", split_axis=0, concat_axis=0, tiled=True
    ).reshape(groups // 2, 2, 2 * capacity, lanes)
    core = lax.axis_index("pts") % 2
    even = lax.dynamic_index_in_dim(arrived, core, 1, keepdims=False)
    odd = lax.dynamic_index_in_dim(arrived, 1 - core, 1, keepdims=False)
    odd = jnp.concatenate([odd[:, capacity:], odd[:, :capacity]], axis=1)
    return even.reshape(slots, lanes), odd.reshape(slots, lanes)


def body(points, landmarks, panels, panel_index, assignment):
    groups, parts = lax.axis_size("pts"), lax.axis_size("lmk")
    point_rows, width = points.shape
    capacity = 2 * point_rows // groups
    slots = groups * capacity
    owned = CLUSTERS // groups
    depth, columns = panels.shape[1:]
    half = landmarks.shape[0] // 2
    lanes = -(-(depth // 2 + 2) // LANES) * LANES
    line = lax.axis_index("lmk").astype(jnp.int32).reshape(1)
    mine = lax.dynamic_slice_in_dim(landmarks, (lax.axis_index("pts") % 2) * half, half, 0)
    halves = [mine] + [swap(mine, "lmk", mask) for mask in range(1, parts)]
    blocks = spread(panels[0], parts, panel_index[0], groups)
    assignment = assignment.reshape(1, point_rows)
    placed, tags = call(
        lambda *refs: place_kernel(groups, capacity, *refs),
        (array((2, slots, width)), array((slots, lanes - depth // 2))),
        points,
        assignment,
        swap(points, "pts", 1),
        swap(assignment, "pts", 1),
    )
    rows = call(
        lambda *refs: rows_kernel(groups, capacity, *refs),
        array((groups, 2, capacity, lanes) if capacity % 16 == 0 else (2, slots, lanes)),
        placed,
        tags,
        *halves,
        place=line,
        scratch=[pltpu.VMEM((depth // 2, width), jnp.bfloat16)],
    )
    even, odd = exchange(rows, groups, capacity)
    totals, counts = call(
        lambda *refs: sums_kernel(CLUSTERS / (point_rows * groups), *refs),
        (array((owned, columns), jnp.float32), array((1, owned), jnp.int32)),
        even,
        odd,
        *blocks,
        scratch=[pltpu.VMEM((2, lanes, columns), jnp.bfloat16)],
    )
    return (totals, counts.reshape(owned))


def solution(mesh):
    in_specs = (P("pts", None), P("lmk", None), P("pts", None, "lmk"), P(), P("pts"))
    out_specs = (P("pts", "lmk"), P("pts"))
    return jax.shard_map(body, mesh=mesh, in_specs=in_specs, out_specs=out_specs, check_vma=False)
```

```python
import math

import jax
import jax.numpy as jnp
from jax import lax
from jax.experimental import pallas as pl
from jax.experimental.pallas import tpu as pltpu
from jax.sharding import PartitionSpec as P

CLUSTERS = 4096
LANES = 128
VMEM_LIMIT = 48 * 1024 * 1024
NT = (((1,), (1,)), ((), ()))


def unit_rows(values_in):
    widened = values_in.astype(jnp.float32)
    scale = lax.rsqrt(jnp.mean(widened * widened, axis=1, keepdims=True) + 1e-06)
    return (widened * scale).astype(jnp.bfloat16)


def place_kernel(groups, capacity, *refs):
    points_out, tags_out = refs[-2:]
    for core in range(2):
        points_ref, assignment_ref = refs[2 * core : 2 * core + 2]
        point_rows = points_ref.shape[0]
        ids = assignment_ref[...]
        owned = CLUSTERS // groups
        owners = lax.div(ids, owned)
        tags = ids - owners * owned + 1
        hits = lax.broadcasted_iota(jnp.int32, (groups, point_rows), 0) == owners
        earlier = lax.broadcasted_iota(
            jnp.int32, (point_rows, point_rows), 0
        ) < lax.broadcasted_iota(jnp.int32, (point_rows, point_rows), 1)
        before = jnp.dot(
            hits.astype(jnp.float32).astype(jnp.bfloat16),
            earlier.astype(jnp.float32).astype(jnp.bfloat16),
            preferred_element_type=jnp.float32,
        )
        rank = jnp.sum(jnp.where(hits, before, 0.0), axis=0, keepdims=True).astype(jnp.int32)
        slots = owners * capacity + rank
        placed = (
            (lax.broadcasted_iota(jnp.int32, (groups * capacity, point_rows), 0) == slots)
            .astype(jnp.float32)
            .astype(jnp.bfloat16)
        )
        points_out[core] = jnp.dot(
            placed, unit_rows(points_ref[...]), preferred_element_type=jnp.float32
        ).astype(jnp.bfloat16)
        if core == 0:
            high = lax.div(tags, 256)
            which = lax.broadcasted_iota(jnp.int32, (tags_out.shape[1], point_rows), 0)
            coded = jnp.where(which == 0, high, jnp.where(which == 1, tags - high * 256, 0))
            tags_out[...] = lax.dot_general(
                placed,
                coded.astype(jnp.float32).astype(jnp.bfloat16),
                NT,
                preferred_element_type=jnp.float32,
            ).astype(jnp.bfloat16)


def rows_kernel(groups, capacity, place_ref, points_ref, tags_ref, *refs):
    halves, out_ref, keep_ref, marks_ref = refs[:-3], refs[-3], refs[-2], refs[-1]
    keep_ref[0] = place_ref[1]
    half, marks = halves[0].shape[0], marks_ref.shape[0]
    no_tags = jnp.zeros(tags_ref.shape, jnp.bfloat16)
    for away, block in enumerate(halves):
        first = pl.multiple_of(lax.bitwise_xor(place_ref[0], away) * half, 16)
        marks_ref[pl.ds(first, half), :] = unit_rows(block[...])
    for core, tags in enumerate((tags_ref[...], no_tags)):
        scores = lax.dot_general(
            points_ref[core], marks_ref[...], NT, preferred_element_type=jnp.float32
        )
        rows = jnp.exp(scores * (0.5 / math.sqrt(points_ref.shape[2]))).astype(jnp.bfloat16)
        if len(out_ref.shape) == 4:
            for group in range(groups):
                here = slice(group * capacity, (group + 1) * capacity)
                out_ref[group, core, :, :marks] = rows[here]
                out_ref[group, core, :, marks:] = tags[here]
        else:
            out_ref[core, :, :marks] = rows
            out_ref[core, :, marks:] = tags


def sums_kernel(scale, even_ref, odd_ref, mine_ref, other_ref, totals_ref, counts_ref, panel_ref):
    slots, lanes = even_ref.shape
    owned, marks = totals_ref.shape[0], mine_ref.shape[0]
    for side, half in enumerate((mine_ref, other_ref)):
        panel_ref[side, :marks, :] = half[...]
        panel_ref[side, marks:, :] = jnp.zeros((lanes - marks, half.shape[1]), jnp.bfloat16)
    features = (
        jnp.dot(even_ref[...], panel_ref[0], preferred_element_type=jnp.float32)
        + jnp.dot(odd_ref[...], panel_ref[1], preferred_element_type=jnp.float32)
    ).astype(jnp.bfloat16)
    which = lax.broadcasted_iota(jnp.int32, (8, lanes - marks), 1)
    weights = jnp.where(which == 0, 256.0, jnp.where(which == 1, 1.0, 0.0)).astype(jnp.bfloat16)
    tags = lax.dot_general(weights, even_ref[:, marks:], NT, preferred_element_type=jnp.float32)
    tags += lax.dot_general(weights, odd_ref[:, marks:], NT, preferred_element_type=jnp.float32)
    tags = tags[:1].astype(jnp.int32)
    member = (
        (lax.broadcasted_iota(jnp.int32, (owned, slots), 0) + 1 == tags)
        .astype(jnp.float32)
        .astype(jnp.bfloat16)
    )
    totals_ref[...] = jnp.dot(member, features, preferred_element_type=jnp.float32) * scale
    counts_ref[...] = lax.dot_general(
        jnp.ones((8, slots), jnp.bfloat16), member, NT, preferred_element_type=jnp.float32
    )[:1].astype(jnp.int32)


def call(kernel, shapes, *operands, place=None, scratch=()):
    held, scalar = pl.BlockSpec(memory_space=pltpu.VMEM), pl.BlockSpec(memory_space=pltpu.SMEM)
    first = [] if place is None else [place]
    return pl.pallas_call(
        kernel,
        out_shape=shapes,
        in_specs=[scalar] * len(first) + [held] * len(operands),
        out_specs=tuple(scalar if shape.shape == (1,) else held for shape in shapes),
        scratch_shapes=scratch,
        compiler_params=pltpu.CompilerParams(vmem_limit_bytes=VMEM_LIMIT),
    )(*first, *operands)


def array(shape, dtype=jnp.bfloat16):
    return jax.ShapeDtypeStruct(shape, dtype)


def swap(block, axis, mask):
    return lax.ppermute(block, axis, [(i, i ^ mask) for i in range(lax.axis_size(axis))])


def spread(panel, parts, holder):
    me = lax.axis_index("pts")
    sides = panel.reshape(parts, 2, -1, panel.shape[1])
    mine, other = (
        lax.dynamic_index_in_dim(sides, side, 1, keepdims=False).reshape(-1, panel.shape[1])
        for side in (me % 2, 1 - me % 2)
    )
    return jnp.where(((holder ^ me) & 1) == 0, mine, swap(other, "pts", 1))


def exchange(rows, groups, capacity):
    slots, lanes = groups * capacity, rows.shape[-1]
    if rows.ndim == 3:
        rows = rows.reshape(2, groups, capacity, lanes).swapaxes(0, 1)
    arrived = lax.all_to_all(
        rows.reshape(groups, 2 * capacity, lanes), "pts", split_axis=0, concat_axis=0, tiled=True
    ).reshape(groups // 2, 2, 2 * capacity, lanes)
    core = lax.axis_index("pts") % 2
    even = lax.dynamic_index_in_dim(arrived, core, 1, keepdims=False)
    odd = lax.dynamic_index_in_dim(arrived, 1 - core, 1, keepdims=False)
    odd = jnp.concatenate([odd[:, capacity:], odd[:, :capacity]], axis=1)
    return even.reshape(slots, lanes), odd.reshape(slots, lanes)


def body(points, landmarks, panels, panel_index, assignment):
    groups, parts = lax.axis_size("pts"), lax.axis_size("lmk")
    point_rows, width = points.shape
    capacity = 2 * point_rows // groups
    slots = groups * capacity
    owned = CLUSTERS // groups
    depth, columns = panels.shape[1:]
    half = landmarks.shape[0] // 2
    lanes = -(-(depth // 2 + 2) // LANES) * LANES
    me = lax.axis_index("pts")
    mine = lax.dynamic_slice_in_dim(landmarks, (me % 2) * half, half, 0)
    halves = [mine] + [swap(mine, "lmk", mask) for mask in range(1, parts)]
    differs = panel_index[0] ^ me
    panel = spread(panels[0], parts, panel_index[0])
    masks = [1 << bit for bit in range(1, groups.bit_length() - 1)]
    panel_met = swap(panel, "pts", masks[0])
    place = jnp.stack([lax.axis_index("lmk"), (differs & masks[0]) == 0]).astype(jnp.int32)
    assignment = assignment.reshape(1, point_rows)
    placed, tags = call(
        lambda *refs: place_kernel(groups, capacity, *refs),
        (array((2, slots, width)), array((slots, lanes - depth // 2))),
        points,
        assignment,
        swap(points, "pts", 1),
        swap(assignment, "pts", 1),
    )
    rows, keep = call(
        lambda *refs: rows_kernel(groups, capacity, *refs),
        (
            array((groups, 2, capacity, lanes) if capacity % 16 == 0 else (2, slots, lanes)),
            array((1,), jnp.int32),
        ),
        placed,
        tags,
        *halves,
        place=place,
        scratch=[pltpu.VMEM((depth // 2, width), jnp.bfloat16)],
    )
    panel = jnp.where(keep[0] != 0, panel, panel_met)
    for mask in masks[1:]:
        panel = jnp.where((differs & mask) == 0, panel, swap(panel, "pts", mask))
    even, odd = exchange(rows, groups, capacity)
    totals, counts = call(
        lambda *refs: sums_kernel(CLUSTERS / (point_rows * groups), *refs),
        (array((owned, columns), jnp.float32), array((1, owned), jnp.int32)),
        even,
        odd,
        panel,
        swap(panel, "pts", 1),
        scratch=[pltpu.VMEM((2, lanes, columns), jnp.bfloat16)],
    )
    return (totals, counts.reshape(owned))


def solution(mesh):
    in_specs = (P("pts", None), P("lmk", None), P("pts", None, "lmk"), P(), P("pts"))
    out_specs = (P("pts", "lmk"), P("pts"))
    return jax.shard_map(body, mesh=mesh, in_specs=in_specs, out_specs=out_specs, check_vma=False)
```

```python
import math

import jax
import jax.numpy as jnp
from jax import lax
from jax.experimental import pallas as pl
from jax.experimental.pallas import tpu as pltpu
from jax.sharding import PartitionSpec as P

CLUSTERS = 4096
LANES = 128
VMEM_LIMIT = 48 * 1024 * 1024
NT = (((1,), (1,)), ((), ()))


def unit_rows(values_in):
    widened = values_in.astype(jnp.float32)
    scale = lax.rsqrt(jnp.mean(widened * widened, axis=1, keepdims=True) + 1e-06)
    return (widened * scale).astype(jnp.bfloat16)


def place_kernel(groups, capacity, *refs):
    points_out, tags_out = refs[-2:]
    for core in range(2):
        points_ref, assignment_ref = refs[2 * core : 2 * core + 2]
        point_rows = points_ref.shape[0]
        ids = assignment_ref[...]
        owned = CLUSTERS // groups
        owners = lax.div(ids, owned)
        tags = ids - owners * owned + 1
        hits = lax.broadcasted_iota(jnp.int32, (groups, point_rows), 0) == owners
        earlier = lax.broadcasted_iota(
            jnp.int32, (point_rows, point_rows), 0
        ) < lax.broadcasted_iota(jnp.int32, (point_rows, point_rows), 1)
        before = jnp.dot(
            hits.astype(jnp.float32).astype(jnp.bfloat16),
            earlier.astype(jnp.float32).astype(jnp.bfloat16),
            preferred_element_type=jnp.float32,
        )
        rank = jnp.sum(jnp.where(hits, before, 0.0), axis=0, keepdims=True).astype(jnp.int32)
        slots = owners * capacity + rank
        placed = (
            (lax.broadcasted_iota(jnp.int32, (groups * capacity, point_rows), 0) == slots)
            .astype(jnp.float32)
            .astype(jnp.bfloat16)
        )
        points_out[core] = jnp.dot(
            placed, unit_rows(points_ref[...]), preferred_element_type=jnp.float32
        ).astype(jnp.bfloat16)
        if core == 0:
            high = lax.div(tags, 256)
            which = lax.broadcasted_iota(jnp.int32, (tags_out.shape[1], point_rows), 0)
            coded = jnp.where(which == 0, high, jnp.where(which == 1, tags - high * 256, 0))
            tags_out[...] = lax.dot_general(
                placed,
                coded.astype(jnp.float32).astype(jnp.bfloat16),
                NT,
                preferred_element_type=jnp.float32,
            ).astype(jnp.bfloat16)


def marks_kernel(place_ref, after_ref, *refs):
    halves, marks_ref, keep_ref = refs[:-2], refs[-2], refs[-1]
    half = halves[0].shape[0]
    for away, block in enumerate(halves):
        first = pl.multiple_of(lax.bitwise_xor(place_ref[0], away) * half, 16)
        marks_ref[pl.ds(first, half), :] = unit_rows(block[...])
    keep_ref[...] = jnp.full(keep_ref.shape, place_ref[1], jnp.int32)


def rows_kernel(groups, capacity, points_ref, tags_ref, marks_ref, out_ref):
    marks = marks_ref.shape[0]
    no_tags = jnp.zeros(tags_ref.shape, jnp.bfloat16)
    for core, tags in enumerate((tags_ref[...], no_tags)):
        scores = lax.dot_general(
            points_ref[core], marks_ref[...], NT, preferred_element_type=jnp.float32
        )
        rows = jnp.exp(scores * (0.5 / math.sqrt(points_ref.shape[2]))).astype(jnp.bfloat16)
        if len(out_ref.shape) == 4:
            for group in range(groups):
                here = slice(group * capacity, (group + 1) * capacity)
                out_ref[group, core, :, :marks] = rows[here]
                out_ref[group, core, :, marks:] = tags[here]
        else:
            out_ref[core, :, :marks] = rows
            out_ref[core, :, marks:] = tags


def sums_kernel(scale, even_ref, odd_ref, mine_ref, other_ref, totals_ref, counts_ref, panel_ref):
    slots, lanes = even_ref.shape
    owned, marks = totals_ref.shape[0], mine_ref.shape[0]
    for side, half in enumerate((mine_ref, other_ref)):
        panel_ref[side, :marks, :] = half[...]
        panel_ref[side, marks:, :] = jnp.zeros((lanes - marks, half.shape[1]), jnp.bfloat16)
    features = (
        jnp.dot(even_ref[...], panel_ref[0], preferred_element_type=jnp.float32)
        + jnp.dot(odd_ref[...], panel_ref[1], preferred_element_type=jnp.float32)
    ).astype(jnp.bfloat16)
    which = lax.broadcasted_iota(jnp.int32, (8, lanes - marks), 1)
    weights = jnp.where(which == 0, 256.0, jnp.where(which == 1, 1.0, 0.0)).astype(jnp.bfloat16)
    tags = lax.dot_general(weights, even_ref[:, marks:], NT, preferred_element_type=jnp.float32)
    tags += lax.dot_general(weights, odd_ref[:, marks:], NT, preferred_element_type=jnp.float32)
    tags = tags[:1].astype(jnp.int32)
    member = (
        (lax.broadcasted_iota(jnp.int32, (owned, slots), 0) + 1 == tags)
        .astype(jnp.float32)
        .astype(jnp.bfloat16)
    )
    totals_ref[...] = jnp.dot(member, features, preferred_element_type=jnp.float32) * scale
    counts_ref[...] = lax.dot_general(
        jnp.ones((8, slots), jnp.bfloat16), member, NT, preferred_element_type=jnp.float32
    )[:1].astype(jnp.int32)


def call(kernel, shapes, *operands, place=None, scratch=()):
    held = pl.BlockSpec(memory_space=pltpu.VMEM)
    first = [] if place is None else [place]
    return pl.pallas_call(
        kernel,
        out_shape=shapes,
        in_specs=[pl.BlockSpec(memory_space=pltpu.SMEM)] * len(first) + [held] * len(operands),
        out_specs=(held,) * len(shapes) if isinstance(shapes, tuple) else held,
        scratch_shapes=scratch,
        compiler_params=pltpu.CompilerParams(vmem_limit_bytes=VMEM_LIMIT),
    )(*first, *operands)


def array(shape, dtype=jnp.bfloat16):
    return jax.ShapeDtypeStruct(shape, dtype)


def swap(block, axis, mask):
    return lax.ppermute(block, axis, [(i, i ^ mask) for i in range(lax.axis_size(axis))])


def spread(panel, parts, holder):
    me = lax.axis_index("pts")
    sides = panel.reshape(parts, 2, -1, panel.shape[1])
    mine, other = (
        lax.dynamic_index_in_dim(sides, side, 1, keepdims=False).reshape(-1, panel.shape[1])
        for side in (me % 2, 1 - me % 2)
    )
    return jnp.where(((holder ^ me) & 1) == 0, mine, swap(other, "pts", 1))


def exchange(rows, groups, capacity):
    slots, lanes = groups * capacity, rows.shape[-1]
    if rows.ndim == 3:
        rows = rows.reshape(2, groups, capacity, lanes).swapaxes(0, 1)
    arrived = lax.all_to_all(
        rows.reshape(groups, 2 * capacity, lanes), "pts", split_axis=0, concat_axis=0, tiled=True
    ).reshape(groups // 2, 2, 2 * capacity, lanes)
    core = lax.axis_index("pts") % 2
    even = lax.dynamic_index_in_dim(arrived, core, 1, keepdims=False)
    odd = lax.dynamic_index_in_dim(arrived, 1 - core, 1, keepdims=False)
    odd = jnp.concatenate([odd[:, capacity:], odd[:, :capacity]], axis=1)
    return even.reshape(slots, lanes), odd.reshape(slots, lanes)


def body(points, landmarks, panels, panel_index, assignment):
    groups, parts = lax.axis_size("pts"), lax.axis_size("lmk")
    point_rows, width = points.shape
    capacity = 2 * point_rows // groups
    slots = groups * capacity
    owned = CLUSTERS // groups
    depth, columns = panels.shape[1:]
    half = landmarks.shape[0] // 2
    lanes = -(-(depth // 2 + 2) // LANES) * LANES
    me = lax.axis_index("pts")
    mine = lax.dynamic_slice_in_dim(landmarks, (me % 2) * half, half, 0)
    halves = [mine] + [swap(mine, "lmk", mask) for mask in range(1, parts)]
    differs = panel_index[0] ^ me
    panel = spread(panels[0], parts, panel_index[0])
    masks = [1 << bit for bit in range(1, groups.bit_length() - 1)]
    panel_met = swap(panel, "pts", masks[0])
    place = jnp.stack([lax.axis_index("lmk"), (differs & masks[0]) == 0]).astype(jnp.int32)
    assignment = assignment.reshape(1, point_rows)
    placed, tags = call(
        lambda *refs: place_kernel(groups, capacity, *refs),
        (array((2, slots, width)), array((slots, lanes - depth // 2))),
        points,
        assignment,
        swap(points, "pts", 1),
        swap(assignment, "pts", 1),
    )
    marks, keep = call(
        marks_kernel,
        (array((depth // 2, width)), array((1, columns), jnp.int32)),
        tags,
        *halves,
        place=place,
    )
    rows = call(
        lambda *refs: rows_kernel(groups, capacity, *refs),
        array((groups, 2, capacity, lanes) if capacity % 16 == 0 else (2, slots, lanes)),
        placed,
        tags,
        marks,
    )
    panel = jnp.where(keep != 0, panel, panel_met)
    for mask in masks[1:]:
        panel = jnp.where((differs & mask) == 0, panel, swap(panel, "pts", mask))
    even, odd = exchange(rows, groups, capacity)
    totals, counts = call(
        lambda *refs: sums_kernel(CLUSTERS / (point_rows * groups), *refs),
        (array((owned, columns), jnp.float32), array((1, owned), jnp.int32)),
        even,
        odd,
        panel,
        swap(panel, "pts", 1),
        scratch=[pltpu.VMEM((2, lanes, columns), jnp.bfloat16)],
    )
    return (totals, counts.reshape(owned))


def solution(mesh):
    in_specs = (P("pts", None), P("lmk", None), P("pts", None, "lmk"), P(), P("pts"))
    out_specs = (P("pts", "lmk"), P("pts"))
    return jax.shard_map(body, mesh=mesh, in_specs=in_specs, out_specs=out_specs, check_vma=False)
```

```python
import math

import jax
import jax.numpy as jnp
from jax import lax
from jax.experimental import pallas as pl
from jax.experimental.pallas import tpu as pltpu
from jax.sharding import PartitionSpec as P

CLUSTERS = 4096
LANES = 128
DIRECT_GROUPS = 16
VMEM_LIMIT = 48 * 1024 * 1024
NT = (((1,), (1,)), ((), ()))


def unit_rows(values_in):
    widened = values_in.astype(jnp.float32)
    scale = lax.rsqrt(jnp.mean(widened * widened, axis=1, keepdims=True) + 1e-06)
    return (widened * scale).astype(jnp.bfloat16)


def place_kernel(groups, capacity, turn_ref, *refs):
    points_out, tags_out = refs[-2:]
    for core in range(2):
        points_ref, assignment_ref = refs[2 * core : 2 * core + 2]
        point_rows = points_ref.shape[0]
        ids = assignment_ref[...]
        owned = CLUSTERS // groups
        owners = lax.div(ids, owned)
        tags = ids - owners * owned + 1
        hits = lax.broadcasted_iota(jnp.int32, (groups, point_rows), 0) == owners
        earlier = lax.broadcasted_iota(
            jnp.int32, (point_rows, point_rows), 0
        ) < lax.broadcasted_iota(jnp.int32, (point_rows, point_rows), 1)
        before = jnp.dot(
            hits.astype(jnp.float32).astype(jnp.bfloat16),
            earlier.astype(jnp.float32).astype(jnp.bfloat16),
            preferred_element_type=jnp.float32,
        )
        rank = jnp.sum(jnp.where(hits, before, 0.0), axis=0, keepdims=True).astype(jnp.int32)
        slots = lax.bitwise_xor(owners, turn_ref[0]) * capacity + rank
        placed = (
            (lax.broadcasted_iota(jnp.int32, (groups * capacity, point_rows), 0) == slots)
            .astype(jnp.float32)
            .astype(jnp.bfloat16)
        )
        points_out[core] = jnp.dot(
            placed, unit_rows(points_ref[...]), preferred_element_type=jnp.float32
        ).astype(jnp.bfloat16)
        if core == 0:
            high = lax.div(tags, 256)
            which = lax.broadcasted_iota(jnp.int32, (tags_out.shape[1], point_rows), 0)
            coded = jnp.where(which == 0, high, jnp.where(which == 1, tags - high * 256, 0))
            tags_out[...] = lax.dot_general(
                placed,
                coded.astype(jnp.float32).astype(jnp.bfloat16),
                NT,
                preferred_element_type=jnp.float32,
            ).astype(jnp.bfloat16)


def marks_kernel(place_ref, after_ref, *refs):
    halves, marks_ref, keep_ref = refs[:-2], refs[-2], refs[-1]
    half = halves[0].shape[0]
    for away, block in enumerate(halves):
        first = pl.multiple_of(lax.bitwise_xor(place_ref[0], away) * half, 16)
        marks_ref[pl.ds(first, half), :] = unit_rows(block[...])
    keep_ref[...] = jnp.full(keep_ref.shape, place_ref[1], jnp.int32)


def pick_kernel(keep_ref, mine_ref, met_ref, *refs):
    refs[-1][...] = jnp.where(keep_ref[0] != 0, mine_ref[...], met_ref[...])


def rows_kernel(capacity, points_ref, tags_ref, marks_ref, *outs):
    marks = marks_ref.shape[0]
    no_tags = jnp.zeros(tags_ref.shape, jnp.bfloat16)
    for core, tags in enumerate((tags_ref[...], no_tags)):
        scores = lax.dot_general(
            points_ref[core], marks_ref[...], NT, preferred_element_type=jnp.float32
        )
        rows = jnp.exp(scores * (0.5 / math.sqrt(points_ref.shape[2]))).astype(jnp.bfloat16)
        if len(outs) == 1:
            outs[0][core, :, :marks] = rows
            outs[0][core, :, marks:] = tags
        for group, out in enumerate(outs if len(outs) > 1 else ()):
            here = slice(group * capacity, (group + 1) * capacity)
            there = slice(core * capacity, (core + 1) * capacity)
            out[there, :marks] = rows[here]
            out[there, marks:] = tags[here]


def sums_kernel(scale, swapped, mine_ref, other_ref, *refs):
    blocks, (totals_ref, counts_ref, rows_ref, panel_ref) = refs[:-4], refs[-4:]
    slots, lanes = rows_ref.shape[1:]
    owned, marks = totals_ref.shape[0], mine_ref.shape[0]
    for at, block in enumerate(blocks):
        side, first = at % 2, at // 2 * block.shape[0]
        if side and swapped:
            rows_ref[side, first : first + swapped, :] = block[swapped:, :]
            rows_ref[side, first + swapped : first + 2 * swapped, :] = block[:swapped, :]
        else:
            rows_ref[side, first : first + block.shape[0], :] = block[...]
    for side, half in enumerate((mine_ref, other_ref)):
        panel_ref[side, :marks, :] = half[...]
        panel_ref[side, marks:, :] = jnp.zeros((lanes - marks, half.shape[1]), jnp.bfloat16)
    features = (
        jnp.dot(rows_ref[0], panel_ref[0], preferred_element_type=jnp.float32)
        + jnp.dot(rows_ref[1], panel_ref[1], preferred_element_type=jnp.float32)
    ).astype(jnp.bfloat16)
    which = lax.broadcasted_iota(jnp.int32, (8, lanes - marks), 1)
    weights = jnp.where(which == 0, 256.0, jnp.where(which == 1, 1.0, 0.0)).astype(jnp.bfloat16)
    tags = lax.dot_general(weights, rows_ref[0, :, marks:], NT, preferred_element_type=jnp.float32)
    tags += lax.dot_general(weights, rows_ref[1, :, marks:], NT, preferred_element_type=jnp.float32)
    tags = tags[:1].astype(jnp.int32)
    member = (
        (lax.broadcasted_iota(jnp.int32, (owned, slots), 0) + 1 == tags)
        .astype(jnp.float32)
        .astype(jnp.bfloat16)
    )
    totals_ref[...] = jnp.dot(member, features, preferred_element_type=jnp.float32) * scale
    counts_ref[...] = lax.dot_general(
        jnp.ones((8, slots), jnp.bfloat16), member, NT, preferred_element_type=jnp.float32
    )[:1].astype(jnp.int32)


def call(kernel, shapes, *operands, place=None, scratch=()):
    held = pl.BlockSpec(memory_space=pltpu.VMEM)
    first = [] if place is None else [place]
    return pl.pallas_call(
        kernel,
        out_shape=shapes,
        in_specs=[pl.BlockSpec(memory_space=pltpu.SMEM)] * len(first) + [held] * len(operands),
        out_specs=(held,) * len(shapes) if isinstance(shapes, tuple) else held,
        scratch_shapes=scratch,
        compiler_params=pltpu.CompilerParams(vmem_limit_bytes=VMEM_LIMIT),
    )(*first, *operands)


def array(shape, dtype=jnp.bfloat16):
    return jax.ShapeDtypeStruct(shape, dtype)


def swap(block, axis, mask):
    return lax.ppermute(block, axis, [(i, i ^ mask) for i in range(lax.axis_size(axis))])


def spread(panel, parts, holder):
    me = lax.axis_index("pts")
    sides = panel.reshape(parts, 2, -1, panel.shape[1])
    mine, other = (
        lax.dynamic_index_in_dim(sides, side, 1, keepdims=False).reshape(-1, panel.shape[1])
        for side in (me % 2, 1 - me % 2)
    )
    return jnp.where(((holder ^ me) & 1) == 0, mine, swap(other, "pts", 1))


def exchange(rows, groups, capacity):
    slots, lanes = groups * capacity, rows.shape[-1]
    rows = rows.reshape(2, groups, capacity, lanes).swapaxes(0, 1)
    arrived = lax.all_to_all(
        rows.reshape(groups, 2 * capacity, lanes), "pts", split_axis=0, concat_axis=0, tiled=True
    ).reshape(groups // 2, 2, 2 * capacity, lanes)
    core = lax.axis_index("pts") % 2
    even = lax.dynamic_index_in_dim(arrived, core, 1, keepdims=False)
    odd = lax.dynamic_index_in_dim(arrived, 1 - core, 1, keepdims=False)
    odd = jnp.concatenate([odd[:, capacity:], odd[:, :capacity]], axis=1)
    return even.reshape(slots, lanes), odd.reshape(slots, lanes)


def body(points, landmarks, panels, panel_index, assignment):
    groups, parts = lax.axis_size("pts"), lax.axis_size("lmk")
    point_rows, width = points.shape
    capacity = 2 * point_rows // groups
    slots = groups * capacity
    owned = CLUSTERS // groups
    depth, columns = panels.shape[1:]
    half = landmarks.shape[0] // 2
    lanes = -(-(depth // 2 + 2) // LANES) * LANES
    me = lax.axis_index("pts")
    mine = lax.dynamic_slice_in_dim(landmarks, (me % 2) * half, half, 0)
    halves = [mine] + [swap(mine, "lmk", mask) for mask in range(1, parts)]
    differs = panel_index[0] ^ me
    panel = spread(panels[0], parts, panel_index[0])
    masks = [1 << bit for bit in range(1, groups.bit_length() - 1)]
    panel_met = swap(panel, "pts", masks[0])
    place = jnp.stack([lax.axis_index("lmk"), (differs & masks[0]) == 0]).astype(jnp.int32)
    assignment = assignment.reshape(1, point_rows)
    direct = groups <= DIRECT_GROUPS
    placed, tags = call(
        lambda *refs: place_kernel(groups, capacity, *refs),
        (array((2, slots, width)), array((slots, lanes - depth // 2))),
        points,
        assignment,
        swap(points, "pts", 1),
        swap(assignment, "pts", 1),
        place=(me if direct else 0 * me).astype(jnp.int32).reshape(1),
    )
    marks, keep = call(
        marks_kernel,
        (array((depth // 2, width)), array((1, columns), jnp.int32)),
        tags,
        *halves,
        place=place,
    )
    rows = call(
        lambda *refs: rows_kernel(capacity, *refs),
        (array((2 * capacity, lanes)),) * groups if direct else array((2, slots, lanes)),
        placed,
        tags,
        marks,
    )
    panel = jnp.where(keep != 0, panel, panel_met)
    if direct:
        rows = [rows[0]] + [swap(rows[mask], "pts", mask) for mask in range(1, groups)]
    else:
        rows = exchange(rows, groups, capacity)
    for mask in masks[1:]:
        met, keep = swap(panel, "pts", mask), (differs & mask) == 0
        if direct:
            keep = keep.astype(jnp.int32).reshape(1)
            panel = call(pick_kernel, array(panel.shape), panel, met, *rows[1:], place=keep)
        else:
            panel = jnp.where(keep, panel, met)
    totals, counts = call(
        lambda *refs: sums_kernel(
            CLUSTERS / (point_rows * groups), capacity if direct else 0, *refs
        ),
        (array((owned, columns), jnp.float32), array((1, owned), jnp.int32)),
        panel,
        swap(panel, "pts", 1),
        *rows,
        scratch=[
            pltpu.VMEM((2, slots, lanes), jnp.bfloat16),
            pltpu.VMEM((2, lanes, columns), jnp.bfloat16),
        ],
    )
    return (totals, counts.reshape(owned))


def solution(mesh):
    in_specs = (P("pts", None), P("lmk", None), P("pts", None, "lmk"), P(), P("pts"))
    out_specs = (P("pts", "lmk"), P("pts"))
    return jax.shard_map(body, mesh=mesh, in_specs=in_specs, out_specs=out_specs, check_vma=False)
```

```python
import math

import jax
import jax.numpy as jnp
from jax import lax
from jax.experimental import pallas as pl
from jax.experimental.pallas import tpu as pltpu
from jax.sharding import PartitionSpec as P

CLUSTERS = 4096
LANES = 128
VMEM_LIMIT = 48 * 1024 * 1024
NT = (((1,), (1,)), ((), ()))


def unit_rows(values_in):
    widened = values_in.astype(jnp.float32)
    scale = lax.rsqrt(jnp.mean(widened * widened, axis=1, keepdims=True) + 1e-06)
    return (widened * scale).astype(jnp.bfloat16)


def place_kernel(groups, capacity, *refs):
    points_out, tags_out = refs[-2:]
    for core in range(2):
        points_ref, assignment_ref = refs[2 * core : 2 * core + 2]
        point_rows = points_ref.shape[0]
        ids = assignment_ref[...]
        owned = CLUSTERS // groups
        owners = lax.div(ids, owned)
        tags = ids - owners * owned + 1
        hits = lax.broadcasted_iota(jnp.int32, (groups, point_rows), 0) == owners
        earlier = lax.broadcasted_iota(
            jnp.int32, (point_rows, point_rows), 0
        ) < lax.broadcasted_iota(jnp.int32, (point_rows, point_rows), 1)
        before = jnp.dot(
            hits.astype(jnp.float32).astype(jnp.bfloat16),
            earlier.astype(jnp.float32).astype(jnp.bfloat16),
            preferred_element_type=jnp.float32,
        )
        rank = jnp.sum(jnp.where(hits, before, 0.0), axis=0, keepdims=True).astype(jnp.int32)
        slots = owners * capacity + rank
        placed = (
            (lax.broadcasted_iota(jnp.int32, (groups * capacity, point_rows), 0) == slots)
            .astype(jnp.float32)
            .astype(jnp.bfloat16)
        )
        points_out[core] = jnp.dot(
            placed, unit_rows(points_ref[...]), preferred_element_type=jnp.float32
        ).astype(jnp.bfloat16)
        if core == 0:
            high = lax.div(tags, 256)
            which = lax.broadcasted_iota(jnp.int32, (tags_out.shape[1], point_rows), 0)
            coded = jnp.where(which == 0, high, jnp.where(which == 1, tags - high * 256, 0))
            tags_out[...] = lax.dot_general(
                placed,
                coded.astype(jnp.float32).astype(jnp.bfloat16),
                NT,
                preferred_element_type=jnp.float32,
            ).astype(jnp.bfloat16)


def marks_kernel(place_ref, after_ref, *refs):
    halves, marks_ref, keep_ref = refs[:-2], refs[-2], refs[-1]
    half = halves[0].shape[0]
    for away, block in enumerate(halves):
        first = pl.multiple_of(lax.bitwise_xor(place_ref[0], away) * half, 16)
        marks_ref[pl.ds(first, half), :] = unit_rows(block[...])
    keep_ref[...] = jnp.full(keep_ref.shape, place_ref[1], jnp.int32)


def pick_kernel(keep_ref, mine_ref, met_ref, *refs):
    refs[-1][...] = jnp.where(keep_ref[0] != 0, mine_ref[...], met_ref[...])


def pass_kernel(block_ref, after_ref, out_ref):
    out_ref[...] = block_ref[...]


def rows_kernel(groups, capacity, points_ref, tags_ref, marks_ref, out_ref):
    marks = marks_ref.shape[0]
    no_tags = jnp.zeros(tags_ref.shape, jnp.bfloat16)
    for core, tags in enumerate((tags_ref[...], no_tags)):
        scores = lax.dot_general(
            points_ref[core], marks_ref[...], NT, preferred_element_type=jnp.float32
        )
        rows = jnp.exp(scores * (0.5 / math.sqrt(points_ref.shape[2]))).astype(jnp.bfloat16)
        if len(out_ref.shape) == 4:
            for group in range(groups):
                here = slice(group * capacity, (group + 1) * capacity)
                out_ref[group, core, :, :marks] = rows[here]
                out_ref[group, core, :, marks:] = tags[here]
        else:
            out_ref[core, :, :marks] = rows
            out_ref[core, :, marks:] = tags


def sums_kernel(scale, even_ref, odd_ref, mine_ref, *refs):
    others, (totals_ref, counts_ref, panel_ref) = refs[:-3], refs[-3:]
    slots, lanes = even_ref.shape
    owned, marks = totals_ref.shape[0], mine_ref.shape[0]
    panel_ref[0, :marks, :] = mine_ref[...]
    first = 0
    for other in others:
        panel_ref[1, first : first + other.shape[0], :] = other[...]
        first += other.shape[0]
    panel_ref[:, marks:, :] = jnp.zeros((2, lanes - marks, mine_ref.shape[1]), jnp.bfloat16)
    features = (
        jnp.dot(even_ref[...], panel_ref[0], preferred_element_type=jnp.float32)
        + jnp.dot(odd_ref[...], panel_ref[1], preferred_element_type=jnp.float32)
    ).astype(jnp.bfloat16)
    which = lax.broadcasted_iota(jnp.int32, (8, lanes - marks), 1)
    weights = jnp.where(which == 0, 256.0, jnp.where(which == 1, 1.0, 0.0)).astype(jnp.bfloat16)
    tags = lax.dot_general(weights, even_ref[:, marks:], NT, preferred_element_type=jnp.float32)
    tags += lax.dot_general(weights, odd_ref[:, marks:], NT, preferred_element_type=jnp.float32)
    tags = tags[:1].astype(jnp.int32)
    member = (
        (lax.broadcasted_iota(jnp.int32, (owned, slots), 0) + 1 == tags)
        .astype(jnp.float32)
        .astype(jnp.bfloat16)
    )
    totals_ref[...] = jnp.dot(member, features, preferred_element_type=jnp.float32) * scale
    counts_ref[...] = lax.dot_general(
        jnp.ones((8, slots), jnp.bfloat16), member, NT, preferred_element_type=jnp.float32
    )[:1].astype(jnp.int32)


def call(kernel, shapes, *operands, place=None, scratch=()):
    held = pl.BlockSpec(memory_space=pltpu.VMEM)
    first = [] if place is None else [place]
    return pl.pallas_call(
        kernel,
        out_shape=shapes,
        in_specs=[pl.BlockSpec(memory_space=pltpu.SMEM)] * len(first) + [held] * len(operands),
        out_specs=(held,) * len(shapes) if isinstance(shapes, tuple) else held,
        scratch_shapes=scratch,
        compiler_params=pltpu.CompilerParams(vmem_limit_bytes=VMEM_LIMIT),
    )(*first, *operands)


def array(shape, dtype=jnp.bfloat16):
    return jax.ShapeDtypeStruct(shape, dtype)


def swap(block, axis, mask):
    return lax.ppermute(block, axis, [(i, i ^ mask) for i in range(lax.axis_size(axis))])


def pick(keep, mine, met, *after):
    keep = keep.astype(jnp.int32).reshape(1)
    return call(pick_kernel, array(mine.shape), mine, met, *after, place=keep)


def sides_of(panel, parts, core):
    sides = panel.reshape(parts, 2, -1, panel.shape[1])
    return (
        lax.dynamic_index_in_dim(sides, side, 1, keepdims=False).reshape(-1, panel.shape[1])
        for side in (core, 1 - core)
    )


def exchange(rows, groups, capacity):
    slots, lanes = groups * capacity, rows.shape[-1]
    if rows.ndim == 3:
        rows = rows.reshape(2, groups, capacity, lanes).swapaxes(0, 1)
    arrived = lax.all_to_all(
        rows.reshape(groups, 2 * capacity, lanes), "pts", split_axis=0, concat_axis=0, tiled=True
    ).reshape(groups // 2, 2, 2 * capacity, lanes)
    core = lax.axis_index("pts") % 2
    even = lax.dynamic_index_in_dim(arrived, core, 1, keepdims=False)
    odd = lax.dynamic_index_in_dim(arrived, 1 - core, 1, keepdims=False)
    odd = jnp.concatenate([odd[:, capacity:], odd[:, :capacity]], axis=1)
    return even.reshape(slots, lanes), odd.reshape(slots, lanes)


def body(points, landmarks, panels, panel_index, assignment):
    groups, parts = lax.axis_size("pts"), lax.axis_size("lmk")
    point_rows, width = points.shape
    capacity = 2 * point_rows // groups
    slots = groups * capacity
    owned = CLUSTERS // groups
    depth, columns = panels.shape[1:]
    half = landmarks.shape[0] // 2
    lanes = -(-(depth // 2 + 2) // LANES) * LANES
    me = lax.axis_index("pts")
    marks = lax.dynamic_slice_in_dim(landmarks, (me % 2) * half, half, 0)
    halves = [marks] + [swap(marks, "lmk", mask) for mask in range(1, parts)]
    assignment = assignment.reshape(1, point_rows)
    points_met, assignment_met = swap(points, "pts", 1), swap(assignment, "pts", 1)
    differs = panel_index[0] ^ me
    mine, other = sides_of(panels[0], parts, me % 2)
    panel = pick((differs & 1) == 0, mine, swap(other, "pts", 1), points_met, assignment_met)
    masks = [1 << bit for bit in range(1, groups.bit_length() - 1)]
    panel_met = swap(panel, "pts", masks[0])
    place = jnp.stack([lax.axis_index("lmk"), (differs & masks[0]) == 0]).astype(jnp.int32)
    placed, tags = call(
        lambda *refs: place_kernel(groups, capacity, *refs),
        (array((2, slots, width)), array((slots, lanes - depth // 2))),
        points,
        assignment,
        points_met,
        assignment_met,
    )
    marks, keep = call(
        marks_kernel,
        (array((depth // 2, width)), array((1, columns), jnp.int32)),
        tags,
        *halves,
        place=place,
    )
    rows = call(
        lambda *refs: rows_kernel(groups, capacity, *refs),
        array((groups, 2, capacity, lanes) if capacity % 16 == 0 else (2, slots, lanes)),
        placed,
        tags,
        marks,
    )
    panel = jnp.where(keep != 0, panel, panel_met)
    for mask in masks[1:]:
        panel = jnp.where((differs & mask) == 0, panel, swap(panel, "pts", mask))
    cut = panel.shape[0] // 2
    others = [swap(panel[:cut], "pts", 1)]
    others.append(swap(call(pass_kernel, array((cut, columns)), panel[cut:], others[0]), "pts", 1))
    even, odd = exchange(rows, groups, capacity)
    totals, counts = call(
        lambda *refs: sums_kernel(CLUSTERS / (point_rows * groups), *refs),
        (array((owned, columns), jnp.float32), array((1, owned), jnp.int32)),
        even,
        odd,
        panel,
        *others,
        scratch=[pltpu.VMEM((2, lanes, columns), jnp.bfloat16)],
    )
    return (totals, counts.reshape(owned))


def solution(mesh):
    in_specs = (P("pts", None), P("lmk", None), P("pts", None, "lmk"), P(), P("pts"))
    out_specs = (P("pts", "lmk"), P("pts"))
    return jax.shard_map(body, mesh=mesh, in_specs=in_specs, out_specs=out_specs, check_vma=False)
```

```python
import math

import jax
import jax.numpy as jnp
from jax import lax
from jax.experimental import pallas as pl
from jax.experimental.pallas import tpu as pltpu
from jax.sharding import PartitionSpec as P

CLUSTERS = 4096
LANES = 128
VMEM_LIMIT = 48 * 1024 * 1024
NT = (((1,), (1,)), ((), ()))


def unit_rows(values_in):
    widened = values_in.astype(jnp.float32)
    scale = lax.rsqrt(jnp.mean(widened * widened, axis=1, keepdims=True) + 1e-06)
    return (widened * scale).astype(jnp.bfloat16)


def place_kernel(groups, capacity, *refs):
    points_out, tags_out = refs[-2:]
    for core in range(2):
        points_ref, assignment_ref = refs[2 * core : 2 * core + 2]
        point_rows = points_ref.shape[0]
        ids = assignment_ref[...]
        owned = CLUSTERS // groups
        owners = lax.div(ids, owned)
        tags = ids - owners * owned + 1
        hits = lax.broadcasted_iota(jnp.int32, (groups, point_rows), 0) == owners
        earlier = lax.broadcasted_iota(
            jnp.int32, (point_rows, point_rows), 0
        ) < lax.broadcasted_iota(jnp.int32, (point_rows, point_rows), 1)
        before = jnp.dot(
            hits.astype(jnp.float32).astype(jnp.bfloat16),
            earlier.astype(jnp.float32).astype(jnp.bfloat16),
            preferred_element_type=jnp.float32,
        )
        rank = jnp.sum(jnp.where(hits, before, 0.0), axis=0, keepdims=True).astype(jnp.int32)
        slots = owners * capacity + rank
        placed = (
            (lax.broadcasted_iota(jnp.int32, (groups * capacity, point_rows), 0) == slots)
            .astype(jnp.float32)
            .astype(jnp.bfloat16)
        )
        points_out[core] = jnp.dot(
            placed, unit_rows(points_ref[...]), preferred_element_type=jnp.float32
        ).astype(jnp.bfloat16)
        if core == 0:
            high = lax.div(tags, 256)
            which = lax.broadcasted_iota(jnp.int32, (tags_out.shape[1], point_rows), 0)
            coded = jnp.where(which == 0, high, jnp.where(which == 1, tags - high * 256, 0))
            tags_out[...] = lax.dot_general(
                placed,
                coded.astype(jnp.float32).astype(jnp.bfloat16),
                NT,
                preferred_element_type=jnp.float32,
            ).astype(jnp.bfloat16)


def marks_kernel(place_ref, after_ref, *refs):
    halves, marks_ref, keep_ref = refs[:-2], refs[-2], refs[-1]
    half = halves[0].shape[0]
    for away, block in enumerate(halves):
        first = pl.multiple_of(lax.bitwise_xor(place_ref[0], away) * half, 16)
        marks_ref[pl.ds(first, half), :] = unit_rows(block[...])
    keep_ref[...] = jnp.full(keep_ref.shape, place_ref[1], jnp.int32)


def pick_kernel(keep_ref, mine_ref, met_ref, *refs):
    refs[-1][...] = jnp.where(keep_ref[0] != 0, mine_ref[...], met_ref[...])


def pass_kernel(block_ref, after_ref, out_ref):
    out_ref[...] = block_ref[...]


def rows_kernel(groups, capacity, points_ref, tags_ref, marks_ref, out_ref):
    marks = marks_ref.shape[0]
    no_tags = jnp.zeros(tags_ref.shape, jnp.bfloat16)
    for core, tags in enumerate((tags_ref[...], no_tags)):
        scores = lax.dot_general(
            points_ref[core], marks_ref[...], NT, preferred_element_type=jnp.float32
        )
        rows = jnp.exp(scores * (0.5 / math.sqrt(points_ref.shape[2]))).astype(jnp.bfloat16)
        if len(out_ref.shape) == 4:
            for group in range(groups):
                here = slice(group * capacity, (group + 1) * capacity)
                out_ref[group, core, :, :marks] = rows[here]
                out_ref[group, core, :, marks:] = tags[here]
        else:
            out_ref[core, :, :marks] = rows
            out_ref[core, :, marks:] = tags


def sums_kernel(scale, even_ref, odd_ref, mine_ref, *refs):
    others, (totals_ref, counts_ref, panel_ref, sums_ref, sems) = refs[:-5], refs[-5:]
    slots, lanes = even_ref.shape
    owned, marks = totals_ref.shape[0], mine_ref.shape[0]
    panel_ref[0, :marks, :] = mine_ref[...]
    first = 0
    for other in others:
        panel_ref[1, first : first + other.shape[0], :] = other[...]
        first += other.shape[0]
    panel_ref[:, marks:, :] = jnp.zeros((2, lanes - marks, mine_ref.shape[1]), jnp.bfloat16)
    features = (
        jnp.dot(even_ref[...], panel_ref[0], preferred_element_type=jnp.float32)
        + jnp.dot(odd_ref[...], panel_ref[1], preferred_element_type=jnp.float32)
    ).astype(jnp.bfloat16)
    which = lax.broadcasted_iota(jnp.int32, (8, lanes - marks), 1)
    weights = jnp.where(which == 0, 256.0, jnp.where(which == 1, 1.0, 0.0)).astype(jnp.bfloat16)
    tags = lax.dot_general(weights, even_ref[:, marks:], NT, preferred_element_type=jnp.float32)
    tags += lax.dot_general(weights, odd_ref[:, marks:], NT, preferred_element_type=jnp.float32)
    tags = tags[:1].astype(jnp.int32)
    member = (
        (lax.broadcasted_iota(jnp.int32, (owned, slots), 0) + 1 == tags)
        .astype(jnp.float32)
        .astype(jnp.bfloat16)
    )
    chunks = sums_ref.shape[0]
    size = owned // chunks
    copies = []
    for at in range(chunks):
        here = slice(at * size, (at + 1) * size)
        sums_ref[at] = jnp.dot(member[here], features, preferred_element_type=jnp.float32) * scale
        copies.append(pltpu.make_async_copy(sums_ref.at[at], totals_ref.at[here, :], sems.at[at]))
        copies[-1].start()
    counts_ref[...] = lax.dot_general(
        jnp.ones((8, slots), jnp.bfloat16), member, NT, preferred_element_type=jnp.float32
    )[:1].astype(jnp.int32)
    for copy in copies:
        copy.wait()


def call(kernel, shapes, *operands, place=None, scratch=(), sent=()):
    held, loose = pl.BlockSpec(memory_space=pltpu.VMEM), pl.BlockSpec(memory_space=pl.ANY)
    first = [] if place is None else [place]
    return pl.pallas_call(
        kernel,
        out_shape=shapes,
        in_specs=[pl.BlockSpec(memory_space=pltpu.SMEM)] * len(first) + [held] * len(operands),
        out_specs=tuple(loose if at in sent else held for at in range(len(shapes)))
        if isinstance(shapes, tuple)
        else held,
        scratch_shapes=scratch,
        compiler_params=pltpu.CompilerParams(vmem_limit_bytes=VMEM_LIMIT),
    )(*first, *operands)


def array(shape, dtype=jnp.bfloat16):
    return jax.ShapeDtypeStruct(shape, dtype)


def swap(block, axis, mask):
    return lax.ppermute(block, axis, [(i, i ^ mask) for i in range(lax.axis_size(axis))])


def pick(keep, mine, met, *after):
    keep = keep.astype(jnp.int32).reshape(1)
    return call(pick_kernel, array(mine.shape), mine, met, *after, place=keep)


def sides_of(panel, parts, core):
    sides = panel.reshape(parts, 2, -1, panel.shape[1])
    return (
        lax.dynamic_index_in_dim(sides, side, 1, keepdims=False).reshape(-1, panel.shape[1])
        for side in (core, 1 - core)
    )


def exchange(rows, groups, capacity):
    slots, lanes = groups * capacity, rows.shape[-1]
    if rows.ndim == 3:
        rows = rows.reshape(2, groups, capacity, lanes).swapaxes(0, 1)
    arrived = lax.all_to_all(
        rows.reshape(groups, 2 * capacity, lanes), "pts", split_axis=0, concat_axis=0, tiled=True
    ).reshape(groups // 2, 2, 2 * capacity, lanes)
    core = lax.axis_index("pts") % 2
    even = lax.dynamic_index_in_dim(arrived, core, 1, keepdims=False)
    odd = lax.dynamic_index_in_dim(arrived, 1 - core, 1, keepdims=False)
    odd = jnp.concatenate([odd[:, capacity:], odd[:, :capacity]], axis=1)
    return even.reshape(slots, lanes), odd.reshape(slots, lanes)


def body(points, landmarks, panels, panel_index, assignment):
    groups, parts = lax.axis_size("pts"), lax.axis_size("lmk")
    point_rows, width = points.shape
    capacity = 2 * point_rows // groups
    slots = groups * capacity
    owned = CLUSTERS // groups
    depth, columns = panels.shape[1:]
    half = landmarks.shape[0] // 2
    lanes = -(-(depth // 2 + 2) // LANES) * LANES
    me = lax.axis_index("pts")
    marks = lax.dynamic_slice_in_dim(landmarks, (me % 2) * half, half, 0)
    halves = [marks] + [swap(marks, "lmk", mask) for mask in range(1, parts)]
    assignment = assignment.reshape(1, point_rows)
    points_met, assignment_met = swap(points, "pts", 1), swap(assignment, "pts", 1)
    differs = panel_index[0] ^ me
    mine, other = sides_of(panels[0], parts, me % 2)
    panel = pick((differs & 1) == 0, mine, swap(other, "pts", 1), points_met, assignment_met)
    masks = [1 << bit for bit in range(1, groups.bit_length() - 1)]
    panel_met = swap(panel, "pts", masks[0])
    place = jnp.stack([lax.axis_index("lmk"), (differs & masks[0]) == 0]).astype(jnp.int32)
    placed, tags = call(
        lambda *refs: place_kernel(groups, capacity, *refs),
        (array((2, slots, width)), array((slots, lanes - depth // 2))),
        points,
        assignment,
        points_met,
        assignment_met,
    )
    marks, keep = call(
        marks_kernel,
        (array((depth // 2, width)), array((1, columns), jnp.int32)),
        tags,
        *halves,
        place=place,
    )
    rows = call(
        lambda *refs: rows_kernel(groups, capacity, *refs),
        array((groups, 2, capacity, lanes) if capacity % 16 == 0 else (2, slots, lanes)),
        placed,
        tags,
        marks,
    )
    panel = jnp.where(keep != 0, panel, panel_met)
    for mask in masks[1:]:
        panel = jnp.where((differs & mask) == 0, panel, swap(panel, "pts", mask))
    cut = min(16, panel.shape[0] // 2)
    others = [swap(panel[:cut], "pts", 1)]
    others.append(swap(call(pass_kernel, array((panel.shape[0] - cut, columns)), panel[cut:], others[0]), "pts", 1))
    even, odd = exchange(rows, groups, capacity)
    chunks = max(1, owned // LANES)
    totals, counts = call(
        lambda *refs: sums_kernel(CLUSTERS / (point_rows * groups), *refs),
        (array((owned, columns), jnp.float32), array((1, owned), jnp.int32)),
        even,
        odd,
        panel,
        *others,
        scratch=[
            pltpu.VMEM((2, lanes, columns), jnp.bfloat16),
            pltpu.VMEM((chunks, owned // chunks, columns), jnp.float32),
            pltpu.SemaphoreType.DMA((chunks,)),
        ],
        sent=(0,),
    )
    return (totals, counts.reshape(owned))


def solution(mesh):
    in_specs = (P("pts", None), P("lmk", None), P("pts", None, "lmk"), P(), P("pts"))
    out_specs = (P("pts", "lmk"), P("pts"))
    return jax.shard_map(body, mesh=mesh, in_specs=in_specs, out_specs=out_specs, check_vma=False)
```

```python
import math

import jax
import jax.numpy as jnp
from jax import lax
from jax.experimental import pallas as pl
from jax.experimental.pallas import tpu as pltpu
from jax.sharding import PartitionSpec as P

CLUSTERS = 4096
LANES = 128
VMEM_LIMIT = 48 * 1024 * 1024
NT = (((1,), (1,)), ((), ()))


def unit_rows(values_in):
    widened = values_in.astype(jnp.float32)
    scale = lax.rsqrt(jnp.mean(widened * widened, axis=1, keepdims=True) + 1e-06)
    return (widened * scale).astype(jnp.bfloat16)


def place_kernel(groups, capacity, *refs):
    points_out, tags_out = refs[-2:]
    for core in range(2):
        points_ref, assignment_ref = refs[2 * core : 2 * core + 2]
        point_rows = points_ref.shape[0]
        ids = assignment_ref[...]
        owned = CLUSTERS // groups
        owners = lax.div(ids, owned)
        tags = ids - owners * owned + 1
        hits = lax.broadcasted_iota(jnp.int32, (groups, point_rows), 0) == owners
        earlier = lax.broadcasted_iota(
            jnp.int32, (point_rows, point_rows), 0
        ) < lax.broadcasted_iota(jnp.int32, (point_rows, point_rows), 1)
        before = jnp.dot(
            hits.astype(jnp.float32).astype(jnp.bfloat16),
            earlier.astype(jnp.float32).astype(jnp.bfloat16),
            preferred_element_type=jnp.float32,
        )
        rank = jnp.sum(jnp.where(hits, before, 0.0), axis=0, keepdims=True).astype(jnp.int32)
        slots = owners * capacity + rank
        placed = (
            (lax.broadcasted_iota(jnp.int32, (groups * capacity, point_rows), 0) == slots)
            .astype(jnp.float32)
            .astype(jnp.bfloat16)
        )
        points_out[core] = jnp.dot(
            placed, unit_rows(points_ref[...]), preferred_element_type=jnp.float32
        ).astype(jnp.bfloat16)
        if core == 0:
            high = lax.div(tags, 256)
            which = lax.broadcasted_iota(jnp.int32, (tags_out.shape[1], point_rows), 0)
            coded = jnp.where(which == 0, high, jnp.where(which == 1, tags - high * 256, 0))
            tags_out[...] = lax.dot_general(
                placed,
                coded.astype(jnp.float32).astype(jnp.bfloat16),
                NT,
                preferred_element_type=jnp.float32,
            ).astype(jnp.bfloat16)


def marks_kernel(place_ref, after_ref, *refs):
    halves, marks_ref, keep_ref = refs[:-2], refs[-2], refs[-1]
    half = halves[0].shape[0]
    for away, block in enumerate(halves):
        first = pl.multiple_of(lax.bitwise_xor(place_ref[0], away) * half, 16)
        marks_ref[pl.ds(first, half), :] = unit_rows(block[...])
    keep_ref[...] = jnp.full(keep_ref.shape, place_ref[1], jnp.int32)


def pick_kernel(place_ref, mine_ref, met_ref, *refs):
    out_ref, half = refs[-1], mine_ref.shape[2]
    for part in range(mine_ref.shape[0]):
        out_ref[part * half : (part + 1) * half, :] = jnp.where(
            place_ref[0] != 0, mine_ref[part, place_ref[1]], met_ref[part, place_ref[1]]
        )


def pass_kernel(block_ref, after_ref, out_ref):
    out_ref[...] = block_ref[...]


def rows_kernel(groups, capacity, points_ref, tags_ref, marks_ref, out_ref):
    marks = marks_ref.shape[0]
    no_tags = jnp.zeros(tags_ref.shape, jnp.bfloat16)
    for core, tags in enumerate((tags_ref[...], no_tags)):
        scores = lax.dot_general(
            points_ref[core], marks_ref[...], NT, preferred_element_type=jnp.float32
        )
        rows = jnp.exp(scores * (0.5 / math.sqrt(points_ref.shape[2]))).astype(jnp.bfloat16)
        if len(out_ref.shape) == 4:
            for group in range(groups):
                here = slice(group * capacity, (group + 1) * capacity)
                out_ref[group, core, :, :marks] = rows[here]
                out_ref[group, core, :, marks:] = tags[here]
        else:
            out_ref[core, :, :marks] = rows
            out_ref[core, :, marks:] = tags


def sums_kernel(scale, even_ref, odd_ref, mine_ref, *refs):
    others, (totals_ref, counts_ref, panel_ref) = refs[:-3], refs[-3:]
    slots, lanes = even_ref.shape
    owned, marks = totals_ref.shape[0], mine_ref.shape[0]
    panel_ref[0, :marks, :] = mine_ref[...]
    first = 0
    for other in others:
        panel_ref[1, first : first + other.shape[0], :] = other[...]
        first += other.shape[0]
    panel_ref[:, marks:, :] = jnp.zeros((2, lanes - marks, mine_ref.shape[1]), jnp.bfloat16)
    features = (
        jnp.dot(even_ref[...], panel_ref[0], preferred_element_type=jnp.float32)
        + jnp.dot(odd_ref[...], panel_ref[1], preferred_element_type=jnp.float32)
    ).astype(jnp.bfloat16)
    which = lax.broadcasted_iota(jnp.int32, (8, lanes - marks), 1)
    weights = jnp.where(which == 0, 256.0, jnp.where(which == 1, 1.0, 0.0)).astype(jnp.bfloat16)
    tags = lax.dot_general(weights, even_ref[:, marks:], NT, preferred_element_type=jnp.float32)
    tags += lax.dot_general(weights, odd_ref[:, marks:], NT, preferred_element_type=jnp.float32)
    tags = tags[:1].astype(jnp.int32)
    member = (
        (lax.broadcasted_iota(jnp.int32, (owned, slots), 0) + 1 == tags)
        .astype(jnp.float32)
        .astype(jnp.bfloat16)
    )
    totals_ref[...] = jnp.dot(member, features, preferred_element_type=jnp.float32) * scale
    counts_ref[...] = lax.dot_general(
        jnp.ones((8, slots), jnp.bfloat16), member, NT, preferred_element_type=jnp.float32
    )[:1].astype(jnp.int32)


def call(kernel, shapes, *operands, place=None, scratch=()):
    held = pl.BlockSpec(memory_space=pltpu.VMEM)
    first = [] if place is None else [place]
    return pl.pallas_call(
        kernel,
        out_shape=shapes,
        in_specs=[pl.BlockSpec(memory_space=pltpu.SMEM)] * len(first) + [held] * len(operands),
        out_specs=(held,) * len(shapes) if isinstance(shapes, tuple) else held,
        scratch_shapes=scratch,
        compiler_params=pltpu.CompilerParams(vmem_limit_bytes=VMEM_LIMIT),
    )(*first, *operands)


def array(shape, dtype=jnp.bfloat16):
    return jax.ShapeDtypeStruct(shape, dtype)


def swap(block, axis, mask):
    return lax.ppermute(block, axis, [(i, i ^ mask) for i in range(lax.axis_size(axis))])


def exchange(rows, groups, capacity):
    slots, lanes = groups * capacity, rows.shape[-1]
    if rows.ndim == 3:
        rows = rows.reshape(2, groups, capacity, lanes).swapaxes(0, 1)
    arrived = lax.all_to_all(
        rows.reshape(groups, 2 * capacity, lanes), "pts", split_axis=0, concat_axis=0, tiled=True
    ).reshape(groups // 2, 2, 2 * capacity, lanes)
    core = lax.axis_index("pts") % 2
    even = lax.dynamic_index_in_dim(arrived, core, 1, keepdims=False)
    odd = lax.dynamic_index_in_dim(arrived, 1 - core, 1, keepdims=False)
    odd = jnp.concatenate([odd[:, capacity:], odd[:, :capacity]], axis=1)
    return even.reshape(slots, lanes), odd.reshape(slots, lanes)


def body(points, landmarks, panels, panel_index, assignment):
    groups, parts = lax.axis_size("pts"), lax.axis_size("lmk")
    point_rows, width = points.shape
    capacity = 2 * point_rows // groups
    slots = groups * capacity
    owned = CLUSTERS // groups
    depth, columns = panels.shape[1:]
    half = landmarks.shape[0] // 2
    lanes = -(-(depth // 2 + 2) // LANES) * LANES
    me = lax.axis_index("pts")
    marks = lax.dynamic_slice_in_dim(landmarks, (me % 2) * half, half, 0)
    halves = [marks] + [swap(marks, "lmk", mask) for mask in range(1, parts)]
    assignment = assignment.reshape(1, point_rows)
    points_met, assignment_met = swap(points, "pts", 1), swap(assignment, "pts", 1)
    differs = panel_index[0] ^ me
    panel_met = swap(panels[0], "pts", 1)
    panel = call(
        pick_kernel,
        array((depth // 2, columns)),
        panels.reshape(parts, 2, half, columns),
        panel_met.reshape(parts, 2, half, columns),
        points_met,
        assignment_met,
        place=jnp.stack([(differs & 1) == 0, me % 2]).astype(jnp.int32),
    )
    masks = [1 << bit for bit in range(1, groups.bit_length() - 1)]
    panel_met = swap(panel, "pts", masks[0])
    place = jnp.stack([lax.axis_index("lmk"), (differs & masks[0]) == 0]).astype(jnp.int32)
    placed, tags = call(
        lambda *refs: place_kernel(groups, capacity, *refs),
        (array((2, slots, width)), array((slots, lanes - depth // 2))),
        points,
        assignment,
        points_met,
        assignment_met,
    )
    marks, keep = call(
        marks_kernel,
        (array((depth // 2, width)), array((1, columns), jnp.int32)),
        tags,
        *halves,
        place=place,
    )
    rows = call(
        lambda *refs: rows_kernel(groups, capacity, *refs),
        array((groups, 2, capacity, lanes) if capacity % 16 == 0 else (2, slots, lanes)),
        placed,
        tags,
        marks,
    )
    panel = jnp.where(keep != 0, panel, panel_met)
    for mask in masks[1:]:
        panel = jnp.where((differs & mask) == 0, panel, swap(panel, "pts", mask))
    cut = panel.shape[0] // 2
    others = [swap(panel[:cut], "pts", 1)]
    others.append(swap(call(pass_kernel, array((cut, columns)), panel[cut:], others[0]), "pts", 1))
    even, odd = exchange(rows, groups, capacity)
    totals, counts = call(
        lambda *refs: sums_kernel(CLUSTERS / (point_rows * groups), *refs),
        (array((owned, columns), jnp.float32), array((1, owned), jnp.int32)),
        even,
        odd,
        panel,
        *others,
        scratch=[pltpu.VMEM((2, lanes, columns), jnp.bfloat16)],
    )
    return (totals, counts.reshape(owned))


def solution(mesh):
    in_specs = (P("pts", None), P("lmk", None), P("pts", None, "lmk"), P(), P("pts"))
    out_specs = (P("pts", "lmk"), P("pts"))
    return jax.shard_map(body, mesh=mesh, in_specs=in_specs, out_specs=out_specs, check_vma=False)
```

```python
import math

import jax
import jax.numpy as jnp
from jax import lax
from jax.experimental import pallas as pl
from jax.experimental.pallas import tpu as pltpu
from jax.sharding import PartitionSpec as P

CLUSTERS = 4096
LANES = 128
VMEM_LIMIT = 48 * 1024 * 1024
NT = (((1,), (1,)), ((), ()))


def unit_rows(values_in):
    widened = values_in.astype(jnp.float32)
    scale = lax.rsqrt(jnp.mean(widened * widened, axis=1, keepdims=True) + 1e-06)
    return (widened * scale).astype(jnp.bfloat16)


def place_kernel(groups, capacity, *refs):
    points_out, tags_out = refs[-2:]
    for core in range(2):
        points_ref, assignment_ref = refs[2 * core : 2 * core + 2]
        point_rows = points_ref.shape[0]
        ids = assignment_ref[...]
        owned = CLUSTERS // groups
        owners = lax.div(ids, owned)
        tags = ids - owners * owned + 1
        hits = lax.broadcasted_iota(jnp.int32, (groups, point_rows), 0) == owners
        earlier = lax.broadcasted_iota(
            jnp.int32, (point_rows, point_rows), 0
        ) < lax.broadcasted_iota(jnp.int32, (point_rows, point_rows), 1)
        before = jnp.dot(
            hits.astype(jnp.float32).astype(jnp.bfloat16),
            earlier.astype(jnp.float32).astype(jnp.bfloat16),
            preferred_element_type=jnp.float32,
        )
        rank = jnp.sum(jnp.where(hits, before, 0.0), axis=0, keepdims=True).astype(jnp.int32)
        slots = owners * capacity + rank
        placed = (
            (lax.broadcasted_iota(jnp.int32, (groups * capacity, point_rows), 0) == slots)
            .astype(jnp.float32)
            .astype(jnp.bfloat16)
        )
        points_out[core] = jnp.dot(
            placed, unit_rows(points_ref[...]), preferred_element_type=jnp.float32
        ).astype(jnp.bfloat16)
        if core == 0:
            high = lax.div(tags, 256)
            which = lax.broadcasted_iota(jnp.int32, (tags_out.shape[1], point_rows), 0)
            coded = jnp.where(which == 0, high, jnp.where(which == 1, tags - high * 256, 0))
            tags_out[...] = lax.dot_general(
                placed,
                coded.astype(jnp.float32).astype(jnp.bfloat16),
                NT,
                preferred_element_type=jnp.float32,
            ).astype(jnp.bfloat16)


def marks_kernel(place_ref, after_ref, *refs):
    halves, marks_ref, keep_ref = refs[:-2], refs[-2], refs[-1]
    half = halves[0].shape[0]
    for away, block in enumerate(halves):
        first = pl.multiple_of(lax.bitwise_xor(place_ref[0], away) * half, 16)
        marks_ref[pl.ds(first, half), :] = unit_rows(block[...])
    keep_ref[...] = jnp.full(keep_ref.shape, place_ref[1], jnp.int32)


def pick_kernel(keep_ref, mine_ref, met_ref, *refs):
    refs[-1][...] = jnp.where(keep_ref[0] != 0, mine_ref[...], met_ref[...])


def pass_kernel(block_ref, after_ref, out_ref):
    out_ref[...] = block_ref[...]


def rows_kernel(groups, capacity, points_ref, tags_ref, marks_ref, out_ref):
    marks = marks_ref.shape[0]
    no_tags = jnp.zeros(tags_ref.shape, jnp.bfloat16)
    for core, tags in enumerate((tags_ref[...], no_tags)):
        scores = lax.dot_general(
            points_ref[core], marks_ref[...], NT, preferred_element_type=jnp.float32
        )
        rows = jnp.exp(scores * (0.5 / math.sqrt(points_ref.shape[2]))).astype(jnp.bfloat16)
        if len(out_ref.shape) == 4:
            for group in range(groups):
                here = slice(group * capacity, (group + 1) * capacity)
                out_ref[group, core, :, :marks] = rows[here]
                out_ref[group, core, :, marks:] = tags[here]
        else:
            out_ref[core, :, :marks] = rows
            out_ref[core, :, marks:] = tags


def sums_kernel(scale, core_ref, arrived_ref, mine_ref, *refs):
    others, (totals_ref, counts_ref, panel_ref, rows_ref) = refs[:-4], refs[-4:]
    slots, lanes = rows_ref.shape[1:]
    owned, marks = totals_ref.shape[0], mine_ref.shape[0]
    if len(arrived_ref.shape) == 3:
        rows_ref[...] = arrived_ref[...]
    else:
        part = arrived_ref.shape[2] // 2
        for chip in range(arrived_ref.shape[0]):
            first, middle, last = 2 * chip * part, (2 * chip + 1) * part, (2 * chip + 2) * part
            rows_ref[0, first:last, :] = arrived_ref[chip, core_ref[0]]
            rows_ref[1, first:middle, :] = arrived_ref[chip, 1 - core_ref[0], part:, :]
            rows_ref[1, middle:last, :] = arrived_ref[chip, 1 - core_ref[0], :part, :]
    panel_ref[0, :marks, :] = mine_ref[...]
    first = 0
    for other in others:
        panel_ref[1, first : first + other.shape[0], :] = other[...]
        first += other.shape[0]
    panel_ref[:, marks:, :] = jnp.zeros((2, lanes - marks, mine_ref.shape[1]), jnp.bfloat16)
    features = (
        jnp.dot(rows_ref[0], panel_ref[0], preferred_element_type=jnp.float32)
        + jnp.dot(rows_ref[1], panel_ref[1], preferred_element_type=jnp.float32)
    ).astype(jnp.bfloat16)
    which = lax.broadcasted_iota(jnp.int32, (8, lanes - marks), 1)
    weights = jnp.where(which == 0, 256.0, jnp.where(which == 1, 1.0, 0.0)).astype(jnp.bfloat16)
    tags = lax.dot_general(weights, rows_ref[0, :, marks:], NT, preferred_element_type=jnp.float32)
    tags += lax.dot_general(weights, rows_ref[1, :, marks:], NT, preferred_element_type=jnp.float32)
    tags = tags[:1].astype(jnp.int32)
    member = (
        (lax.broadcasted_iota(jnp.int32, (owned, slots), 0) + 1 == tags)
        .astype(jnp.float32)
        .astype(jnp.bfloat16)
    )
    totals_ref[...] = jnp.dot(member, features, preferred_element_type=jnp.float32) * scale
    counts_ref[...] = lax.dot_general(
        jnp.ones((8, slots), jnp.bfloat16), member, NT, preferred_element_type=jnp.float32
    )[:1].astype(jnp.int32)


def call(kernel, shapes, *operands, place=None, scratch=()):
    held = pl.BlockSpec(memory_space=pltpu.VMEM)
    first = [] if place is None else [place]
    return pl.pallas_call(
        kernel,
        out_shape=shapes,
        in_specs=[pl.BlockSpec(memory_space=pltpu.SMEM)] * len(first) + [held] * len(operands),
        out_specs=(held,) * len(shapes) if isinstance(shapes, tuple) else held,
        scratch_shapes=scratch,
        compiler_params=pltpu.CompilerParams(vmem_limit_bytes=VMEM_LIMIT),
    )(*first, *operands)


def array(shape, dtype=jnp.bfloat16):
    return jax.ShapeDtypeStruct(shape, dtype)


def swap(block, axis, mask):
    return lax.ppermute(block, axis, [(i, i ^ mask) for i in range(lax.axis_size(axis))])


def pick(keep, mine, met, *after):
    keep = keep.astype(jnp.int32).reshape(1)
    return call(pick_kernel, array(mine.shape), mine, met, *after, place=keep)


def sides_of(panel, parts, core):
    sides = panel.reshape(parts, 2, -1, panel.shape[1])
    return (
        lax.dynamic_index_in_dim(sides, side, 1, keepdims=False).reshape(-1, panel.shape[1])
        for side in (core, 1 - core)
    )


def exchange(rows, groups, capacity, core):
    slots, lanes = groups * capacity, rows.shape[-1]
    whole_tiles = rows.ndim == 4
    if not whole_tiles:
        rows = rows.reshape(2, groups, capacity, lanes).swapaxes(0, 1)
    arrived = lax.all_to_all(
        rows.reshape(groups, 2 * capacity, lanes), "pts", split_axis=0, concat_axis=0, tiled=True
    ).reshape(groups // 2, 2, 2 * capacity, lanes)
    if whole_tiles:
        return arrived
    even = lax.dynamic_index_in_dim(arrived, core, 1, keepdims=False)
    odd = lax.dynamic_index_in_dim(arrived, 1 - core, 1, keepdims=False)
    odd = jnp.concatenate([odd[:, capacity:], odd[:, :capacity]], axis=1)
    return jnp.stack([even.reshape(slots, lanes), odd.reshape(slots, lanes)])


def body(points, landmarks, panels, panel_index, assignment):
    groups, parts = lax.axis_size("pts"), lax.axis_size("lmk")
    point_rows, width = points.shape
    capacity = 2 * point_rows // groups
    slots = groups * capacity
    owned = CLUSTERS // groups
    depth, columns = panels.shape[1:]
    half = landmarks.shape[0] // 2
    lanes = -(-(depth // 2 + 2) // LANES) * LANES
    me = lax.axis_index("pts")
    marks = lax.dynamic_slice_in_dim(landmarks, (me % 2) * half, half, 0)
    halves = [marks] + [swap(marks, "lmk", mask) for mask in range(1, parts)]
    assignment = assignment.reshape(1, point_rows)
    points_met, assignment_met = swap(points, "pts", 1), swap(assignment, "pts", 1)
    differs = panel_index[0] ^ me
    mine, other = sides_of(panels[0], parts, me % 2)
    panel = pick((differs & 1) == 0, mine, swap(other, "pts", 1), points_met, assignment_met)
    masks = [1 << bit for bit in range(1, groups.bit_length() - 1)]
    panel_met = swap(panel, "pts", masks[0])
    place = jnp.stack([lax.axis_index("lmk"), (differs & masks[0]) == 0]).astype(jnp.int32)
    placed, tags = call(
        lambda *refs: place_kernel(groups, capacity, *refs),
        (array((2, slots, width)), array((slots, lanes - depth // 2))),
        points,
        assignment,
        points_met,
        assignment_met,
    )
    marks, keep = call(
        marks_kernel,
        (array((depth // 2, width)), array((1, columns), jnp.int32)),
        tags,
        *halves,
        place=place,
    )
    rows = call(
        lambda *refs: rows_kernel(groups, capacity, *refs),
        array((groups, 2, capacity, lanes) if capacity % 16 == 0 else (2, slots, lanes)),
        placed,
        tags,
        marks,
    )
    panel = jnp.where(keep != 0, panel, panel_met)
    for mask in masks[1:]:
        panel = jnp.where((differs & mask) == 0, panel, swap(panel, "pts", mask))
    cut = panel.shape[0] // 2
    others = [swap(panel[:cut], "pts", 1)]
    others.append(swap(call(pass_kernel, array((cut, columns)), panel[cut:], others[0]), "pts", 1))
    arrived = exchange(rows, groups, capacity, me % 2)
    totals, counts = call(
        lambda *refs: sums_kernel(CLUSTERS / (point_rows * groups), *refs),
        (array((owned, columns), jnp.float32), array((1, owned), jnp.int32)),
        arrived,
        panel,
        *others,
        place=(me % 2).astype(jnp.int32).reshape(1),
        scratch=[
            pltpu.VMEM((2, lanes, columns), jnp.bfloat16),
            pltpu.VMEM((2, slots, lanes), jnp.bfloat16),
        ],
    )
    return (totals, counts.reshape(owned))


def solution(mesh):
    in_specs = (P("pts", None), P("lmk", None), P("pts", None, "lmk"), P(), P("pts"))
    out_specs = (P("pts", "lmk"), P("pts"))
    return jax.shard_map(body, mesh=mesh, in_specs=in_specs, out_specs=out_specs, check_vma=False)
```

```python
import math

import jax
import jax.numpy as jnp
from jax import lax
from jax.experimental import pallas as pl
from jax.experimental.pallas import tpu as pltpu
from jax.sharding import PartitionSpec as P

CLUSTERS = 4096
LANES = 128
VMEM_LIMIT = 48 * 1024 * 1024
NT = (((1,), (1,)), ((), ()))


def unit_rows(values_in):
    widened = values_in.astype(jnp.float32)
    scale = lax.rsqrt(jnp.mean(widened * widened, axis=1, keepdims=True) + 1e-06)
    return (widened * scale).astype(jnp.bfloat16)


def place_kernel(groups, capacity, *refs):
    points_out, tags_out = refs[-2:]
    for core in range(2):
        points_ref, assignment_ref = refs[2 * core : 2 * core + 2]
        point_rows = points_ref.shape[0]
        ids = assignment_ref[...]
        owned = CLUSTERS // groups
        owners = lax.div(ids, owned)
        tags = ids - owners * owned + 1
        hits = lax.broadcasted_iota(jnp.int32, (groups, point_rows), 0) == owners
        earlier = lax.broadcasted_iota(
            jnp.int32, (point_rows, point_rows), 0
        ) < lax.broadcasted_iota(jnp.int32, (point_rows, point_rows), 1)
        before = jnp.dot(
            hits.astype(jnp.float32).astype(jnp.bfloat16),
            earlier.astype(jnp.float32).astype(jnp.bfloat16),
            preferred_element_type=jnp.float32,
        )
        rank = jnp.sum(jnp.where(hits, before, 0.0), axis=0, keepdims=True).astype(jnp.int32)
        slots = owners * capacity + rank
        placed = (
            (lax.broadcasted_iota(jnp.int32, (groups * capacity, point_rows), 0) == slots)
            .astype(jnp.float32)
            .astype(jnp.bfloat16)
        )
        points_out[core] = jnp.dot(
            placed, unit_rows(points_ref[...]), preferred_element_type=jnp.float32
        ).astype(jnp.bfloat16)
        if core == 0:
            high = lax.div(tags, 256)
            which = lax.broadcasted_iota(jnp.int32, (tags_out.shape[1], point_rows), 0)
            coded = jnp.where(which == 0, high, jnp.where(which == 1, tags - high * 256, 0))
            tags_out[...] = lax.dot_general(
                placed,
                coded.astype(jnp.float32).astype(jnp.bfloat16),
                NT,
                preferred_element_type=jnp.float32,
            ).astype(jnp.bfloat16)


def marks_kernel(place_ref, after_ref, *refs):
    halves, marks_ref, keep_ref = refs[:-2], refs[-2], refs[-1]
    half = halves[0].shape[0]
    for away, block in enumerate(halves):
        first = pl.multiple_of(lax.bitwise_xor(place_ref[0], away) * half, 16)
        marks_ref[pl.ds(first, half), :] = unit_rows(block[...])
    keep_ref[...] = jnp.full(keep_ref.shape, place_ref[1], jnp.int32)


def pick_kernel(keep_ref, mine_ref, met_ref, *refs):
    refs[-1][...] = jnp.where(keep_ref[0] != 0, mine_ref[...], met_ref[...])


def pass_kernel(block_ref, after_ref, out_ref):
    out_ref[...] = block_ref[...]


def rows_kernel(groups, capacity, points_ref, tags_ref, marks_ref, out_ref):
    marks = marks_ref.shape[0]
    no_tags = jnp.zeros(tags_ref.shape, jnp.bfloat16)
    for core, tags in enumerate((tags_ref[...], no_tags)):
        scores = lax.dot_general(
            points_ref[core], marks_ref[...], NT, preferred_element_type=jnp.float32
        )
        rows = jnp.exp(scores * (0.5 / math.sqrt(points_ref.shape[2]))).astype(jnp.bfloat16)
        if len(out_ref.shape) == 2:
            for group in range(groups):
                here = slice(group * capacity, (group + 1) * capacity)
                first = (2 * group + core) * capacity
                out_ref[first : first + capacity, :marks] = rows[here]
                out_ref[first : first + capacity, marks:] = tags[here]
        else:
            out_ref[core, :, :marks] = rows
            out_ref[core, :, marks:] = tags


def sums_kernel(scale, core_ref, arrived_ref, mine_ref, *refs):
    others, (totals_ref, counts_ref, panel_ref, rows_ref) = refs[:-4], refs[-4:]
    slots, lanes = rows_ref.shape[1:]
    owned, marks = totals_ref.shape[0], mine_ref.shape[0]
    if len(arrived_ref.shape) == 3:
        rows_ref[...] = arrived_ref[...]
    else:
        part = arrived_ref.shape[2] // 2
        for chip in range(arrived_ref.shape[0]):
            first, middle, last = 2 * chip * part, (2 * chip + 1) * part, (2 * chip + 2) * part
            rows_ref[0, first:last, :] = arrived_ref[chip, core_ref[0]]
            rows_ref[1, first:middle, :] = arrived_ref[chip, 1 - core_ref[0], part:, :]
            rows_ref[1, middle:last, :] = arrived_ref[chip, 1 - core_ref[0], :part, :]
    panel_ref[0, :marks, :] = mine_ref[...]
    first = 0
    for other in others:
        panel_ref[1, first : first + other.shape[0], :] = other[...]
        first += other.shape[0]
    panel_ref[:, marks:, :] = jnp.zeros((2, lanes - marks, mine_ref.shape[1]), jnp.bfloat16)
    features = (
        jnp.dot(rows_ref[0], panel_ref[0], preferred_element_type=jnp.float32)
        + jnp.dot(rows_ref[1], panel_ref[1], preferred_element_type=jnp.float32)
    ).astype(jnp.bfloat16)
    which = lax.broadcasted_iota(jnp.int32, (8, lanes - marks), 1)
    weights = jnp.where(which == 0, 256.0, jnp.where(which == 1, 1.0, 0.0)).astype(jnp.bfloat16)
    tags = lax.dot_general(weights, rows_ref[0, :, marks:], NT, preferred_element_type=jnp.float32)
    tags += lax.dot_general(weights, rows_ref[1, :, marks:], NT, preferred_element_type=jnp.float32)
    tags = tags[:1].astype(jnp.int32)
    member = (
        (lax.broadcasted_iota(jnp.int32, (owned, slots), 0) + 1 == tags)
        .astype(jnp.float32)
        .astype(jnp.bfloat16)
    )
    totals_ref[...] = jnp.dot(member, features, preferred_element_type=jnp.float32) * scale
    counts_ref[...] = lax.dot_general(
        jnp.ones((8, slots), jnp.bfloat16), member, NT, preferred_element_type=jnp.float32
    )[:1].astype(jnp.int32)


def call(kernel, shapes, *operands, place=None, scratch=()):
    held = pl.BlockSpec(memory_space=pltpu.VMEM)
    first = [] if place is None else [place]
    return pl.pallas_call(
        kernel,
        out_shape=shapes,
        in_specs=[pl.BlockSpec(memory_space=pltpu.SMEM)] * len(first) + [held] * len(operands),
        out_specs=(held,) * len(shapes) if isinstance(shapes, tuple) else held,
        scratch_shapes=scratch,
        compiler_params=pltpu.CompilerParams(vmem_limit_bytes=VMEM_LIMIT),
    )(*first, *operands)


def array(shape, dtype=jnp.bfloat16):
    return jax.ShapeDtypeStruct(shape, dtype)


def swap(block, axis, mask):
    return lax.ppermute(block, axis, [(i, i ^ mask) for i in range(lax.axis_size(axis))])


def pick(keep, mine, met, *after):
    keep = keep.astype(jnp.int32).reshape(1)
    return call(pick_kernel, array(mine.shape), mine, met, *after, place=keep)


def sides_of(panel, parts, core):
    sides = panel.reshape(parts, 2, -1, panel.shape[1])
    return (
        lax.dynamic_index_in_dim(sides, side, 1, keepdims=False).reshape(-1, panel.shape[1])
        for side in (core, 1 - core)
    )


def exchange(rows, groups, capacity, core):
    slots, lanes = groups * capacity, rows.shape[-1]
    whole_tiles = rows.ndim == 2
    if not whole_tiles:
        rows = rows.reshape(2, groups, capacity, lanes).swapaxes(0, 1)
    arrived = lax.all_to_all(
        rows.reshape(groups, 2 * capacity, lanes), "pts", split_axis=0, concat_axis=0, tiled=True
    ).reshape(groups // 2, 2, 2 * capacity, lanes)
    if whole_tiles:
        return arrived
    even = lax.dynamic_index_in_dim(arrived, core, 1, keepdims=False)
    odd = lax.dynamic_index_in_dim(arrived, 1 - core, 1, keepdims=False)
    odd = jnp.concatenate([odd[:, capacity:], odd[:, :capacity]], axis=1)
    return jnp.stack([even.reshape(slots, lanes), odd.reshape(slots, lanes)])


def body(points, landmarks, panels, panel_index, assignment):
    groups, parts = lax.axis_size("pts"), lax.axis_size("lmk")
    point_rows, width = points.shape
    capacity = 2 * point_rows // groups
    slots = groups * capacity
    owned = CLUSTERS // groups
    depth, columns = panels.shape[1:]
    half = landmarks.shape[0] // 2
    lanes = -(-(depth // 2 + 2) // LANES) * LANES
    me = lax.axis_index("pts")
    marks = lax.dynamic_slice_in_dim(landmarks, (me % 2) * half, half, 0)
    assignment = assignment.reshape(1, point_rows)
    points_met, assignment_met = swap(points, "pts", 1), swap(assignment, "pts", 1)
    differs = panel_index[0] ^ me
    mine, other = sides_of(panels[0], parts, me % 2)
    panel = pick((differs & 1) == 0, mine, swap(other, "pts", 1), points_met, assignment_met)
    near = call(pass_kernel, array(marks.shape), marks, panel)
    halves = [marks] + [
        swap(near if mask == 1 else marks, "lmk", mask) for mask in range(1, parts)
    ]
    masks = [1 << bit for bit in range(1, groups.bit_length() - 1)]
    panel_met = swap(panel, "pts", masks[0])
    place = jnp.stack([lax.axis_index("lmk"), (differs & masks[0]) == 0]).astype(jnp.int32)
    placed, tags = call(
        lambda *refs: place_kernel(groups, capacity, *refs),
        (array((2, slots, width)), array((slots, lanes - depth // 2))),
        points,
        assignment,
        points_met,
        assignment_met,
    )
    marks, keep = call(
        marks_kernel,
        (array((depth // 2, width)), array((1, columns), jnp.int32)),
        tags,
        *halves,
        place=place,
    )
    rows = call(
        lambda *refs: rows_kernel(groups, capacity, *refs),
        array((2 * slots, lanes) if capacity % 16 == 0 else (2, slots, lanes)),
        placed,
        tags,
        marks,
    )
    panel = jnp.where(keep != 0, panel, panel_met)
    for mask in masks[1:]:
        panel = jnp.where((differs & mask) == 0, panel, swap(panel, "pts", mask))
    cut = panel.shape[0] // 2
    others = [swap(panel[:cut], "pts", 1)]
    others.append(swap(call(pass_kernel, array((cut, columns)), panel[cut:], others[0]), "pts", 1))
    arrived = exchange(rows, groups, capacity, me % 2)
    totals, counts = call(
        lambda *refs: sums_kernel(CLUSTERS / (point_rows * groups), *refs),
        (array((owned, columns), jnp.float32), array((1, owned), jnp.int32)),
        arrived,
        panel,
        *others,
        place=(me % 2).astype(jnp.int32).reshape(1),
        scratch=[
            pltpu.VMEM((2, lanes, columns), jnp.bfloat16),
            pltpu.VMEM((2, slots, lanes), jnp.bfloat16),
        ],
    )
    return (totals, counts.reshape(owned))


def solution(mesh):
    in_specs = (P("pts", None), P("lmk", None), P("pts", None, "lmk"), P(), P("pts"))
    out_specs = (P("pts", "lmk"), P("pts"))
    return jax.shard_map(body, mesh=mesh, in_specs=in_specs, out_specs=out_specs, check_vma=False)
```

```python
import math

import jax
import jax.numpy as jnp
from jax import lax
from jax.experimental import pallas as pl
from jax.experimental.pallas import tpu as pltpu
from jax.sharding import PartitionSpec as P

CLUSTERS = 4096
LANES = 128
VMEM_LIMIT = 48 * 1024 * 1024
NT = (((1,), (1,)), ((), ()))


def unit_rows(values_in):
    widened = values_in.astype(jnp.float32)
    scale = lax.rsqrt(jnp.mean(widened * widened, axis=1, keepdims=True) + 1e-06)
    return (widened * scale).astype(jnp.bfloat16)


def place_kernel(groups, capacity, *refs):
    points_out, tags_out = refs[-2:]
    for core in range(2):
        points_ref, assignment_ref = refs[2 * core : 2 * core + 2]
        point_rows = points_ref.shape[0]
        ids = assignment_ref[...]
        owned = CLUSTERS // groups
        owners = lax.div(ids, owned)
        tags = ids - owners * owned + 1
        hits = lax.broadcasted_iota(jnp.int32, (groups, point_rows), 0) == owners
        earlier = lax.broadcasted_iota(
            jnp.int32, (point_rows, point_rows), 0
        ) < lax.broadcasted_iota(jnp.int32, (point_rows, point_rows), 1)
        before = jnp.dot(
            hits.astype(jnp.float32).astype(jnp.bfloat16),
            earlier.astype(jnp.float32).astype(jnp.bfloat16),
            preferred_element_type=jnp.float32,
        )
        rank = jnp.sum(jnp.where(hits, before, 0.0), axis=0, keepdims=True).astype(jnp.int32)
        slots = owners * capacity + rank
        placed = (
            (lax.broadcasted_iota(jnp.int32, (groups * capacity, point_rows), 0) == slots)
            .astype(jnp.float32)
            .astype(jnp.bfloat16)
        )
        points_out[core] = jnp.dot(
            placed, unit_rows(points_ref[...]), preferred_element_type=jnp.float32
        ).astype(jnp.bfloat16)
        if core == 0:
            high = lax.div(tags, 256)
            which = lax.broadcasted_iota(jnp.int32, (tags_out.shape[1], point_rows), 0)
            coded = jnp.where(which == 0, high, jnp.where(which == 1, tags - high * 256, 0))
            tags_out[...] = lax.dot_general(
                placed,
                coded.astype(jnp.float32).astype(jnp.bfloat16),
                NT,
                preferred_element_type=jnp.float32,
            ).astype(jnp.bfloat16)


def keep_kernel(place_ref, *refs):
    refs[-1][...] = jnp.full(refs[-1].shape, place_ref[1], jnp.int32)


def pick_kernel(keep_ref, mine_ref, met_ref, *refs):
    refs[-1][...] = jnp.where(keep_ref[0] != 0, mine_ref[...], met_ref[...])


def pass_kernel(block_ref, after_ref, out_ref):
    out_ref[...] = block_ref[...]


def rows_kernel(groups, capacity, place_ref, points_ref, tags_ref, *refs):
    halves, (out_ref, marks_ref, blocks_ref, sems) = refs[:-4], refs[-4:]
    half, marks = halves[0].shape[0], marks_ref.shape[0]
    for away, block in enumerate(halves):
        first = pl.multiple_of(lax.bitwise_xor(place_ref[0], away) * half, 16)
        marks_ref[pl.ds(first, half), :] = unit_rows(block[...])
    copies = []
    no_tags = jnp.zeros(tags_ref.shape, jnp.bfloat16)
    for core, tags in enumerate((tags_ref[...], no_tags)):
        scores = lax.dot_general(
            points_ref[core], marks_ref[...], NT, preferred_element_type=jnp.float32
        )
        rows = jnp.exp(scores * (0.5 / math.sqrt(points_ref.shape[2]))).astype(jnp.bfloat16)
        if len(out_ref.shape) == 2:
            for group in range(groups):
                here = slice(group * capacity, (group + 1) * capacity)
                there = slice(core * capacity, (core + 1) * capacity)
                blocks_ref[group, there, :marks] = rows[here]
                blocks_ref[group, there, marks:] = tags[here]
                if core == 1:
                    block = slice(2 * group * capacity, 2 * (group + 1) * capacity)
                    copies.append(
                        pltpu.make_async_copy(blocks_ref.at[group], out_ref.at[block, :], sems.at[group])
                    )
                    copies[-1].start()
        else:
            out_ref[core, :, :marks] = rows
            out_ref[core, :, marks:] = tags
    for copy in copies:
        copy.wait()


def sums_kernel(scale, core_ref, arrived_ref, mine_ref, *refs):
    others, (totals_ref, counts_ref, panel_ref, rows_ref) = refs[:-4], refs[-4:]
    slots, lanes = rows_ref.shape[1:]
    owned, marks = totals_ref.shape[0], mine_ref.shape[0]
    if len(arrived_ref.shape) == 3:
        rows_ref[...] = arrived_ref[...]
    else:
        part = arrived_ref.shape[2] // 2
        for chip in range(arrived_ref.shape[0]):
            first, middle, last = 2 * chip * part, (2 * chip + 1) * part, (2 * chip + 2) * part
            rows_ref[0, first:last, :] = arrived_ref[chip, core_ref[0]]
            rows_ref[1, first:middle, :] = arrived_ref[chip, 1 - core_ref[0], part:, :]
            rows_ref[1, middle:last, :] = arrived_ref[chip, 1 - core_ref[0], :part, :]
    panel_ref[0, :marks, :] = mine_ref[...]
    first = 0
    for other in others:
        panel_ref[1, first : first + other.shape[0], :] = other[...]
        first += other.shape[0]
    panel_ref[:, marks:, :] = jnp.zeros((2, lanes - marks, mine_ref.shape[1]), jnp.bfloat16)
    features = (
        jnp.dot(rows_ref[0], panel_ref[0], preferred_element_type=jnp.float32)
        + jnp.dot(rows_ref[1], panel_ref[1], preferred_element_type=jnp.float32)
    ).astype(jnp.bfloat16)
    which = lax.broadcasted_iota(jnp.int32, (8, lanes - marks), 1)
    weights = jnp.where(which == 0, 256.0, jnp.where(which == 1, 1.0, 0.0)).astype(jnp.bfloat16)
    tags = lax.dot_general(weights, rows_ref[0, :, marks:], NT, preferred_element_type=jnp.float32)
    tags += lax.dot_general(weights, rows_ref[1, :, marks:], NT, preferred_element_type=jnp.float32)
    tags = tags[:1].astype(jnp.int32)
    member = (
        (lax.broadcasted_iota(jnp.int32, (owned, slots), 0) + 1 == tags)
        .astype(jnp.float32)
        .astype(jnp.bfloat16)
    )
    totals_ref[...] = jnp.dot(member, features, preferred_element_type=jnp.float32) * scale
    counts_ref[...] = lax.dot_general(
        jnp.ones((8, slots), jnp.bfloat16), member, NT, preferred_element_type=jnp.float32
    )[:1].astype(jnp.int32)


def call(kernel, shapes, *operands, place=None, scratch=(), sent=()):
    held, loose = pl.BlockSpec(memory_space=pltpu.VMEM), pl.BlockSpec(memory_space=pl.ANY)
    first = [] if place is None else [place]
    return pl.pallas_call(
        kernel,
        out_shape=shapes,
        in_specs=[pl.BlockSpec(memory_space=pltpu.SMEM)] * len(first) + [held] * len(operands),
        out_specs=tuple(loose if at in sent else held for at in range(len(shapes)))
        if isinstance(shapes, tuple)
        else held,
        scratch_shapes=scratch,
        compiler_params=pltpu.CompilerParams(vmem_limit_bytes=VMEM_LIMIT),
    )(*first, *operands)


def array(shape, dtype=jnp.bfloat16):
    return jax.ShapeDtypeStruct(shape, dtype)


def swap(block, axis, mask):
    return lax.ppermute(block, axis, [(i, i ^ mask) for i in range(lax.axis_size(axis))])


def pick(keep, mine, met, *after):
    keep = keep.astype(jnp.int32).reshape(1)
    return call(pick_kernel, array(mine.shape), mine, met, *after, place=keep)


def sides_of(panel, parts, core):
    sides = panel.reshape(parts, 2, -1, panel.shape[1])
    return (
        lax.dynamic_index_in_dim(sides, side, 1, keepdims=False).reshape(-1, panel.shape[1])
        for side in (core, 1 - core)
    )


def exchange(rows, groups, capacity, core):
    slots, lanes = groups * capacity, rows.shape[-1]
    whole_tiles = rows.ndim == 2
    if not whole_tiles:
        rows = rows.reshape(2, groups, capacity, lanes).swapaxes(0, 1)
    arrived = lax.all_to_all(
        rows.reshape(groups, 2 * capacity, lanes), "pts", split_axis=0, concat_axis=0, tiled=True
    ).reshape(groups // 2, 2, 2 * capacity, lanes)
    if whole_tiles:
        return arrived
    even = lax.dynamic_index_in_dim(arrived, core, 1, keepdims=False)
    odd = lax.dynamic_index_in_dim(arrived, 1 - core, 1, keepdims=False)
    odd = jnp.concatenate([odd[:, capacity:], odd[:, :capacity]], axis=1)
    return jnp.stack([even.reshape(slots, lanes), odd.reshape(slots, lanes)])


def body(points, landmarks, panels, panel_index, assignment):
    groups, parts = lax.axis_size("pts"), lax.axis_size("lmk")
    point_rows, width = points.shape
    capacity = 2 * point_rows // groups
    slots = groups * capacity
    owned = CLUSTERS // groups
    depth, columns = panels.shape[1:]
    half = landmarks.shape[0] // 2
    lanes = -(-(depth // 2 + 2) // LANES) * LANES
    me = lax.axis_index("pts")
    marks = lax.dynamic_slice_in_dim(landmarks, (me % 2) * half, half, 0)
    assignment = assignment.reshape(1, point_rows)
    points_met, assignment_met = swap(points, "pts", 1), swap(assignment, "pts", 1)
    differs = panel_index[0] ^ me
    mine, other = sides_of(panels[0], parts, me % 2)
    panel = pick((differs & 1) == 0, mine, swap(other, "pts", 1), points_met, assignment_met)
    near = call(pass_kernel, array(marks.shape), marks, panel)
    halves = [marks] + [
        swap(near if mask == 1 else marks, "lmk", mask) for mask in range(1, parts)
    ]
    masks = [1 << bit for bit in range(1, groups.bit_length() - 1)]
    panel_met = swap(panel, "pts", masks[0])
    place = jnp.stack([lax.axis_index("lmk"), (differs & masks[0]) == 0]).astype(jnp.int32)
    placed, tags = call(
        lambda *refs: place_kernel(groups, capacity, *refs),
        (array((2, slots, width)), array((slots, lanes - depth // 2))),
        points,
        assignment,
        points_met,
        assignment_met,
    )
    keep = call(keep_kernel, array((1, columns), jnp.int32), tags, *halves, place=place)
    whole_tiles = capacity % 16 == 0
    (rows,) = call(
        lambda *refs: rows_kernel(groups, capacity, *refs),
        (array((2 * slots, lanes) if whole_tiles else (2, slots, lanes)),),
        placed,
        tags,
        *halves,
        place=place,
        scratch=[
            pltpu.VMEM((depth // 2, width), jnp.bfloat16),
            pltpu.VMEM((groups, 2 * capacity, lanes), jnp.bfloat16),
            pltpu.SemaphoreType.DMA((groups,)),
        ],
        sent=(0,) if whole_tiles else (),
    )
    panel = jnp.where(keep != 0, panel, panel_met)
    for mask in masks[1:]:
        panel = jnp.where((differs & mask) == 0, panel, swap(panel, "pts", mask))
    cut = panel.shape[0] // 2
    others = [swap(panel[:cut], "pts", 1)]
    others.append(swap(call(pass_kernel, array((cut, columns)), panel[cut:], others[0]), "pts", 1))
    arrived = exchange(rows, groups, capacity, me % 2)
    totals, counts = call(
        lambda *refs: sums_kernel(CLUSTERS / (point_rows * groups), *refs),
        (array((owned, columns), jnp.float32), array((1, owned), jnp.int32)),
        arrived,
        panel,
        *others,
        place=(me % 2).astype(jnp.int32).reshape(1),
        scratch=[
            pltpu.VMEM((2, lanes, columns), jnp.bfloat16),
            pltpu.VMEM((2, slots, lanes), jnp.bfloat16),
        ],
    )
    return (totals, counts.reshape(owned))


def solution(mesh):
    in_specs = (P("pts", None), P("lmk", None), P("pts", None, "lmk"), P(), P("pts"))
    out_specs = (P("pts", "lmk"), P("pts"))
    return jax.shard_map(body, mesh=mesh, in_specs=in_specs, out_specs=out_specs, check_vma=False)
```

```python
import math

import jax
import jax.numpy as jnp
from jax import lax
from jax.experimental import pallas as pl
from jax.experimental.pallas import tpu as pltpu
from jax.sharding import PartitionSpec as P

CLUSTERS = 4096
LANES = 128
VMEM_LIMIT = 48 * 1024 * 1024
NT = (((1,), (1,)), ((), ()))


def unit_rows(values_in):
    widened = values_in.astype(jnp.float32)
    scale = lax.rsqrt(jnp.mean(widened * widened, axis=1, keepdims=True) + 1e-06)
    return (widened * scale).astype(jnp.bfloat16)


def place_kernel(groups, capacity, *refs):
    points_out, tags_out = refs[-2:]
    for core in range(2):
        points_ref, assignment_ref = refs[2 * core : 2 * core + 2]
        point_rows = points_ref.shape[0]
        ids = assignment_ref[...]
        owned = CLUSTERS // groups
        owners = lax.div(ids, owned)
        tags = ids - owners * owned + 1
        hits = lax.broadcasted_iota(jnp.int32, (groups, point_rows), 0) == owners
        earlier = lax.broadcasted_iota(
            jnp.int32, (point_rows, point_rows), 0
        ) < lax.broadcasted_iota(jnp.int32, (point_rows, point_rows), 1)
        before = jnp.dot(
            hits.astype(jnp.float32).astype(jnp.bfloat16),
            earlier.astype(jnp.float32).astype(jnp.bfloat16),
            preferred_element_type=jnp.float32,
        )
        rank = jnp.sum(jnp.where(hits, before, 0.0), axis=0, keepdims=True).astype(jnp.int32)
        slots = owners * capacity + rank
        placed = (
            (lax.broadcasted_iota(jnp.int32, (groups * capacity, point_rows), 0) == slots)
            .astype(jnp.float32)
            .astype(jnp.bfloat16)
        )
        points_out[core] = jnp.dot(
            placed, unit_rows(points_ref[...]), preferred_element_type=jnp.float32
        ).astype(jnp.bfloat16)
        if core == 0:
            high = lax.div(tags, 256)
            which = lax.broadcasted_iota(jnp.int32, (tags_out.shape[1], point_rows), 0)
            coded = jnp.where(which == 0, high, jnp.where(which == 1, tags - high * 256, 0))
            tags_out[...] = lax.dot_general(
                placed,
                coded.astype(jnp.float32).astype(jnp.bfloat16),
                NT,
                preferred_element_type=jnp.float32,
            ).astype(jnp.bfloat16)


def marks_kernel(line_ref, choice_ref, after_ref, *refs):
    halves, marks_ref, keep_ref = refs[:-2], refs[-2], refs[-1]
    half = halves[0].shape[0]
    for away, block in enumerate(halves):
        first = pl.multiple_of(lax.bitwise_xor(line_ref[0], away) * half, 16)
        marks_ref[pl.ds(first, half), :] = unit_rows(block[...])
    keep_ref[...] = jnp.full(keep_ref.shape, choice_ref[0], jnp.int32)


def pick_kernel(keep_ref, mine_ref, met_ref, *refs):
    refs[-1][...] = jnp.where(keep_ref[0] != 0, mine_ref[...], met_ref[...])


def pass_kernel(block_ref, after_ref, out_ref):
    out_ref[...] = block_ref[...]


def rows_kernel(groups, capacity, points_ref, tags_ref, marks_ref, out_ref):
    marks = marks_ref.shape[0]
    no_tags = jnp.zeros(tags_ref.shape, jnp.bfloat16)
    for core, tags in enumerate((tags_ref[...], no_tags)):
        scores = lax.dot_general(
            points_ref[core], marks_ref[...], NT, preferred_element_type=jnp.float32
        )
        rows = jnp.exp(scores * (0.5 / math.sqrt(points_ref.shape[2]))).astype(jnp.bfloat16)
        if len(out_ref.shape) == 2:
            for group in range(groups):
                here = slice(group * capacity, (group + 1) * capacity)
                first = (2 * group + core) * capacity
                out_ref[first : first + capacity, :marks] = rows[here]
                out_ref[first : first + capacity, marks:] = tags[here]
        else:
            out_ref[core, :, :marks] = rows
            out_ref[core, :, marks:] = tags


def sums_kernel(scale, core_ref, arrived_ref, mine_ref, *refs):
    others, (totals_ref, counts_ref, panel_ref, rows_ref) = refs[:-4], refs[-4:]
    slots, lanes = rows_ref.shape[1:]
    owned, marks = totals_ref.shape[0], mine_ref.shape[0]
    if len(arrived_ref.shape) == 3:
        rows_ref[...] = arrived_ref[...]
    else:
        part = arrived_ref.shape[2] // 2
        for chip in range(arrived_ref.shape[0]):
            first, middle, last = 2 * chip * part, (2 * chip + 1) * part, (2 * chip + 2) * part
            rows_ref[0, first:last, :] = arrived_ref[chip, core_ref[0]]
            rows_ref[1, first:middle, :] = arrived_ref[chip, 1 - core_ref[0], part:, :]
            rows_ref[1, middle:last, :] = arrived_ref[chip, 1 - core_ref[0], :part, :]
    panel_ref[0, :marks, :] = mine_ref[...]
    first = 0
    for other in others:
        panel_ref[1, first : first + other.shape[0], :] = other[...]
        first += other.shape[0]
    panel_ref[:, marks:, :] = jnp.zeros((2, lanes - marks, mine_ref.shape[1]), jnp.bfloat16)
    features = (
        jnp.dot(rows_ref[0], panel_ref[0], preferred_element_type=jnp.float32)
        + jnp.dot(rows_ref[1], panel_ref[1], preferred_element_type=jnp.float32)
    ).astype(jnp.bfloat16)
    which = lax.broadcasted_iota(jnp.int32, (8, lanes - marks), 1)
    weights = jnp.where(which == 0, 256.0, jnp.where(which == 1, 1.0, 0.0)).astype(jnp.bfloat16)
    tags = lax.dot_general(weights, rows_ref[0, :, marks:], NT, preferred_element_type=jnp.float32)
    tags += lax.dot_general(weights, rows_ref[1, :, marks:], NT, preferred_element_type=jnp.float32)
    tags = tags[:1].astype(jnp.int32)
    member = (
        (lax.broadcasted_iota(jnp.int32, (owned, slots), 0) + 1 == tags)
        .astype(jnp.float32)
        .astype(jnp.bfloat16)
    )
    totals_ref[...] = jnp.dot(member, features, preferred_element_type=jnp.float32) * scale
    counts_ref[...] = lax.dot_general(
        jnp.ones((8, slots), jnp.bfloat16), member, NT, preferred_element_type=jnp.float32
    )[:1].astype(jnp.int32)


def call(kernel, shapes, *operands, place=(), scratch=()):
    held = pl.BlockSpec(memory_space=pltpu.VMEM)
    first = [scalar.astype(jnp.int32).reshape(1) for scalar in place]
    return pl.pallas_call(
        kernel,
        out_shape=shapes,
        in_specs=[pl.BlockSpec(memory_space=pltpu.SMEM)] * len(first) + [held] * len(operands),
        out_specs=(held,) * len(shapes) if isinstance(shapes, tuple) else held,
        scratch_shapes=scratch,
        compiler_params=pltpu.CompilerParams(vmem_limit_bytes=VMEM_LIMIT),
    )(*first, *operands)


def array(shape, dtype=jnp.bfloat16):
    return jax.ShapeDtypeStruct(shape, dtype)


def swap(block, axis, mask):
    return lax.ppermute(block, axis, [(i, i ^ mask) for i in range(lax.axis_size(axis))])


def pick(keep, mine, met, *after):
    return call(pick_kernel, array(mine.shape), mine, met, *after, place=(keep,))


def sides_of(panel, parts, core):
    sides = panel.reshape(parts, 2, -1, panel.shape[1])
    return (
        lax.dynamic_index_in_dim(sides, side, 1, keepdims=False).reshape(-1, panel.shape[1])
        for side in (core, 1 - core)
    )


def exchange(rows, groups, capacity, core):
    slots, lanes = groups * capacity, rows.shape[-1]
    whole_tiles = rows.ndim == 2
    if not whole_tiles:
        rows = rows.reshape(2, groups, capacity, lanes).swapaxes(0, 1)
    arrived = lax.all_to_all(
        rows.reshape(groups, 2 * capacity, lanes), "pts", split_axis=0, concat_axis=0, tiled=True
    ).reshape(groups // 2, 2, 2 * capacity, lanes)
    if whole_tiles:
        return arrived
    even = lax.dynamic_index_in_dim(arrived, core, 1, keepdims=False)
    odd = lax.dynamic_index_in_dim(arrived, 1 - core, 1, keepdims=False)
    odd = jnp.concatenate([odd[:, capacity:], odd[:, :capacity]], axis=1)
    return jnp.stack([even.reshape(slots, lanes), odd.reshape(slots, lanes)])


def body(points, landmarks, panels, panel_index, assignment):
    groups, parts = lax.axis_size("pts"), lax.axis_size("lmk")
    point_rows, width = points.shape
    capacity = 2 * point_rows // groups
    slots = groups * capacity
    owned = CLUSTERS // groups
    depth, columns = panels.shape[1:]
    half = landmarks.shape[0] // 2
    lanes = -(-(depth // 2 + 2) // LANES) * LANES
    me = lax.axis_index("pts")
    marks = lax.dynamic_slice_in_dim(landmarks, (me % 2) * half, half, 0)
    assignment = assignment.reshape(1, point_rows)
    points_met, assignment_met = swap(points, "pts", 1), swap(assignment, "pts", 1)
    differs = panel_index[0] ^ me
    mine, other = sides_of(panels[0], parts, me % 2)
    panel = pick((differs & 1) == 0, mine, swap(other, "pts", 1), points_met, assignment_met)
    near = call(pass_kernel, array(marks.shape), marks, panel)
    halves = [marks] + [
        swap(near if mask == 1 else marks, "lmk", mask) for mask in range(1, parts)
    ]
    masks = [1 << bit for bit in range(1, groups.bit_length() - 1)]
    panel_met = swap(panel, "pts", masks[0])
    placed, tags = call(
        lambda *refs: place_kernel(groups, capacity, *refs),
        (array((2, slots, width)), array((slots, lanes - depth // 2))),
        points,
        assignment,
        points_met,
        assignment_met,
    )
    marks, keep = call(
        marks_kernel,
        (array((depth // 2, width)), array((1, columns), jnp.int32)),
        tags,
        *halves,
        place=(lax.axis_index("lmk"), (differs & masks[0]) == 0),
    )
    rows = call(
        lambda *refs: rows_kernel(groups, capacity, *refs),
        array((2 * slots, lanes) if capacity % 16 == 0 else (2, slots, lanes)),
        placed,
        tags,
        marks,
    )
    panel = jnp.where(keep != 0, panel, panel_met)
    for mask in masks[1:]:
        panel = jnp.where((differs & mask) == 0, panel, swap(panel, "pts", mask))
    cut = panel.shape[0] // 2
    others = [swap(panel[:cut], "pts", 1)]
    others.append(swap(call(pass_kernel, array((cut, columns)), panel[cut:], others[0]), "pts", 1))
    arrived = exchange(rows, groups, capacity, me % 2)
    totals, counts = call(
        lambda *refs: sums_kernel(CLUSTERS / (point_rows * groups), *refs),
        (array((owned, columns), jnp.float32), array((1, owned), jnp.int32)),
        arrived,
        panel,
        *others,
        place=(me % 2,),
        scratch=[
            pltpu.VMEM((2, lanes, columns), jnp.bfloat16),
            pltpu.VMEM((2, slots, lanes), jnp.bfloat16),
        ],
    )
    return (totals, counts.reshape(owned))


def solution(mesh):
    in_specs = (P("pts", None), P("lmk", None), P("pts", None, "lmk"), P(), P("pts"))
    out_specs = (P("pts", "lmk"), P("pts"))
    return jax.shard_map(body, mesh=mesh, in_specs=in_specs, out_specs=out_specs, check_vma=False)
```

```python
import math

import jax
import jax.numpy as jnp
from jax import lax
from jax.experimental import pallas as pl
from jax.experimental.pallas import tpu as pltpu
from jax.sharding import PartitionSpec as P

CLUSTERS = 4096
LANES = 128
VMEM_LIMIT = 48 * 1024 * 1024
NT = (((1,), (1,)), ((), ()))


def unit_rows(values_in):
    widened = values_in.astype(jnp.float32)
    scale = lax.rsqrt(jnp.mean(widened * widened, axis=1, keepdims=True) + 1e-06)
    return (widened * scale).astype(jnp.bfloat16)


def place_kernel(groups, capacity, after_ref, *refs):
    points_out, tags_out = refs[-2:]
    for core in range(2):
        points_ref, assignment_ref = refs[2 * core : 2 * core + 2]
        point_rows = points_ref.shape[0]
        ids = assignment_ref[...]
        owned = CLUSTERS // groups
        owners = lax.div(ids, owned)
        tags = ids - owners * owned + 1
        hits = lax.broadcasted_iota(jnp.int32, (groups, point_rows), 0) == owners
        earlier = lax.broadcasted_iota(
            jnp.int32, (point_rows, point_rows), 0
        ) < lax.broadcasted_iota(jnp.int32, (point_rows, point_rows), 1)
        before = jnp.dot(
            hits.astype(jnp.float32).astype(jnp.bfloat16),
            earlier.astype(jnp.float32).astype(jnp.bfloat16),
            preferred_element_type=jnp.float32,
        )
        rank = jnp.sum(jnp.where(hits, before, 0.0), axis=0, keepdims=True).astype(jnp.int32)
        slots = owners * capacity + rank
        placed = (
            (lax.broadcasted_iota(jnp.int32, (groups * capacity, point_rows), 0) == slots)
            .astype(jnp.float32)
            .astype(jnp.bfloat16)
        )
        points_out[core] = jnp.dot(
            placed, unit_rows(points_ref[...]), preferred_element_type=jnp.float32
        ).astype(jnp.bfloat16)
        if core == 0:
            high = lax.div(tags, 256)
            which = lax.broadcasted_iota(jnp.int32, (tags_out.shape[1], point_rows), 0)
            coded = jnp.where(which == 0, high, jnp.where(which == 1, tags - high * 256, 0))
            tags_out[...] = lax.dot_general(
                placed,
                coded.astype(jnp.float32).astype(jnp.bfloat16),
                NT,
                preferred_element_type=jnp.float32,
            ).astype(jnp.bfloat16)


def marks_kernel(line_ref, choice_ref, after_ref, *refs):
    halves, marks_ref, keep_ref = refs[:-2], refs[-2], refs[-1]
    half = halves[0].shape[0]
    for away, block in enumerate(halves):
        first = pl.multiple_of(lax.bitwise_xor(line_ref[0], away) * half, 16)
        marks_ref[pl.ds(first, half), :] = unit_rows(block[...])
    keep_ref[...] = jnp.full(keep_ref.shape, choice_ref[0], jnp.int32)


def pick_kernel(keep_ref, mine_ref, met_ref, *refs):
    refs[-1][...] = jnp.where(keep_ref[0] != 0, mine_ref[...], met_ref[...])


def pass_kernel(block_ref, after_ref, out_ref):
    out_ref[...] = block_ref[...]


def rows_kernel(groups, capacity, points_ref, tags_ref, marks_ref, out_ref):
    marks = marks_ref.shape[0]
    no_tags = jnp.zeros(tags_ref.shape, jnp.bfloat16)
    for core, tags in enumerate((tags_ref[...], no_tags)):
        scores = lax.dot_general(
            points_ref[core], marks_ref[...], NT, preferred_element_type=jnp.float32
        )
        rows = jnp.exp(scores * (0.5 / math.sqrt(points_ref.shape[2]))).astype(jnp.bfloat16)
        if len(out_ref.shape) == 2:
            for group in range(groups):
                here = slice(group * capacity, (group + 1) * capacity)
                first = (2 * group + core) * capacity
                out_ref[first : first + capacity, :marks] = rows[here]
                out_ref[first : first + capacity, marks:] = tags[here]
        else:
            out_ref[core, :, :marks] = rows
            out_ref[core, :, marks:] = tags


def sums_kernel(scale, core_ref, arrived_ref, mine_ref, *refs):
    others, (totals_ref, counts_ref, panel_ref, rows_ref) = refs[:-4], refs[-4:]
    slots, lanes = rows_ref.shape[1:]
    owned, marks = totals_ref.shape[0], mine_ref.shape[0]
    if len(arrived_ref.shape) == 3:
        rows_ref[...] = arrived_ref[...]
    else:
        part = arrived_ref.shape[2] // 2
        for chip in range(arrived_ref.shape[0]):
            first, middle, last = 2 * chip * part, (2 * chip + 1) * part, (2 * chip + 2) * part
            rows_ref[0, first:last, :] = arrived_ref[chip, core_ref[0]]
            rows_ref[1, first:middle, :] = arrived_ref[chip, 1 - core_ref[0], part:, :]
            rows_ref[1, middle:last, :] = arrived_ref[chip, 1 - core_ref[0], :part, :]
    panel_ref[0, :marks, :] = mine_ref[...]
    first = 0
    for other in others:
        panel_ref[1, first : first + other.shape[0], :] = other[...]
        first += other.shape[0]
    panel_ref[:, marks:, :] = jnp.zeros((2, lanes - marks, mine_ref.shape[1]), jnp.bfloat16)
    features = (
        jnp.dot(rows_ref[0], panel_ref[0], preferred_element_type=jnp.float32)
        + jnp.dot(rows_ref[1], panel_ref[1], preferred_element_type=jnp.float32)
    ).astype(jnp.bfloat16)
    which = lax.broadcasted_iota(jnp.int32, (8, lanes - marks), 1)
    weights = jnp.where(which == 0, 256.0, jnp.where(which == 1, 1.0, 0.0)).astype(jnp.bfloat16)
    tags = lax.dot_general(weights, rows_ref[0, :, marks:], NT, preferred_element_type=jnp.float32)
    tags += lax.dot_general(weights, rows_ref[1, :, marks:], NT, preferred_element_type=jnp.float32)
    tags = tags[:1].astype(jnp.int32)
    member = (
        (lax.broadcasted_iota(jnp.int32, (owned, slots), 0) + 1 == tags)
        .astype(jnp.float32)
        .astype(jnp.bfloat16)
    )
    totals_ref[...] = jnp.dot(member, features, preferred_element_type=jnp.float32) * scale
    counts_ref[...] = lax.dot_general(
        jnp.ones((8, slots), jnp.bfloat16), member, NT, preferred_element_type=jnp.float32
    )[:1].astype(jnp.int32)


def call(kernel, shapes, *operands, place=(), scratch=()):
    held = pl.BlockSpec(memory_space=pltpu.VMEM)
    first = [scalar.astype(jnp.int32).reshape(-1) for scalar in place]
    return pl.pallas_call(
        kernel,
        out_shape=shapes,
        in_specs=[pl.BlockSpec(memory_space=pltpu.SMEM)] * len(first) + [held] * len(operands),
        out_specs=(held,) * len(shapes) if isinstance(shapes, tuple) else held,
        scratch_shapes=scratch,
        compiler_params=pltpu.CompilerParams(vmem_limit_bytes=VMEM_LIMIT),
    )(*first, *operands)


def array(shape, dtype=jnp.bfloat16):
    return jax.ShapeDtypeStruct(shape, dtype)


def swap(block, axis, mask):
    return lax.ppermute(block, axis, [(i, i ^ mask) for i in range(lax.axis_size(axis))])


def pick(keep, mine, met, *after):
    return call(pick_kernel, array(mine.shape), mine, met, *after, place=(keep,))


def sides_of(panel, parts, core):
    sides = panel.reshape(parts, 2, -1, panel.shape[1])
    return (
        lax.dynamic_index_in_dim(sides, side, 1, keepdims=False).reshape(-1, panel.shape[1])
        for side in (core, 1 - core)
    )


def exchange(rows, groups, capacity, core):
    slots, lanes = groups * capacity, rows.shape[-1]
    whole_tiles = rows.ndim == 2
    if not whole_tiles:
        rows = rows.reshape(2, groups, capacity, lanes).swapaxes(0, 1)
    arrived = lax.all_to_all(
        rows.reshape(groups, 2 * capacity, lanes), "pts", split_axis=0, concat_axis=0, tiled=True
    ).reshape(groups // 2, 2, 2 * capacity, lanes)
    if whole_tiles:
        return arrived
    even = lax.dynamic_index_in_dim(arrived, core, 1, keepdims=False)
    odd = lax.dynamic_index_in_dim(arrived, 1 - core, 1, keepdims=False)
    odd = jnp.concatenate([odd[:, capacity:], odd[:, :capacity]], axis=1)
    return jnp.stack([even.reshape(slots, lanes), odd.reshape(slots, lanes)])


def body(points, landmarks, panels, panel_index, assignment):
    groups, parts = lax.axis_size("pts"), lax.axis_size("lmk")
    point_rows, width = points.shape
    capacity = 2 * point_rows // groups
    slots = groups * capacity
    owned = CLUSTERS // groups
    depth, columns = panels.shape[1:]
    half = landmarks.shape[0] // 2
    lanes = -(-(depth // 2 + 2) // LANES) * LANES
    me = lax.axis_index("pts")
    marks = lax.dynamic_slice_in_dim(landmarks, (me % 2) * half, half, 0)
    assignment = assignment.reshape(1, point_rows)
    points_met, assignment_met = swap(points, "pts", 1), swap(assignment, "pts", 1)
    differs = panel_index[0] ^ me
    mine, other = sides_of(panels[0], parts, me % 2)
    panel = pick((differs & 1) == 0, mine, swap(other, "pts", 1), points_met, assignment_met)
    near = call(pass_kernel, array(marks.shape), marks, panel)
    halves = [marks] + [
        swap(near if mask == 1 else marks, "lmk", mask) for mask in range(1, parts)
    ]
    masks = [1 << bit for bit in range(1, groups.bit_length() - 1)]
    panel_met = swap(panel, "pts", masks[0])
    placed, tags = call(
        lambda *refs: place_kernel(groups, capacity, *refs),
        (array((2, slots, width)), array((slots, lanes - depth // 2))),
        points,
        assignment,
        points_met,
        assignment_met,
        place=(jnp.stack([lax.axis_index("lmk"), (differs & masks[0]) == 0]).astype(jnp.int32),),
    )
    marks, keep = call(
        marks_kernel,
        (array((depth // 2, width)), array((1, columns), jnp.int32)),
        tags,
        *halves,
        place=(lax.axis_index("lmk"), (differs & masks[0]) == 0),
    )
    rows = call(
        lambda *refs: rows_kernel(groups, capacity, *refs),
        array((2 * slots, lanes) if capacity % 16 == 0 else (2, slots, lanes)),
        placed,
        tags,
        marks,
    )
    panel = jnp.where(keep != 0, panel, panel_met)
    for mask in masks[1:]:
        panel = jnp.where((differs & mask) == 0, panel, swap(panel, "pts", mask))
    cut = panel.shape[0] // 2
    others = [swap(panel[:cut], "pts", 1)]
    others.append(swap(call(pass_kernel, array((cut, columns)), panel[cut:], others[0]), "pts", 1))
    arrived = exchange(rows, groups, capacity, me % 2)
    totals, counts = call(
        lambda *refs: sums_kernel(CLUSTERS / (point_rows * groups), *refs),
        (array((owned, columns), jnp.float32), array((1, owned), jnp.int32)),
        arrived,
        panel,
        *others,
        place=(me % 2,),
        scratch=[
            pltpu.VMEM((2, lanes, columns), jnp.bfloat16),
            pltpu.VMEM((2, slots, lanes), jnp.bfloat16),
        ],
    )
    return (totals, counts.reshape(owned))


def solution(mesh):
    in_specs = (P("pts", None), P("lmk", None), P("pts", None, "lmk"), P(), P("pts"))
    out_specs = (P("pts", "lmk"), P("pts"))
    return jax.shard_map(body, mesh=mesh, in_specs=in_specs, out_specs=out_specs, check_vma=False)
```

```python
import math

import jax
import jax.numpy as jnp
from jax import lax
from jax.experimental import pallas as pl
from jax.experimental.pallas import tpu as pltpu
from jax.sharding import PartitionSpec as P

CLUSTERS = 4096
LANES = 128
VMEM_LIMIT = 48 * 1024 * 1024
NT = (((1,), (1,)), ((), ()))


def unit_rows(values_in):
    widened = values_in.astype(jnp.float32)
    scale = lax.rsqrt(jnp.mean(widened * widened, axis=1, keepdims=True) + 1e-06)
    return (widened * scale).astype(jnp.bfloat16)


def place_kernel(groups, capacity, after_ref, *refs):
    points_out, tags_out = refs[-2:]
    for core in range(2):
        points_ref, assignment_ref = refs[2 * core : 2 * core + 2]
        point_rows = points_ref.shape[0]
        ids = assignment_ref[...]
        owned = CLUSTERS // groups
        owners = lax.div(ids, owned)
        tags = ids - owners * owned + 1
        hits = lax.broadcasted_iota(jnp.int32, (groups, point_rows), 0) == owners
        earlier = lax.broadcasted_iota(
            jnp.int32, (point_rows, point_rows), 0
        ) < lax.broadcasted_iota(jnp.int32, (point_rows, point_rows), 1)
        before = jnp.dot(
            hits.astype(jnp.float32).astype(jnp.bfloat16),
            earlier.astype(jnp.float32).astype(jnp.bfloat16),
            preferred_element_type=jnp.float32,
        )
        rank = jnp.sum(jnp.where(hits, before, 0.0), axis=0, keepdims=True).astype(jnp.int32)
        slots = owners * capacity + rank
        placed = (
            (lax.broadcasted_iota(jnp.int32, (groups * capacity, point_rows), 0) == slots)
            .astype(jnp.float32)
            .astype(jnp.bfloat16)
        )
        points_out[core] = jnp.dot(
            placed, unit_rows(points_ref[...]), preferred_element_type=jnp.float32
        ).astype(jnp.bfloat16)
        if core == 0:
            high = lax.div(tags, 256)
            which = lax.broadcasted_iota(jnp.int32, (tags_out.shape[1], point_rows), 0)
            coded = jnp.where(which == 0, high, jnp.where(which == 1, tags - high * 256, 0))
            tags_out[...] = lax.dot_general(
                placed,
                coded.astype(jnp.float32).astype(jnp.bfloat16),
                NT,
                preferred_element_type=jnp.float32,
            ).astype(jnp.bfloat16)


def marks_kernel(line_ref, choice_ref, after_ref, *refs):
    halves, marks_ref, keep_ref = refs[:-2], refs[-2], refs[-1]
    half = halves[0].shape[0]
    for away, block in enumerate(halves):
        first = pl.multiple_of(lax.bitwise_xor(line_ref[0], away) * half, 16)
        marks_ref[pl.ds(first, half), :] = unit_rows(block[...])
    keep_ref[...] = jnp.full(keep_ref.shape, choice_ref[0], jnp.int32)


def pick_kernel(keep_ref, mine_ref, met_ref, *refs):
    refs[-1][...] = jnp.where(keep_ref[0] != 0, mine_ref[...], met_ref[...])


def pass_kernel(block_ref, after_ref, out_ref):
    out_ref[...] = block_ref[...]


def rows_kernel(groups, capacity, points_ref, tags_ref, marks_ref, out_ref):
    marks = marks_ref.shape[0]
    no_tags = jnp.zeros(tags_ref.shape, jnp.bfloat16)
    slots, width = points_ref.shape[1:]
    scores = lax.dot_general(
        points_ref[...].reshape(2 * slots, width), marks_ref[...], NT, preferred_element_type=jnp.float32
    )
    both = jnp.exp(scores * (0.5 / math.sqrt(width))).astype(jnp.bfloat16)
    for core, tags in enumerate((tags_ref[...], no_tags)):
        rows = both[core * slots : (core + 1) * slots]
        if len(out_ref.shape) == 2:
            for group in range(groups):
                here = slice(group * capacity, (group + 1) * capacity)
                first = (2 * group + core) * capacity
                out_ref[first : first + capacity, :marks] = rows[here]
                out_ref[first : first + capacity, marks:] = tags[here]
        else:
            out_ref[core, :, :marks] = rows
            out_ref[core, :, marks:] = tags


def sums_kernel(scale, core_ref, arrived_ref, mine_ref, *refs):
    others, (totals_ref, counts_ref, panel_ref, rows_ref) = refs[:-4], refs[-4:]
    slots, lanes = rows_ref.shape[1:]
    owned, marks = totals_ref.shape[0], mine_ref.shape[0]
    if len(arrived_ref.shape) == 3:
        rows_ref[...] = arrived_ref[...]
    else:
        part = arrived_ref.shape[2] // 2
        for chip in range(arrived_ref.shape[0]):
            first, middle, last = 2 * chip * part, (2 * chip + 1) * part, (2 * chip + 2) * part
            rows_ref[0, first:last, :] = arrived_ref[chip, core_ref[0]]
            rows_ref[1, first:middle, :] = arrived_ref[chip, 1 - core_ref[0], part:, :]
            rows_ref[1, middle:last, :] = arrived_ref[chip, 1 - core_ref[0], :part, :]
    panel_ref[0, :marks, :] = mine_ref[...]
    first = 0
    for other in others:
        panel_ref[1, first : first + other.shape[0], :] = other[...]
        first += other.shape[0]
    panel_ref[:, marks:, :] = jnp.zeros((2, lanes - marks, mine_ref.shape[1]), jnp.bfloat16)
    features = (
        jnp.dot(rows_ref[0], panel_ref[0], preferred_element_type=jnp.float32)
        + jnp.dot(rows_ref[1], panel_ref[1], preferred_element_type=jnp.float32)
    ).astype(jnp.bfloat16)
    which = lax.broadcasted_iota(jnp.int32, (8, lanes - marks), 1)
    weights = jnp.where(which == 0, 256.0, jnp.where(which == 1, 1.0, 0.0)).astype(jnp.bfloat16)
    tags = lax.dot_general(weights, rows_ref[0, :, marks:], NT, preferred_element_type=jnp.float32)
    tags += lax.dot_general(weights, rows_ref[1, :, marks:], NT, preferred_element_type=jnp.float32)
    tags = tags[:1].astype(jnp.int32)
    member = (
        (lax.broadcasted_iota(jnp.int32, (owned, slots), 0) + 1 == tags)
        .astype(jnp.float32)
        .astype(jnp.bfloat16)
    )
    totals_ref[...] = jnp.dot(member, features, preferred_element_type=jnp.float32) * scale
    counts_ref[...] = lax.dot_general(
        jnp.ones((8, slots), jnp.bfloat16), member, NT, preferred_element_type=jnp.float32
    )[:1].astype(jnp.int32)


def call(kernel, shapes, *operands, place=(), scratch=()):
    held = pl.BlockSpec(memory_space=pltpu.VMEM)
    first = [scalar.astype(jnp.int32).reshape(-1) for scalar in place]
    return pl.pallas_call(
        kernel,
        out_shape=shapes,
        in_specs=[pl.BlockSpec(memory_space=pltpu.SMEM)] * len(first) + [held] * len(operands),
        out_specs=(held,) * len(shapes) if isinstance(shapes, tuple) else held,
        scratch_shapes=scratch,
        compiler_params=pltpu.CompilerParams(vmem_limit_bytes=VMEM_LIMIT),
    )(*first, *operands)


def array(shape, dtype=jnp.bfloat16):
    return jax.ShapeDtypeStruct(shape, dtype)


def swap(block, axis, mask):
    return lax.ppermute(block, axis, [(i, i ^ mask) for i in range(lax.axis_size(axis))])


def pick(keep, mine, met, *after):
    return call(pick_kernel, array(mine.shape), mine, met, *after, place=(keep,))


def sides_of(panel, parts, core):
    sides = panel.reshape(parts, 2, -1, panel.shape[1])
    return (
        lax.dynamic_index_in_dim(sides, side, 1, keepdims=False).reshape(-1, panel.shape[1])
        for side in (core, 1 - core)
    )


def exchange(rows, groups, capacity, core):
    slots, lanes = groups * capacity, rows.shape[-1]
    whole_tiles = rows.ndim == 2
    if not whole_tiles:
        rows = rows.reshape(2, groups, capacity, lanes).swapaxes(0, 1)
    arrived = lax.all_to_all(
        rows.reshape(groups, 2 * capacity, lanes), "pts", split_axis=0, concat_axis=0, tiled=True
    ).reshape(groups // 2, 2, 2 * capacity, lanes)
    if whole_tiles:
        return arrived
    even = lax.dynamic_index_in_dim(arrived, core, 1, keepdims=False)
    odd = lax.dynamic_index_in_dim(arrived, 1 - core, 1, keepdims=False)
    odd = jnp.concatenate([odd[:, capacity:], odd[:, :capacity]], axis=1)
    return jnp.stack([even.reshape(slots, lanes), odd.reshape(slots, lanes)])


def body(points, landmarks, panels, panel_index, assignment):
    groups, parts = lax.axis_size("pts"), lax.axis_size("lmk")
    point_rows, width = points.shape
    capacity = 2 * point_rows // groups
    slots = groups * capacity
    owned = CLUSTERS // groups
    depth, columns = panels.shape[1:]
    half = landmarks.shape[0] // 2
    lanes = -(-(depth // 2 + 2) // LANES) * LANES
    me = lax.axis_index("pts")
    marks = lax.dynamic_slice_in_dim(landmarks, (me % 2) * half, half, 0)
    assignment = assignment.reshape(1, point_rows)
    points_met, assignment_met = swap(points, "pts", 1), swap(assignment, "pts", 1)
    differs = panel_index[0] ^ me
    mine, other = sides_of(panels[0], parts, me % 2)
    panel = pick((differs & 1) == 0, mine, swap(other, "pts", 1), points_met, assignment_met)
    near = call(pass_kernel, array(marks.shape), marks, panel)
    halves = [marks] + [
        swap(near if mask == 1 else marks, "lmk", mask) for mask in range(1, parts)
    ]
    masks = [1 << bit for bit in range(1, groups.bit_length() - 1)]
    panel_met = swap(panel, "pts", masks[0])
    placed, tags = call(
        lambda *refs: place_kernel(groups, capacity, *refs),
        (array((2, slots, width)), array((slots, lanes - depth // 2))),
        points,
        assignment,
        points_met,
        assignment_met,
        place=(jnp.stack([lax.axis_index("lmk"), (differs & masks[0]) == 0]).astype(jnp.int32),),
    )
    marks, keep = call(
        marks_kernel,
        (array((depth // 2, width)), array((1, columns), jnp.int32)),
        tags,
        *halves,
        place=(lax.axis_index("lmk"), (differs & masks[0]) == 0),
    )
    rows = call(
        lambda *refs: rows_kernel(groups, capacity, *refs),
        array((2 * slots, lanes) if capacity % 16 == 0 else (2, slots, lanes)),
        placed,
        tags,
        marks,
    )
    panel = jnp.where(keep != 0, panel, panel_met)
    for mask in masks[1:]:
        panel = jnp.where((differs & mask) == 0, panel, swap(panel, "pts", mask))
    cut = panel.shape[0] // 2
    others = [swap(panel[:cut], "pts", 1)]
    others.append(swap(call(pass_kernel, array((cut, columns)), panel[cut:], others[0]), "pts", 1))
    arrived = exchange(rows, groups, capacity, me % 2)
    totals, counts = call(
        lambda *refs: sums_kernel(CLUSTERS / (point_rows * groups), *refs),
        (array((owned, columns), jnp.float32), array((1, owned), jnp.int32)),
        arrived,
        panel,
        *others,
        place=(me % 2,),
        scratch=[
            pltpu.VMEM((2, lanes, columns), jnp.bfloat16),
            pltpu.VMEM((2, slots, lanes), jnp.bfloat16),
        ],
    )
    return (totals, counts.reshape(owned))


def solution(mesh):
    in_specs = (P("pts", None), P("lmk", None), P("pts", None, "lmk"), P(), P("pts"))
    out_specs = (P("pts", "lmk"), P("pts"))
    return jax.shard_map(body, mesh=mesh, in_specs=in_specs, out_specs=out_specs, check_vma=False)
```

```python
import math

import jax
import jax.numpy as jnp
from jax import lax
from jax.experimental import pallas as pl
from jax.experimental.pallas import tpu as pltpu
from jax.sharding import PartitionSpec as P

CLUSTERS = 4096
LANES = 128
VMEM_LIMIT = 48 * 1024 * 1024
NT = (((1,), (1,)), ((), ()))


def unit_rows(values_in):
    widened = values_in.astype(jnp.float32)
    scale = lax.rsqrt(jnp.mean(widened * widened, axis=1, keepdims=True) + 1e-06)
    return (widened * scale).astype(jnp.bfloat16)


def place_kernel(groups, capacity, after_ref, *refs):
    points_out, tags_out = refs[-2:]
    for core in range(2):
        points_ref, assignment_ref = refs[2 * core : 2 * core + 2]
        point_rows = points_ref.shape[0]
        ids = assignment_ref[...]
        owned = CLUSTERS // groups
        owners = lax.div(ids, owned)
        tags = ids - owners * owned + 1
        hits = lax.broadcasted_iota(jnp.int32, (groups, point_rows), 0) == owners
        earlier = lax.broadcasted_iota(
            jnp.int32, (point_rows, point_rows), 0
        ) < lax.broadcasted_iota(jnp.int32, (point_rows, point_rows), 1)
        before = jnp.dot(
            hits.astype(jnp.float32).astype(jnp.bfloat16),
            earlier.astype(jnp.float32).astype(jnp.bfloat16),
            preferred_element_type=jnp.float32,
        )
        rank = jnp.sum(jnp.where(hits, before, 0.0), axis=0, keepdims=True).astype(jnp.int32)
        slots = owners * capacity + rank
        placed = (
            (lax.broadcasted_iota(jnp.int32, (groups * capacity, point_rows), 0) == slots)
            .astype(jnp.float32)
            .astype(jnp.bfloat16)
        )
        points_out[core] = jnp.dot(
            placed, unit_rows(points_ref[...]), preferred_element_type=jnp.float32
        ).astype(jnp.bfloat16)
        if core == 0:
            high = lax.div(tags, 256)
            which = lax.broadcasted_iota(jnp.int32, (tags_out.shape[1], point_rows), 0)
            coded = jnp.where(which == 0, high, jnp.where(which == 1, tags - high * 256, 0))
            tags_out[...] = lax.dot_general(
                placed,
                coded.astype(jnp.float32).astype(jnp.bfloat16),
                NT,
                preferred_element_type=jnp.float32,
            ).astype(jnp.bfloat16)


def marks_kernel(line_ref, choice_ref, after_ref, *refs):
    halves, marks_ref, keep_ref = refs[:-2], refs[-2], refs[-1]
    half = halves[0].shape[0]
    for away, block in enumerate(halves):
        first = pl.multiple_of(lax.bitwise_xor(line_ref[0], away) * half, 16)
        marks_ref[pl.ds(first, half), :] = unit_rows(block[...])
    keep_ref[...] = jnp.full(keep_ref.shape, choice_ref[0], jnp.int32)


def pick_kernel(keep_ref, mine_ref, met_ref, *refs):
    refs[-1][...] = jnp.where(keep_ref[0] != 0, mine_ref[...], met_ref[...])


def pass_kernel(block_ref, after_ref, out_ref):
    out_ref[...] = block_ref[...]


def rows_kernel(groups, capacity, points_ref, tags_ref, marks_ref, out_ref):
    marks = marks_ref.shape[0]
    no_tags = jnp.zeros(tags_ref.shape, jnp.bfloat16)
    for core, tags in enumerate((tags_ref[...], no_tags)):
        scores = lax.dot_general(
            points_ref[core], marks_ref[...], NT, preferred_element_type=jnp.float32
        )
        rows = jnp.exp(scores * (0.5 / math.sqrt(points_ref.shape[2]))).astype(jnp.bfloat16)
        if len(out_ref.shape) == 2:
            for group in range(groups):
                here = slice(group * capacity, (group + 1) * capacity)
                first = (2 * group + core) * capacity
                out_ref[first : first + capacity, :marks] = rows[here]
                out_ref[first : first + capacity, marks:] = tags[here]
        else:
            out_ref[core, :, :marks] = rows
            out_ref[core, :, marks:] = tags


def sums_kernel(scale, core_ref, arrived_ref, mine_ref, *refs):
    others, (totals_ref, counts_ref, panel_ref, rows_ref) = refs[:-4], refs[-4:]
    slots, lanes = rows_ref.shape[1:]
    owned, marks = totals_ref.shape[0], mine_ref.shape[0]
    if len(arrived_ref.shape) == 3:
        rows_ref[...] = arrived_ref[...]
    else:
        part = arrived_ref.shape[2] // 2
        for chip in range(arrived_ref.shape[0]):
            first, middle, last = 2 * chip * part, (2 * chip + 1) * part, (2 * chip + 2) * part
            rows_ref[0, first:last, :] = arrived_ref[chip, core_ref[0]]
            rows_ref[1, first:middle, :] = arrived_ref[chip, 1 - core_ref[0], part:, :]
            rows_ref[1, middle:last, :] = arrived_ref[chip, 1 - core_ref[0], :part, :]
    panel_ref[0, :marks, :] = mine_ref[...]
    first = 0
    for other in others:
        panel_ref[1, first : first + other.shape[0], :] = other[...]
        first += other.shape[0]
    panel_ref[:, marks:, :] = jnp.zeros((2, lanes - marks, mine_ref.shape[1]), jnp.bfloat16)
    features = (
        jnp.dot(rows_ref[0], panel_ref[0], preferred_element_type=jnp.float32)
        + jnp.dot(rows_ref[1], panel_ref[1], preferred_element_type=jnp.float32)
    ).astype(jnp.bfloat16)
    which = lax.broadcasted_iota(jnp.int32, (8, lanes - marks), 1)
    weights = jnp.where(which == 0, 256.0, jnp.where(which == 1, 1.0, 0.0)).astype(jnp.bfloat16)
    tags = lax.dot_general(weights, rows_ref[0, :, marks:], NT, preferred_element_type=jnp.float32)
    tags += lax.dot_general(weights, rows_ref[1, :, marks:], NT, preferred_element_type=jnp.float32)
    tags = tags[:1].astype(jnp.int32)
    member = (
        (lax.broadcasted_iota(jnp.int32, (owned, slots), 0) + 1 == tags)
        .astype(jnp.float32)
        .astype(jnp.bfloat16)
    )
    totals_ref[...] = jnp.dot(member, features, preferred_element_type=jnp.float32) * scale
    counts_ref[...] = lax.dot_general(
        jnp.ones((8, slots), jnp.bfloat16), member, NT, preferred_element_type=jnp.float32
    )[:1].astype(jnp.int32)


def call(kernel, shapes, *operands, place=(), scratch=()):
    held = pl.BlockSpec(memory_space=pltpu.VMEM)
    first = [scalar.astype(jnp.int32).reshape(-1) for scalar in place]
    return pl.pallas_call(
        kernel,
        out_shape=shapes,
        in_specs=[pl.BlockSpec(memory_space=pltpu.SMEM)] * len(first) + [held] * len(operands),
        out_specs=(held,) * len(shapes) if isinstance(shapes, tuple) else held,
        scratch_shapes=scratch,
        compiler_params=pltpu.CompilerParams(vmem_limit_bytes=VMEM_LIMIT),
    )(*first, *operands)


def array(shape, dtype=jnp.bfloat16):
    return jax.ShapeDtypeStruct(shape, dtype)


def swap(block, axis, mask):
    return lax.ppermute(block, axis, [(i, i ^ mask) for i in range(lax.axis_size(axis))])


def pick(keep, mine, met, *after):
    return call(pick_kernel, array(mine.shape), mine, met, *after, place=(keep,))


def sides_of(panel, parts, core):
    sides = panel.reshape(parts, 2, -1, panel.shape[1])
    return (
        lax.dynamic_index_in_dim(sides, side, 1, keepdims=False).reshape(-1, panel.shape[1])
        for side in (core, 1 - core)
    )


def exchange(rows, groups, capacity, core):
    slots, lanes = groups * capacity, rows.shape[-1]
    whole_tiles = rows.ndim == 2
    if not whole_tiles:
        rows = rows.reshape(2, groups, capacity, lanes).swapaxes(0, 1)
    arrived = lax.all_to_all(
        rows.reshape(groups, 2 * capacity, lanes), "pts", split_axis=0, concat_axis=0, tiled=True
    ).reshape(groups // 2, 2, 2 * capacity, lanes)
    if whole_tiles:
        return arrived
    even = lax.dynamic_index_in_dim(arrived, core, 1, keepdims=False)
    odd = lax.dynamic_index_in_dim(arrived, 1 - core, 1, keepdims=False)
    odd = jnp.concatenate([odd[:, capacity:], odd[:, :capacity]], axis=1)
    return jnp.stack([even.reshape(slots, lanes), odd.reshape(slots, lanes)])


def body(points, landmarks, panels, panel_index, assignment):
    groups, parts = lax.axis_size("pts"), lax.axis_size("lmk")
    point_rows, width = points.shape
    capacity = 2 * point_rows // groups
    slots = groups * capacity
    owned = CLUSTERS // groups
    depth, columns = panels.shape[1:]
    half = landmarks.shape[0] // 2
    lanes = -(-(depth // 2 + 2) // LANES) * LANES
    me = lax.axis_index("pts")
    marks = lax.dynamic_slice_in_dim(landmarks, (me % 2) * half, half, 0)
    assignment = assignment.reshape(1, point_rows)
    points_met, assignment_met = swap(points, "pts", 1), swap(assignment, "pts", 1)
    differs = panel_index[0] ^ me
    mine, other = sides_of(panels[0], parts, me % 2)
    panel = pick((differs & 1) == 0, mine, swap(other, "pts", 1), points_met, assignment_met)
    near = call(pass_kernel, array(marks.shape), marks, panel)
    halves = [marks] + [
        swap(near if mask == 1 else marks, "lmk", mask) for mask in range(1, parts)
    ]
    masks = [1 << bit for bit in range(groups.bit_length() - 2, 0, -1)]
    panel_met = swap(panel, "pts", masks[0])
    placed, tags = call(
        lambda *refs: place_kernel(groups, capacity, *refs),
        (array((2, slots, width)), array((slots, lanes - depth // 2))),
        points,
        assignment,
        points_met,
        assignment_met,
        place=(jnp.stack([lax.axis_index("lmk"), (differs & masks[0]) == 0]).astype(jnp.int32),),
    )
    marks, keep = call(
        marks_kernel,
        (array((depth // 2, width)), array((1, columns), jnp.int32)),
        tags,
        *halves,
        place=(lax.axis_index("lmk"), (differs & masks[0]) == 0),
    )
    rows = call(
        lambda *refs: rows_kernel(groups, capacity, *refs),
        array((2 * slots, lanes) if capacity % 16 == 0 else (2, slots, lanes)),
        placed,
        tags,
        marks,
    )
    panel = jnp.where(keep != 0, panel, panel_met)
    for mask in masks[1:]:
        panel = jnp.where((differs & mask) == 0, panel, swap(panel, "pts", mask))
    cut = panel.shape[0] // 2
    others = [swap(panel[:cut], "pts", 1)]
    others.append(swap(call(pass_kernel, array((cut, columns)), panel[cut:], others[0]), "pts", 1))
    arrived = exchange(rows, groups, capacity, me % 2)
    totals, counts = call(
        lambda *refs: sums_kernel(CLUSTERS / (point_rows * groups), *refs),
        (array((owned, columns), jnp.float32), array((1, owned), jnp.int32)),
        arrived,
        panel,
        *others,
        place=(me % 2,),
        scratch=[
            pltpu.VMEM((2, lanes, columns), jnp.bfloat16),
            pltpu.VMEM((2, slots, lanes), jnp.bfloat16),
        ],
    )
    return (totals, counts.reshape(owned))


def solution(mesh):
    in_specs = (P("pts", None), P("lmk", None), P("pts", None, "lmk"), P(), P("pts"))
    out_specs = (P("pts", "lmk"), P("pts"))
    return jax.shard_map(body, mesh=mesh, in_specs=in_specs, out_specs=out_specs, check_vma=False)
```

```python
import math

import jax
import jax.numpy as jnp
from jax import lax
from jax.experimental import pallas as pl
from jax.experimental.pallas import tpu as pltpu
from jax.sharding import PartitionSpec as P

CLUSTERS = 4096
LANES = 128
VMEM_LIMIT = 48 * 1024 * 1024
NT = (((1,), (1,)), ((), ()))


def unit_rows(values_in):
    widened = values_in.astype(jnp.float32)
    scale = lax.rsqrt(jnp.mean(widened * widened, axis=1, keepdims=True) + 1e-06)
    return (widened * scale).astype(jnp.bfloat16)


def place_kernel(groups, capacity, after_ref, *refs):
    points_out, tags_out = refs[-2:]
    for core in range(2):
        points_ref, assignment_ref = refs[2 * core : 2 * core + 2]
        point_rows = points_ref.shape[0]
        ids = assignment_ref[...]
        owned = CLUSTERS // groups
        owners = lax.div(ids, owned)
        tags = ids - owners * owned + 1
        hits = lax.broadcasted_iota(jnp.int32, (groups, point_rows), 0) == owners
        earlier = lax.broadcasted_iota(
            jnp.int32, (point_rows, point_rows), 0
        ) < lax.broadcasted_iota(jnp.int32, (point_rows, point_rows), 1)
        before = jnp.dot(
            hits.astype(jnp.float32).astype(jnp.bfloat16),
            earlier.astype(jnp.float32).astype(jnp.bfloat16),
            preferred_element_type=jnp.float32,
        )
        rank = jnp.sum(jnp.where(hits, before, 0.0), axis=0, keepdims=True).astype(jnp.int32)
        slots = owners * capacity + rank
        placed = (
            (lax.broadcasted_iota(jnp.int32, (groups * capacity, point_rows), 0) == slots)
            .astype(jnp.float32)
            .astype(jnp.bfloat16)
        )
        points_out[core] = jnp.dot(
            placed, unit_rows(points_ref[...]), preferred_element_type=jnp.float32
        ).astype(jnp.bfloat16)
        if core == 0:
            high = lax.div(tags, 256)
            which = lax.broadcasted_iota(jnp.int32, (tags_out.shape[1], point_rows), 0)
            coded = jnp.where(which == 0, high, jnp.where(which == 1, tags - high * 256, 0))
            tags_out[...] = lax.dot_general(
                placed,
                coded.astype(jnp.float32).astype(jnp.bfloat16),
                NT,
                preferred_element_type=jnp.float32,
            ).astype(jnp.bfloat16)


def marks_kernel(line_ref, choice_ref, after_ref, *refs):
    halves, marks_ref, keep_ref = refs[:-2], refs[-2], refs[-1]
    half = halves[0].shape[0]
    for away, block in enumerate(halves):
        first = pl.multiple_of(lax.bitwise_xor(line_ref[0], away) * half, 16)
        marks_ref[pl.ds(first, half), :] = unit_rows(block[...])
    keep_ref[...] = jnp.full(keep_ref.shape, choice_ref[0], jnp.int32)


def pick_kernel(keep_ref, mine_ref, met_ref, *refs):
    refs[-1][...] = jnp.where(keep_ref[0] != 0, mine_ref[...], met_ref[...])


def pass_kernel(block_ref, after_ref, out_ref):
    out_ref[...] = block_ref[...]


def rows_kernel(groups, capacity, points_ref, tags_ref, marks_ref, out_ref):
    marks = marks_ref.shape[0]
    no_tags = jnp.zeros(tags_ref.shape, jnp.bfloat16)
    for core, tags in enumerate((tags_ref[...], no_tags)):
        scores = lax.dot_general(
            points_ref[core], marks_ref[...], NT, preferred_element_type=jnp.float32
        )
        rows = jnp.exp(scores * (0.5 / math.sqrt(points_ref.shape[2]))).astype(jnp.bfloat16)
        if len(out_ref.shape) == 2:
            for group in range(groups):
                here = slice(group * capacity, (group + 1) * capacity)
                first = (2 * group + core) * capacity
                out_ref[first : first + capacity, :marks] = rows[here]
                out_ref[first : first + capacity, marks:] = tags[here]
        else:
            out_ref[core, :, :marks] = rows
            out_ref[core, :, marks:] = tags


def sums_kernel(scale, core_ref, arrived_ref, mine_ref, *refs):
    others, (totals_ref, counts_ref, panel_ref, rows_ref) = refs[:-4], refs[-4:]
    slots, lanes = rows_ref.shape[1:]
    owned, marks = totals_ref.shape[0], mine_ref.shape[0]
    if len(arrived_ref.shape) == 3:
        rows_ref[...] = arrived_ref[...]
    else:
        part = arrived_ref.shape[2] // 2
        for chip in range(arrived_ref.shape[0]):
            first, middle, last = 2 * chip * part, (2 * chip + 1) * part, (2 * chip + 2) * part
            rows_ref[0, first:last, :] = arrived_ref[chip, core_ref[0]]
            rows_ref[1, first:middle, :] = arrived_ref[chip, 1 - core_ref[0], part:, :]
            rows_ref[1, middle:last, :] = arrived_ref[chip, 1 - core_ref[0], :part, :]
    panel_ref[0, :marks, :] = mine_ref[...]
    first = 0
    for other in others:
        panel_ref[1, first : first + other.shape[0], :] = other[...]
        first += other.shape[0]
    panel_ref[:, marks:, :] = jnp.zeros((2, lanes - marks, mine_ref.shape[1]), jnp.bfloat16)
    features = (
        jnp.dot(rows_ref[0], panel_ref[0], preferred_element_type=jnp.float32)
        + jnp.dot(rows_ref[1], panel_ref[1], preferred_element_type=jnp.float32)
    ).astype(jnp.bfloat16)
    which = lax.broadcasted_iota(jnp.int32, (8, lanes - marks), 1)
    weights = jnp.where(which == 0, 256.0, jnp.where(which == 1, 1.0, 0.0)).astype(jnp.bfloat16)
    tags = lax.dot_general(weights, rows_ref[0, :, marks:], NT, preferred_element_type=jnp.float32)
    tags += lax.dot_general(weights, rows_ref[1, :, marks:], NT, preferred_element_type=jnp.float32)
    tags = tags[:1].astype(jnp.int32)
    member = (
        (lax.broadcasted_iota(jnp.int32, (owned, slots), 0) + 1 == tags)
        .astype(jnp.float32)
        .astype(jnp.bfloat16)
    )
    totals_ref[...] = jnp.dot(member, features, preferred_element_type=jnp.float32) * scale
    counts_ref[...] = lax.dot_general(
        jnp.ones((8, slots), jnp.bfloat16), member, NT, preferred_element_type=jnp.float32
    )[:1].astype(jnp.int32)


def call(kernel, shapes, *operands, place=(), scratch=()):
    held = pl.BlockSpec(memory_space=pltpu.VMEM)
    first = [scalar.astype(jnp.int32).reshape(-1) for scalar in place]
    return pl.pallas_call(
        kernel,
        out_shape=shapes,
        in_specs=[pl.BlockSpec(memory_space=pltpu.SMEM)] * len(first) + [held] * len(operands),
        out_specs=(held,) * len(shapes) if isinstance(shapes, tuple) else held,
        scratch_shapes=scratch,
        compiler_params=pltpu.CompilerParams(vmem_limit_bytes=VMEM_LIMIT),
    )(*first, *operands)


def array(shape, dtype=jnp.bfloat16):
    return jax.ShapeDtypeStruct(shape, dtype)


def swap(block, axis, mask):
    return lax.ppermute(block, axis, [(i, i ^ mask) for i in range(lax.axis_size(axis))])


def pick(keep, mine, met, *after):
    return call(pick_kernel, array(mine.shape), mine, met, *after, place=(keep,))


def sides_of(panel, parts, core):
    sides = panel.reshape(parts, 2, -1, panel.shape[1])
    return (
        lax.dynamic_index_in_dim(sides, side, 1, keepdims=False).reshape(-1, panel.shape[1])
        for side in (core, 1 - core)
    )


def exchange(rows, groups, capacity, core):
    slots, lanes = groups * capacity, rows.shape[-1]
    whole_tiles = rows.ndim == 2
    if not whole_tiles:
        rows = rows.reshape(2, groups, capacity, lanes).swapaxes(0, 1)
    arrived = lax.all_to_all(
        rows.reshape(groups, 2 * capacity, lanes), "pts", split_axis=0, concat_axis=0, tiled=True
    ).reshape(groups // 2, 2, 2 * capacity, lanes)
    if whole_tiles:
        return arrived
    even = lax.dynamic_index_in_dim(arrived, core, 1, keepdims=False)
    odd = lax.dynamic_index_in_dim(arrived, 1 - core, 1, keepdims=False)
    odd = jnp.concatenate([odd[:, capacity:], odd[:, :capacity]], axis=1)
    return jnp.stack([even.reshape(slots, lanes), odd.reshape(slots, lanes)])


def body(points, landmarks, panels, panel_index, assignment):
    groups, parts = lax.axis_size("pts"), lax.axis_size("lmk")
    point_rows, width = points.shape
    capacity = 2 * point_rows // groups
    slots = groups * capacity
    owned = CLUSTERS // groups
    depth, columns = panels.shape[1:]
    half = landmarks.shape[0] // 2
    lanes = -(-(depth // 2 + 2) // LANES) * LANES
    me = lax.axis_index("pts")
    marks = lax.dynamic_slice_in_dim(landmarks, (me % 2) * half, half, 0)
    assignment = assignment.reshape(1, point_rows)
    points_met, assignment_met = swap(points, "pts", 1), swap(assignment, "pts", 1)
    differs = panel_index[0] ^ me
    mine, other = sides_of(panels[0], parts, me % 2)
    panel = pick((differs & 1) == 0, mine, swap(other, "pts", 1), points_met, assignment_met)
    near = call(pass_kernel, array(marks.shape), marks, panel)
    halves = [marks] + [
        swap(near if mask < parts - 1 else marks, "lmk", mask) for mask in range(1, parts)
    ]
    masks = [1 << bit for bit in range(1, groups.bit_length() - 1)]
    panel_met = swap(panel, "pts", masks[0])
    placed, tags = call(
        lambda *refs: place_kernel(groups, capacity, *refs),
        (array((2, slots, width)), array((slots, lanes - depth // 2))),
        points,
        assignment,
        points_met,
        assignment_met,
        place=(jnp.stack([lax.axis_index("lmk"), (differs & masks[0]) == 0]).astype(jnp.int32),),
    )
    marks, keep = call(
        marks_kernel,
        (array((depth // 2, width)), array((1, columns), jnp.int32)),
        tags,
        *halves,
        place=(lax.axis_index("lmk"), (differs & masks[0]) == 0),
    )
    rows = call(
        lambda *refs: rows_kernel(groups, capacity, *refs),
        array((2 * slots, lanes) if capacity % 16 == 0 else (2, slots, lanes)),
        placed,
        tags,
        marks,
    )
    panel = jnp.where(keep != 0, panel, panel_met)
    for mask in masks[1:]:
        panel = jnp.where((differs & mask) == 0, panel, swap(panel, "pts", mask))
    cut = panel.shape[0] // 2
    others = [swap(panel[:cut], "pts", 1)]
    others.append(swap(call(pass_kernel, array((cut, columns)), panel[cut:], others[0]), "pts", 1))
    arrived = exchange(rows, groups, capacity, me % 2)
    totals, counts = call(
        lambda *refs: sums_kernel(CLUSTERS / (point_rows * groups), *refs),
        (array((owned, columns), jnp.float32), array((1, owned), jnp.int32)),
        arrived,
        panel,
        *others,
        place=(me % 2,),
        scratch=[
            pltpu.VMEM((2, lanes, columns), jnp.bfloat16),
            pltpu.VMEM((2, slots, lanes), jnp.bfloat16),
        ],
    )
    return (totals, counts.reshape(owned))


def solution(mesh):
    in_specs = (P("pts", None), P("lmk", None), P("pts", None, "lmk"), P(), P("pts"))
    out_specs = (P("pts", "lmk"), P("pts"))
    return jax.shard_map(body, mesh=mesh, in_specs=in_specs, out_specs=out_specs, check_vma=False)
```

```python
import math

import jax
import jax.numpy as jnp
from jax import lax
from jax.experimental import pallas as pl
from jax.experimental.pallas import tpu as pltpu
from jax.sharding import PartitionSpec as P

CLUSTERS = 4096
LANES = 128
VMEM_LIMIT = 48 * 1024 * 1024
NT = (((1,), (1,)), ((), ()))


def unit_rows(values_in):
    widened = values_in.astype(jnp.float32)
    scale = lax.rsqrt(jnp.mean(widened * widened, axis=1, keepdims=True) + 1e-06)
    return (widened * scale).astype(jnp.bfloat16)


def place_kernel(groups, capacity, after_ref, *refs):
    points_out, tags_out = refs[-2:]
    for core in range(2):
        points_ref, assignment_ref = refs[2 * core : 2 * core + 2]
        point_rows = points_ref.shape[0]
        ids = assignment_ref[...]
        owned = CLUSTERS // groups
        owners = lax.div(ids, owned)
        tags = ids - owners * owned + 1
        hits = lax.broadcasted_iota(jnp.int32, (groups, point_rows), 0) == owners
        earlier = lax.broadcasted_iota(
            jnp.int32, (point_rows, point_rows), 0
        ) < lax.broadcasted_iota(jnp.int32, (point_rows, point_rows), 1)
        before = jnp.dot(
            hits.astype(jnp.float32).astype(jnp.bfloat16),
            earlier.astype(jnp.float32).astype(jnp.bfloat16),
            preferred_element_type=jnp.float32,
        )
        rank = jnp.sum(jnp.where(hits, before, 0.0), axis=0, keepdims=True).astype(jnp.int32)
        slots = owners * capacity + rank
        placed = (
            (lax.broadcasted_iota(jnp.int32, (groups * capacity, point_rows), 0) == slots)
            .astype(jnp.float32)
            .astype(jnp.bfloat16)
        )
        points_out[core] = jnp.dot(
            placed, unit_rows(points_ref[...]), preferred_element_type=jnp.float32
        ).astype(jnp.bfloat16)
        if core == 0:
            high = lax.div(tags, 256)
            which = lax.broadcasted_iota(jnp.int32, (tags_out.shape[1], point_rows), 0)
            coded = jnp.where(which == 0, high, jnp.where(which == 1, tags - high * 256, 0))
            tags_out[...] = lax.dot_general(
                placed,
                coded.astype(jnp.float32).astype(jnp.bfloat16),
                NT,
                preferred_element_type=jnp.float32,
            ).astype(jnp.bfloat16)


def marks_kernel(line_ref, choice_ref, after_ref, *refs):
    halves, marks_ref, keep_ref = refs[:-2], refs[-2], refs[-1]
    half = halves[0].shape[0]
    for away, block in enumerate(halves):
        first = pl.multiple_of(lax.bitwise_xor(line_ref[0], away) * half, 16)
        marks_ref[pl.ds(first, half), :] = unit_rows(block[...])
    keep_ref[...] = jnp.full(keep_ref.shape, choice_ref[0], jnp.int32)


def pick_kernel(keep_ref, mine_ref, met_ref, *refs):
    refs[-1][...] = jnp.where(keep_ref[0] != 0, mine_ref[...], met_ref[...])


def pass_kernel(block_ref, after_ref, out_ref):
    out_ref[...] = block_ref[...]


def rows_kernel(groups, capacity, points_ref, tags_ref, marks_ref, out_ref):
    marks = marks_ref.shape[0]
    no_tags = jnp.zeros(tags_ref.shape, jnp.bfloat16)
    slots, width = points_ref.shape[1:]
    scores = lax.dot_general(
        points_ref[...].reshape(2 * slots, width), marks_ref[...], NT, preferred_element_type=jnp.float32
    )
    both = jnp.exp(scores * (0.5 / math.sqrt(width))).astype(jnp.bfloat16)
    for core, tags in enumerate((tags_ref[...], no_tags)):
        rows = both[core * slots : (core + 1) * slots]
        if len(out_ref.shape) == 2:
            for group in range(groups):
                here = slice(group * capacity, (group + 1) * capacity)
                first = (2 * group + core) * capacity
                out_ref[first : first + capacity, :marks] = rows[here]
                out_ref[first : first + capacity, marks:] = tags[here]
        else:
            out_ref[core, :, :marks] = rows
            out_ref[core, :, marks:] = tags


def sums_kernel(scale, core_ref, arrived_ref, mine_ref, *refs):
    others, (totals_ref, counts_ref, panel_ref, rows_ref) = refs[:-4], refs[-4:]
    slots, lanes = rows_ref.shape[1:]
    owned, marks = totals_ref.shape[0], mine_ref.shape[0]
    if len(arrived_ref.shape) == 3:
        rows_ref[...] = arrived_ref[...]
    else:
        part = arrived_ref.shape[2] // 2
        for chip in range(arrived_ref.shape[0]):
            first, middle, last = 2 * chip * part, (2 * chip + 1) * part, (2 * chip + 2) * part
            rows_ref[0, first:last, :] = arrived_ref[chip, core_ref[0]]
            rows_ref[1, first:middle, :] = arrived_ref[chip, 1 - core_ref[0], part:, :]
            rows_ref[1, middle:last, :] = arrived_ref[chip, 1 - core_ref[0], :part, :]
    panel_ref[0, :marks, :] = mine_ref[...]
    first = 0
    for other in others:
        panel_ref[1, first : first + other.shape[0], :] = other[...]
        first += other.shape[0]
    panel_ref[:, marks:, :] = jnp.zeros((2, lanes - marks, mine_ref.shape[1]), jnp.bfloat16)
    features = (
        jnp.dot(rows_ref[0], panel_ref[0], preferred_element_type=jnp.float32)
        + jnp.dot(rows_ref[1], panel_ref[1], preferred_element_type=jnp.float32)
    ).astype(jnp.bfloat16)
    which = lax.broadcasted_iota(jnp.int32, (8, lanes - marks), 1)
    weights = jnp.where(which == 0, 256.0, jnp.where(which == 1, 1.0, 0.0)).astype(jnp.bfloat16)
    tags = lax.dot_general(weights, rows_ref[0, :, marks:], NT, preferred_element_type=jnp.float32)
    tags += lax.dot_general(weights, rows_ref[1, :, marks:], NT, preferred_element_type=jnp.float32)
    tags = tags[:1].astype(jnp.int32)
    member = (
        (lax.broadcasted_iota(jnp.int32, (owned, slots), 0) + 1 == tags)
        .astype(jnp.float32)
        .astype(jnp.bfloat16)
    )
    totals_ref[...] = jnp.dot(member, features, preferred_element_type=jnp.float32) * scale
    counts_ref[...] = lax.dot_general(
        jnp.ones((8, slots), jnp.bfloat16), member, NT, preferred_element_type=jnp.float32
    )[:1].astype(jnp.int32)


def call(kernel, shapes, *operands, place=(), scratch=()):
    held = pl.BlockSpec(memory_space=pltpu.VMEM)
    first = [scalar.astype(jnp.int32).reshape(-1) for scalar in place]
    return pl.pallas_call(
        kernel,
        out_shape=shapes,
        in_specs=[pl.BlockSpec(memory_space=pltpu.SMEM)] * len(first) + [held] * len(operands),
        out_specs=(held,) * len(shapes) if isinstance(shapes, tuple) else held,
        scratch_shapes=scratch,
        compiler_params=pltpu.CompilerParams(vmem_limit_bytes=VMEM_LIMIT),
    )(*first, *operands)


def array(shape, dtype=jnp.bfloat16):
    return jax.ShapeDtypeStruct(shape, dtype)


def swap(block, axis, mask):
    return lax.ppermute(block, axis, [(i, i ^ mask) for i in range(lax.axis_size(axis))])


def pick(keep, mine, met, *after):
    return call(pick_kernel, array(mine.shape), mine, met, *after, place=(keep,))


def sides_of(panel, parts, core):
    sides = panel.reshape(parts, 2, -1, panel.shape[1])
    return (
        lax.dynamic_index_in_dim(sides, side, 1, keepdims=False).reshape(-1, panel.shape[1])
        for side in (core, 1 - core)
    )


def exchange(rows, groups, capacity, core):
    slots, lanes = groups * capacity, rows.shape[-1]
    whole_tiles = rows.ndim == 2
    if not whole_tiles:
        rows = rows.reshape(2, groups, capacity, lanes).swapaxes(0, 1)
    arrived = lax.all_to_all(
        rows.reshape(groups, 2 * capacity, lanes), "pts", split_axis=0, concat_axis=0, tiled=True
    ).reshape(groups // 2, 2, 2 * capacity, lanes)
    if whole_tiles:
        return arrived
    even = lax.dynamic_index_in_dim(arrived, core, 1, keepdims=False)
    odd = lax.dynamic_index_in_dim(arrived, 1 - core, 1, keepdims=False)
    odd = jnp.concatenate([odd[:, capacity:], odd[:, :capacity]], axis=1)
    return jnp.stack([even.reshape(slots, lanes), odd.reshape(slots, lanes)])


def body(points, landmarks, panels, panel_index, assignment):
    groups, parts = lax.axis_size("pts"), lax.axis_size("lmk")
    point_rows, width = points.shape
    capacity = 2 * point_rows // groups
    slots = groups * capacity
    owned = CLUSTERS // groups
    depth, columns = panels.shape[1:]
    half = landmarks.shape[0] // 2
    lanes = -(-(depth // 2 + 2) // LANES) * LANES
    me = lax.axis_index("pts")
    marks = lax.dynamic_slice_in_dim(landmarks, (me % 2) * half, half, 0)
    assignment = assignment.reshape(1, point_rows)
    points_met, assignment_met = swap(points, "pts", 1), swap(assignment, "pts", 1)
    differs = panel_index[0] ^ me
    mine, other = sides_of(panels[0], parts, me % 2)
    panel = pick((differs & 1) == 0, mine, swap(other, "pts", 1), assignment_met)
    near = call(pass_kernel, array(marks.shape), marks, panel)
    halves = [marks] + [
        swap(near if mask == 1 else marks, "lmk", mask) for mask in range(1, parts)
    ]
    masks = [1 << bit for bit in range(1, groups.bit_length() - 1)]
    panel_met = swap(panel, "pts", masks[0])
    placed, tags = call(
        lambda *refs: place_kernel(groups, capacity, *refs),
        (array((2, slots, width)), array((slots, lanes - depth // 2))),
        points,
        assignment,
        points_met,
        assignment_met,
        place=(jnp.stack([lax.axis_index("lmk"), (differs & masks[0]) == 0]).astype(jnp.int32),),
    )
    marks, keep = call(
        marks_kernel,
        (array((depth // 2, width)), array((1, columns), jnp.int32)),
        tags,
        *halves,
        place=(lax.axis_index("lmk"), (differs & masks[0]) == 0),
    )
    rows = call(
        lambda *refs: rows_kernel(groups, capacity, *refs),
        array((2 * slots, lanes) if capacity % 16 == 0 else (2, slots, lanes)),
        placed,
        tags,
        marks,
    )
    panel = jnp.where(keep != 0, panel, panel_met)
    for mask in masks[1:]:
        panel = jnp.where((differs & mask) == 0, panel, swap(panel, "pts", mask))
    cut = panel.shape[0] // 2
    others = [swap(panel[:cut], "pts", 1)]
    others.append(swap(call(pass_kernel, array((cut, columns)), panel[cut:], others[0]), "pts", 1))
    arrived = exchange(rows, groups, capacity, me % 2)
    totals, counts = call(
        lambda *refs: sums_kernel(CLUSTERS / (point_rows * groups), *refs),
        (array((owned, columns), jnp.float32), array((1, owned), jnp.int32)),
        arrived,
        panel,
        *others,
        place=(me % 2,),
        scratch=[
            pltpu.VMEM((2, lanes, columns), jnp.bfloat16),
            pltpu.VMEM((2, slots, lanes), jnp.bfloat16),
        ],
    )
    return (totals, counts.reshape(owned))


def solution(mesh):
    in_specs = (P("pts", None), P("lmk", None), P("pts", None, "lmk"), P(), P("pts"))
    out_specs = (P("pts", "lmk"), P("pts"))
    return jax.shard_map(body, mesh=mesh, in_specs=in_specs, out_specs=out_specs, check_vma=False)
```
